128 devices in a mesh: fsdp: 4 (over y), context: 16 (over x, z), tensor: 2 (over core).
Axes of the slice: x: 4, y: 4, z: 4, core: 2. Of those that a mesh axis runs over, the one named last changes fastest.
Arguments:
- tokens: bfloat16 [4, 2048, 2048], P('fsdp', 'context'), may hold values from -6 to 6
- cotangent: bfloat16 [4, 2048, 2048], P('fsdp', 'context'), may hold values from -6 to 6
- doc_lengths: int32 [4, 8], P('fsdp'), may hold values from 0 to 2048, as said below
- padding: int32 [4, 2048], P('fsdp', 'context'), may hold values from 0 to 1, as said below
- expert_ids: int32 [4, 2048, 8], P('fsdp', 'context'), may hold values from 0 to 63, as said below
- norm1_gain: bfloat16 [2048], P('fsdp'), may hold values from 0.5 to 1.5
- w_query: bfloat16 [2048, 4096], P('fsdp', 'tensor'), may hold values from -0.125 to 0.125
- key_weight: bfloat16 [2048, 512], P('fsdp', 'tensor'), may hold values from -0.125 to 0.125
- value_weight: bfloat16 [2048, 512], P('fsdp', 'tensor'), may hold values from -0.125 to 0.125
- q_gain: bfloat16 [128], P('fsdp'), may hold values from 0.5 to 1.5
- k_gain: bfloat16 [128], P('fsdp'), may hold values from 0.5 to 1.5
- w_out: bfloat16 [4096, 2048], P('tensor', 'fsdp'), may hold values from -0.375 to 0.375
- norm2_gain: bfloat16 [2048], P('fsdp'), may hold values from 0.5 to 1.5
- w_router: bfloat16 [2048, 64], P('fsdp'), may hold values from -0.0625 to 0.0625
- w_gate: bfloat16 [64, 2048, 768], P('context', 'fsdp', 'tensor'), may hold values from -0.125 to 0.125
- w_up: bfloat16 [64, 2048, 768], P('context', 'fsdp', 'tensor'), may hold values from -0.125 to 0.125
- w_down: bfloat16 [64, 768, 2048], P('context', 'tensor', 'fsdp'), may hold values from -0.625 to 0.625
Outputs:
- output: float32 [4, 2048, 2048], P('fsdp', 'context')
- loss: float32 [], replicated
- expert_load: float32 [64], replicated
- grad_tokens: float32 [4, 2048, 2048], P('fsdp', 'context')
- grad_norm1_gain: float32 [2048], P('fsdp')
- grad_w_query: float32 [2048, 4096], P('fsdp', 'tensor')
- grad_w_key: float32 [2048, 512], P('fsdp', 'tensor')
- grad_w_value: float32 [2048, 512], P('fsdp', 'tensor')
- grad_q_gain: float32 [128], P('fsdp')
- grad_k_gain: float32 [128], P('fsdp')
- grad_w_out: float32 [4096, 2048], P('tensor', 'fsdp')
- grad_norm2_gain: float32 [2048], P('fsdp')
- grad_w_router: float32 [2048, 64], P('fsdp')
- grad_w_gate: float32 [64, 2048, 768], P('context', 'fsdp', 'tensor')
- grad_w_up: float32 [64, 2048, 768], P('context', 'fsdp', 'tensor')
- grad_w_down: float32 [64, 768, 2048], P('context', 'tensor', 'fsdp')
The draws below stay inside these ranges and needn't reach their ends.
Inputs may be any that keep to these rules, and one draw needn't show every extreme that they name: `doc_lengths`: each row sums to 2048. In one row, chosen by the seed, the first entry is 2048 and the others are 0. Each sequence ends with a run of 1 to 512 padding positions; all earlier positions are 0. `expert_ids`: each token names 8 different experts. In each aligned block of 128 positions of one sequence every expert is named by 0 or by exactly 32 tokens, and half of the experts by 32.
All inputs are finite; a program needn't handle non-finite values.
Results may differ from the reference program's by a relative error of at most 0.025.
Values may be sent and summed in bfloat16 or wider, within the bound.
No kernel may reach another device: no remote copies, remote signals or barrier semaphores. Data moves between devices by JAX's collectives and lax.ppermute only.
A program may use at most 320 MiB of HBM per device.

```python
import jax
import jax.numpy as jnp
from jax import lax

MODEL_DIM = 2048
QUERY_HEADS = 32
KEY_VALUE_HEADS = 4
HEAD_SIZE = 128
FF = 768
TOPK = 8
SEQUENCE_TOKENS = 2048
WINDOW = 1024
NDOC = 8
EXPERTS = 64
BATCH = 4
SPAN = 128
ROUTE_MOST = 32
N_CONTEXT = 16
N_TENSOR = 2


def draw_doc_lengths(key, part):
    key = jax.random.fold_in(key, 11)
    cut_key, pick_key = jax.random.split(key)
    cuts = jnp.sort(jax.random.randint(cut_key, (BATCH, NDOC - 1), 0, SEQUENCE_TOKENS + 1), axis=1)
    bounds = jnp.concatenate([jnp.zeros((BATCH, 1), jnp.int32), cuts.astype(jnp.int32), jnp.full((BATCH, 1), SEQUENCE_TOKENS, jnp.int32)], axis=1)
    lengths = bounds[:, 1:] - bounds[:, :-1]
    picked_row = jax.random.randint(pick_key, (), 0, BATCH)
    whole_doc = jnp.zeros((NDOC,), jnp.int32).at[0].set(SEQUENCE_TOKENS)
    row_hit = jnp.arange(BATCH)[:, None] == picked_row
    return jnp.where(row_hit, whole_doc[None, :], lengths).astype(jnp.int32)


def draw_padding(key, part):
    key = jax.random.fold_in(key, 23)
    tails = jax.random.randint(key, (BATCH, 1), 1, SEQUENCE_TOKENS // 4 + 1)
    return (jnp.arange(SEQUENCE_TOKENS)[None, :] >= SEQUENCE_TOKENS - tails).astype(jnp.int32)


def draw_expert_ids(key, part):
    key = jax.random.fold_in(key, 37)
    order_key, shift_key = jax.random.split(key)
    order = jax.random.permutation(order_key, EXPERTS).astype(jnp.int32)
    shifts = jax.random.randint(shift_key, (BATCH, 1, 1), 0, EXPERTS).astype(jnp.int32)
    positions = jnp.arange(SEQUENCE_TOKENS, dtype=jnp.int32)
    block_index = positions // SPAN
    within = positions % SPAN
    slot_number = within[:, None] * TOPK + jnp.arange(TOPK, dtype=jnp.int32)[None, :]
    busy_index = slot_number % (EXPERTS // 2)
    stride = EXPERTS // (2 * (SEQUENCE_TOKENS // SPAN))
    index = (shifts + block_index[None, :, None] * stride + busy_index[None, :, :]) % EXPERTS
    return order[index].astype(jnp.int32)


def steps_of(stream_key, shape, cuts, smallest, high):
    def one(dim, shards_of):
        heights = jax.random.uniform(jax.random.fold_in(jax.random.fold_in(stream_key, 6), dim), (shards_of,), jnp.float32, smallest / len(cuts), high / len(cuts))
        return jnp.repeat(jnp.exp(heights), shape[dim] // shards_of).reshape((-1,) + (1,) * (len(shape) - dim - 1))

    loudness = one(*cuts[0])
    for cut in cuts[1:]:
        loudness = loudness * one(*cut)
    return loudness


def noise(own_key, dims, scale, limit, cuts=(), kind=jnp.bfloat16):
    result = scale * jax.random.normal(own_key, dims, jnp.float32)
    if cuts:
        result = result * steps_of(own_key, dims, cuts, -0.22, 0.18)
    return jnp.clip(result, -limit, limit).astype(kind)


def setup_inputs(seed: int = 0) -> dict:
    arg_keys = jax.random.split(jax.random.key(seed), 18)
    return {
        "tokens": noise(arg_keys[0], (BATCH, SEQUENCE_TOKENS, MODEL_DIM), 1.0, 6.0, ((0, 4), (1, 16))),
        "cotangent": noise(arg_keys[1], (BATCH, SEQUENCE_TOKENS, MODEL_DIM), 1.0, 6.0, ((0, 4), (1, 16))),
        "doc_lengths": draw_doc_lengths(jax.random.fold_in(arg_keys[17], 71), 0),
        "padding": draw_padding(jax.random.fold_in(arg_keys[17], 71), 0),
        "expert_ids": draw_expert_ids(jax.random.fold_in(arg_keys[17], 71), 0),
        "norm1_gain": jnp.clip(1.0 + 0.1 * jax.random.normal(arg_keys[5], (MODEL_DIM,), jnp.float32), 0.5, 1.5).astype(jnp.bfloat16),
        "w_query": noise(arg_keys[6], (MODEL_DIM, QUERY_HEADS * HEAD_SIZE), MODEL_DIM ** -0.5, 0.125, ((0, 4), (1, 2))),
        "key_weight": noise(arg_keys[7], (MODEL_DIM, KEY_VALUE_HEADS * HEAD_SIZE), MODEL_DIM ** -0.5, 0.125, ((0, 4), (1, 2))),
        "value_weight": noise(arg_keys[8], (MODEL_DIM, KEY_VALUE_HEADS * HEAD_SIZE), MODEL_DIM ** -0.5, 0.125, ((0, 4), (1, 2))),
        "q_gain": jnp.clip(1.0 + 0.1 * jax.random.normal(arg_keys[9], (HEAD_SIZE,), jnp.float32), 0.5, 1.5).astype(jnp.bfloat16),
        "k_gain": jnp.clip(1.0 + 0.1 * jax.random.normal(arg_keys[10], (HEAD_SIZE,), jnp.float32), 0.5, 1.5).astype(jnp.bfloat16),
        "w_out": noise(arg_keys[11], (QUERY_HEADS * HEAD_SIZE, MODEL_DIM), (QUERY_HEADS * HEAD_SIZE // 16) ** -0.5, 0.375, ((0, 2), (1, 4))),
        "norm2_gain": jnp.clip(1.0 + 0.1 * jax.random.normal(arg_keys[12], (MODEL_DIM,), jnp.float32), 0.5, 1.5).astype(jnp.bfloat16),
        "w_router": noise(arg_keys[13], (MODEL_DIM, EXPERTS), (4 * MODEL_DIM) ** -0.5, 0.0625, ((0, 4),)),
        "w_gate": noise(arg_keys[14], (EXPERTS, MODEL_DIM, FF), MODEL_DIM ** -0.5, 0.125, ((0, 16), (1, 4), (2, 2))),
        "w_up": noise(arg_keys[15], (EXPERTS, MODEL_DIM, FF), MODEL_DIM ** -0.5, 0.125, ((0, 16), (1, 4), (2, 2))),
        "w_down": noise(arg_keys[16], (EXPERTS, FF, MODEL_DIM), (FF // 8) ** -0.5, 0.625, ((0, 16), (1, 2), (2, 4))),
    }


@jax.custom_vjp
def reduced_copy(v):
    return lax.optimization_barrier(v.astype(jnp.bfloat16)).astype(jnp.float32)

@jax.custom_vjp
def reduced_backward(v):
    return v

def low_keep(v):
    return (reduced_copy(v), None)

def low_pass(kept, grad):
    return (grad,)

def back_keep(v):
    return (v, None)

def back_low(kept, grad):
    return (reduced_copy(grad),)
reduced_copy.defvjp(low_keep, low_pass)
reduced_backward.defvjp(back_keep, back_low)
epsilon = 1e-06
theta_base = 1000000.0
negative = -1e+30
highest = lax.Precision.HIGHEST

def matmul_product(left, right):
    return jnp.dot(left, right, precision=highest, preferred_element_type=jnp.float32)

def rms_scale(value_rows, gain_vec):
    inverse = lax.rsqrt(lax.optimization_barrier(jnp.mean(value_rows * value_rows, axis=-1, keepdims=True)) + epsilon)
    return value_rows * inverse * gain_vec

def rotate(value_rows, cosine, sine_table):
    half_size = value_rows.shape[-1] // 2
    first_half = value_rows[..., :half_size]
    second_half = value_rows[..., half_size:]
    return jnp.concatenate([first_half * cosine - second_half * sine_table, second_half * cosine + first_half * sine_table], axis=-1)

def head_prep(cosine, sine_table, projected, gain_vec):
    return rotate(rms_scale(projected, gain_vec), cosine, sine_table)

def doc_layout(doc_lengths, positions):
    ends = jnp.cumsum(doc_lengths, axis=-1)
    passed = positions[..., :, None] >= ends[..., None, :]
    doc_index = lax.optimization_barrier(jnp.sum(passed.astype(jnp.int32), axis=-1))
    starts = lax.optimization_barrier(jnp.sum(jnp.where(passed, doc_lengths[..., None, :], 0), axis=-1))
    return (doc_index, starts)

def sequence_forward(weights, seq_tokens, seq_lengths, seq_padding, seq_experts):
    norm1_gain, w_query, key_weight, value_weight, q_gain, k_gain, w_out, norm2_gain, w_router, w_gate, w_up, w_down = weights
    positions = jnp.arange(SEQUENCE_TOKENS, dtype=jnp.int32)
    doc_index, starts = doc_layout(seq_lengths, positions)
    offsets = (positions - starts).astype(jnp.float32)
    frequency = theta_base ** (-jnp.arange(HEAD_SIZE // 2, dtype=jnp.float32) * 2.0 / HEAD_SIZE)
    angles = offsets[:, None] * frequency[None, :]
    cosine = jnp.cos(angles)[:, None, :]
    sine_table = jnp.sin(angles)[:, None, :]
    first_normed = reduced_copy(rms_scale(seq_tokens, norm1_gain))
    query_proj = reduced_backward(matmul_product(first_normed, w_query)).reshape(SEQUENCE_TOKENS, QUERY_HEADS, HEAD_SIZE)
    key_projected = reduced_backward(matmul_product(first_normed, key_weight)).reshape(SEQUENCE_TOKENS, KEY_VALUE_HEADS, HEAD_SIZE)
    query_rows = reduced_copy(head_prep(cosine, sine_table, query_proj, q_gain))
    keys = reduced_copy(head_prep(cosine, sine_table, key_projected, k_gain))
    value_rows = reduced_copy(reduced_backward(matmul_product(first_normed, value_weight))).reshape(SEQUENCE_TOKENS, KEY_VALUE_HEADS, HEAD_SIZE)
    distance_grid = positions[:, None] - positions[None, :]
    allowed = (doc_index[:, None] == doc_index[None, :]) & (distance_grid >= 0) & (distance_grid < WINDOW) & ((seq_padding[None, :] == 0) | (distance_grid == 0))
    heads_per_group = QUERY_HEADS // KEY_VALUE_HEADS
    score_scale = HEAD_SIZE ** (-0.5)
    grouped_queries = query_rows.reshape(SEQUENCE_TOKENS, KEY_VALUE_HEADS, heads_per_group, HEAD_SIZE).transpose(1, 2, 0, 3)
    key_groups = keys.transpose(1, 0, 2)
    value_groups = value_rows.transpose(1, 0, 2)

    def head_block(operands):
        query_block, key_block, value_block = operands
        scores = reduced_backward(jnp.einsum('gqd,kd->gqk', query_block, key_block, precision=highest) * score_scale)
        scores = jnp.where(allowed[None], scores, negative)
        soft_weights = jax.nn.softmax(scores, axis=-1)
        return jnp.einsum('gqk,kd->gqd', reduced_copy(soft_weights), value_block, precision=highest)
    mixed_heads = lax.map(jax.checkpoint(head_block), (grouped_queries, key_groups, value_groups))
    heads_out = reduced_copy(reduced_backward(mixed_heads.transpose(2, 0, 1, 3).reshape(SEQUENCE_TOKENS, QUERY_HEADS * HEAD_SIZE)))
    block_size = QUERY_HEADS * HEAD_SIZE // N_TENSOR
    branch = jnp.zeros((SEQUENCE_TOKENS, MODEL_DIM), jnp.float32)
    for part_index in range(N_TENSOR):
        lower_row = part_index * block_size
        branch = branch + reduced_copy(matmul_product(heads_out[:, lower_row:lower_row + block_size], w_out[lower_row:lower_row + block_size]))
    branch = reduced_backward(branch)
    residual2 = seq_tokens + branch
    normed2 = reduced_copy(rms_scale(residual2, norm2_gain))
    logits = reduced_backward(matmul_product(normed2, w_router))
    router_probs = jax.nn.softmax(logits, axis=-1)
    chosen = seq_experts[:, :, None] == jnp.arange(EXPERTS, dtype=jnp.int32)[None, None, :]
    picked = lax.optimization_barrier(jnp.sum(jnp.where(chosen, router_probs[:, None, :], 0.0), axis=2))
    route_gates = picked / lax.optimization_barrier(jnp.sum(picked, axis=1, keepdims=True))
    flat_experts = seq_experts.reshape(-1)
    flat_gates = route_gates.reshape(-1)
    row_limit = N_CONTEXT * ROUTE_MOST
    half_size = FF // N_TENSOR

    def expert_block(operands):
        expert_index, gate_matrix, up_matrix, down_matrix = operands
        matches = flat_experts == expert_index
        found_at = jnp.nonzero(matches, size=row_limit, fill_value=0)[0].astype(jnp.int32)
        slot_used = (jnp.arange(row_limit, dtype=jnp.int32) < jnp.sum(matches.astype(jnp.int32))).astype(jnp.float32)
        token_rows = normed2[found_at // TOPK]
        gate_pre = reduced_backward(matmul_product(token_rows, gate_matrix))
        up_pre = reduced_backward(matmul_product(token_rows, up_matrix))
        hidden = reduced_copy(jax.nn.silu(gate_pre) * up_pre)
        part_list = []
        for part_index in range(N_TENSOR):
            lower_row = part_index * half_size
            part_list.append(reduced_backward(matmul_product(hidden[:, lower_row:lower_row + half_size], down_matrix[lower_row:lower_row + half_size])))
        expert_rows = jnp.stack(part_list, axis=1)
        return (expert_rows * (flat_gates[found_at] * slot_used)[:, None, None], found_at // TOPK)
    contributions, targets = lax.map(jax.checkpoint(expert_block), (jnp.arange(EXPERTS, dtype=jnp.int32), w_gate, w_up, w_down))
    mixture = jnp.zeros((SEQUENCE_TOKENS, N_TENSOR, MODEL_DIM), jnp.float32).at[targets.reshape(-1)].add(contributions.reshape(-1, N_TENSOR, MODEL_DIM))
    expert_mix = jnp.zeros((SEQUENCE_TOKENS, MODEL_DIM), jnp.float32)
    for part_index in range(N_TENSOR):
        expert_mix = expert_mix + reduced_copy(mixture[:, part_index])
    output = residual2 + expert_mix
    kept_rows = (1 - seq_padding).astype(jnp.float32)
    counts = lax.optimization_barrier(jnp.sum(lax.optimization_barrier(jnp.sum(chosen.astype(jnp.float32), axis=1)) * kept_rows[:, None], axis=0))
    prob_sums = lax.optimization_barrier(jnp.sum(router_probs * kept_rows[:, None], axis=0))
    return (output, counts, prob_sums)

def reference(tokens, cotangent, doc_lengths, padding, expert_ids, norm1_gain, w_query, key_weight, value_weight, q_gain, k_gain, w_out, norm2_gain, w_router, w_gate, w_up, w_down):
    weights = tuple((weight_item.astype(jnp.float32) for weight_item in (norm1_gain, w_query, key_weight, value_weight, q_gain, k_gain, w_out, norm2_gain, w_router, w_gate, w_up, w_down)))
    inputs = tokens.astype(jnp.float32)

    def forward(inputs, weights):

        def scan_step(carried, operands):
            seq_tokens, seq_lengths, seq_padding, seq_experts = operands
            output, counts, prob_sums = jax.checkpoint(sequence_forward)(weights, seq_tokens, seq_lengths, seq_padding, seq_experts)
            return ((carried[0] + counts, carried[1] + prob_sums), output)
        initial = (jnp.zeros((EXPERTS,), jnp.float32), jnp.zeros((EXPERTS,), jnp.float32))
        totals, outputs = lax.scan(scan_step, initial, (inputs, doc_lengths, padding, expert_ids))
        return (outputs, totals)
    (outputs, totals), pullback = jax.vjp(forward, inputs, weights)
    zero_pair = (jnp.zeros((EXPERTS,), jnp.float32), jnp.zeros((EXPERTS,), jnp.float32))
    grad_tokens, grad_weights = pullback((cotangent.astype(jnp.float32), zero_pair))
    kept_total = jnp.sum((1 - padding).astype(jnp.float32))
    load_share = totals[0] / (kept_total * TOPK)
    balance_loss = EXPERTS * jnp.sum(load_share * (totals[1] / kept_total))
    expert_load = EXPERTS * load_share
    return (outputs, balance_loss, expert_load, grad_tokens, grad_weights[0], grad_weights[1], grad_weights[2], grad_weights[3], grad_weights[4], grad_weights[5], grad_weights[6], grad_weights[7], grad_weights[8], grad_weights[9], grad_weights[10], grad_weights[11])
```

```python
import jax
import jax.numpy as jnp
from jax import lax
from jax.experimental import pallas as pl
from jax.experimental.pallas import tpu as pltpu
from jax.sharding import PartitionSpec as P

WINDOW = 1024
SIDE = 4
HALF = 64
QUERY_BLOCK = 256
SLOTS = 32
EXTRA = 128
SMALL = 16

epsilon = 1e-06
theta_base = 1000000.0
negative = -1e30
f32 = jnp.float32
bf16 = jnp.bfloat16
vmem_limit = 56 * 1024 * 1024
whole = pl.BlockSpec(memory_space=pltpu.VMEM)
scalars = pl.BlockSpec(memory_space=pltpu.SMEM)


def call(kernel, in_specs, out_shape, flops=10**6, moved=10**6, **rest):
    if in_specs is not None:
        rest["in_specs"] = in_specs
    return pl.pallas_call(
        kernel,
        out_shape=[jax.ShapeDtypeStruct(shape, kind) for shape, kind in out_shape],
        compiler_params=pltpu.CompilerParams(vmem_limit_bytes=vmem_limit),
        cost_estimate=pl.CostEstimate(flops=flops, bytes_accessed=moved, transcendentals=0),
        **rest,
    )


def dot_nt(left, right):
    return lax.dot_general(left, right, (((1,), (1,)), ((), ())), preferred_element_type=f32)


def dot_tn(left, right):
    return lax.dot_general(left, right, (((0,), (0,)), ((), ())), preferred_element_type=f32)


def dot_nn(left, right):
    return jnp.dot(left, right, preferred_element_type=f32)


def join(parts, axis=0):
    return jnp.concatenate(parts, axis=axis)


def ring_moves(axis, target):
    forward = []
    backward = []
    count = lax.axis_size(axis)
    for i in range(count):
        for core, sign in ((0, 1), (1, -1)):
            forward.append((2 * i + core, 2 * target(i, sign) + core))
            backward.append((2 * i + core, 2 * target(i, -sign) + core))

    def move(pairs):
        return lambda value: lax.ppermute(value, (axis, "tensor"), pairs)

    return move(forward), move(backward)


def moves_z():
    return ring_moves("context", lambda i, step: (i // SIDE) * SIDE + (i + step) % SIDE)


def moves_x():
    return ring_moves("context", lambda i, step: (i + SIDE * step) % (SIDE * SIDE))


def moves_y():
    return ring_moves("fsdp", lambda i, step: (i + step) % SIDE)


def other_core(value):
    return lax.ppermute(value, "tensor", [(0, 1), (1, 0)])


def after(value, *events):
    return lax.optimization_barrier((value, *events))[0]


def ring_gather(value, moves):
    behind = moves[0](value)
    ahead = moves[1](value)
    far = moves[0](behind)
    return [value, ahead, far, behind]


def add_low(left, right):
    return (left.astype(f32) + right.astype(f32)).astype(bf16)


def low_sum(terms):
    return sum(term.astype(f32) for term in terms).astype(bf16)


def across(value, step):
    pairs = [(i, i ^ (SIDE * step)) for i in range(SIDE * SIDE)]
    return lax.ppermute(value, "context", pairs)


def along_z(value, step):
    pairs = [(i, (i // SIDE) * SIDE + (i + step) % SIDE) for i in range(SIDE * SIDE)]
    return lax.ppermute(value, "context", pairs)


def ring_scatter(parts, moves):
    passing = moves[0](parts[2])
    from_ahead = moves[1](parts[3])
    from_behind = moves[0](add_low(parts[1], passing))
    return parts[0], from_behind, from_ahead


def together(*values):
    return lax.optimization_barrier(values)


def stack_kernel(a, b, c, d, result):
    for i, part in enumerate((a, b, c, d)):
        result[i] = part[...]


def stack(parts):
    shape = parts[0].shape
    return call(stack_kernel, [whole] * 4, [((4,) + shape, bf16)])(*parts)[0]


def two_gathers(left, right, left_moves, right_moves, events=(), last=()):
    left_behind = left_moves[0](left)
    left_ahead = left_moves[1](left)
    right_behind = right_moves[0](right)
    right_ahead = right_moves[1](right)
    left_behind, left_ahead, right_behind, right_ahead = together(
        left_behind, left_ahead, right_behind, right_ahead, *events
    )[:4]
    left_far = left_moves[0](left_behind)
    right_far = right_moves[0](right_behind)
    left_far, right_far = together(left_far, right_far, *last)[:2]
    return [left, left_ahead, left_far, left_behind], [right, right_ahead, right_far, right_behind]


def plane_gather(first, second, events=((), (), (), ())):
    first_near, second_near = two_gathers(first, second, moves_z(), moves_x(), *events[:2])
    first_pieces, second_pieces = two_gathers(
        stack(first_near), stack(second_near), moves_x(), moves_z(), *events[2:]
    )
    return first_pieces + second_pieces


def unstack_kernel(a, b, c, r0, r1, r2, r3):
    for i, part in enumerate((r0, r1, r2, r3)):
        part[...] = (a[i].astype(f32) + b[i].astype(f32) + c[i].astype(f32)).astype(bf16)


def unstack(terms):
    shape = terms[0].shape[1:]
    return call(unstack_kernel, [whole] * 3, [(shape, bf16)] * 4)(*terms)


def total_kernel(a, b, c, d, e, f, result):
    result[:HALF] = a[...].astype(f32) + b[...].astype(f32) + c[...].astype(f32)
    result[HALF:] = d[...].astype(f32) + e[...].astype(f32) + f[...].astype(f32)


def two_scatters(left, right, left_moves, right_moves, events=(), last=()):
    left_passing = left_moves[0](left[2])
    left_from_ahead = left_moves[1](left[3])
    right_passing = right_moves[0](right[2])
    right_from_ahead = right_moves[1](right[3])
    left_passing, left_from_ahead, right_passing, right_from_ahead, *events = together(
        left_passing, left_from_ahead, right_passing, right_from_ahead, *events
    )
    left_from_behind = left_moves[0](add_low(left[1], left_passing))
    right_from_behind = right_moves[0](add_low(right[1], right_passing))
    left_from_behind, right_from_behind, *last = together(left_from_behind, right_from_behind, *last)
    left_terms = (left[0], left_from_behind, left_from_ahead)
    right_terms = (right[0], right_from_behind, right_from_ahead)
    return left_terms, right_terms, events, last


def plane_scatter(pieces, events=((), (), (), ())):
    first, second, *_ = two_scatters(pieces[:4], pieces[4:], moves_x(), moves_z(), *events[:2])
    first, second, *_ = two_scatters(unstack(first), unstack(second), moves_z(), moves_x(), *events[2:])
    width = pieces[0].shape[-1]
    return call(total_kernel, [whole] * 6, [((2 * HALF, width), f32)])(*first, *second)[0]


def scatter_chain(arrays, moves):
    done = []
    results = []

    def step(move, value):
        done.append(move(after(value, *done[-2:-1])))
        return done[-1]

    for parts in arrays:
        passing = step(moves[0], parts[2])
        from_ahead = step(moves[1], parts[3])
        from_behind = step(moves[0], add_low(parts[1], passing))
        results.append((passing, from_ahead, from_behind))
    return results


def split_low(value, count):
    parts = []
    rest = value
    for _ in range(count):
        part = rest.astype(bf16)
        parts.append(part)
        rest = rest - part.astype(f32)
    return parts


def core_columns(core, width):
    return pl.ds(pl.multiple_of(core * width, width), width)


def token_message_kernel(info, tokens, ids, padding, first, second, inverse_out):
    width = tokens.shape[1]
    half = width // 2
    rows = tokens[...].astype(f32)
    inverse = lax.rsqrt(jnp.mean(rows * rows, axis=-1, keepdims=True) + epsilon)
    inverse_out[...] = inverse
    lanes = lax.broadcasted_iota(jnp.int32, (rows.shape[0], EXTRA), 1)
    marks = jnp.zeros((rows.shape[0], EXTRA), f32)
    for k in range(8):
        marks = jnp.where(lanes == k, ids[:, k : k + 1].astype(f32), marks)
    marks = jnp.where(lanes == 8, padding[...].astype(f32), marks)
    for k, part in enumerate(split_low(inverse, 3)):
        marks = jnp.where(lanes == 9 + k, part.astype(f32), marks)
    marks = marks.astype(bf16)
    own = tokens[:, core_columns(info[0], half)]
    first[:, :half] = own[:HALF]
    first[:, half:] = marks[:HALF]
    second[:, :half] = own[HALF:]
    second[:, half:] = marks[HALF:]


def dense_message_kernel(info, query, key, value, out, router, gain1, gain2, q_gain, k_gain, result):
    size = query.shape[1]
    experts = router.shape[0]
    result[:size] = query[...].T
    result[size : 2 * size] = key[...].T
    result[2 * size : 3 * size] = value[...].T
    result[3 * size : 4 * size] = out[...]
    result[4 * size : 4 * size + experts] = router[...]
    base = 4 * size + experts
    rows = lax.broadcasted_iota(jnp.int32, (SMALL, result.shape[1]), 0)
    gains = jnp.where(rows == 0, gain1[...].astype(f32), 0.0)
    gains = jnp.where(rows == 1, gain2[...].astype(f32), gains)
    rest = jnp.zeros((1, result.shape[1] - q_gain.shape[1]), f32)
    gains = jnp.where(rows == 2, join([q_gain[...].astype(f32), rest], 1), gains)
    gains = jnp.where(rows == 3, join([k_gain[...].astype(f32), rest], 1), gains)
    result[base:] = gains.astype(bf16)


def dense_split_kernel(info, a, b, c, d, own, away, own_out, away_out, out, extra):
    shard = a.shape[1]
    rows = own.shape[0]
    size = out.shape[0]
    core = info[0]
    for i, piece in enumerate((a, b, c, d)):
        place = info[4 + i]
        columns = core_columns(place % 2, shard)

        @pl.when(place // 2 == core)
        def _():
            own[:, columns] = piece[:rows]
            own_out[:, columns] = piece[rows : rows + size]

        @pl.when(place // 2 != core)
        def _():
            away[:, columns] = piece[:rows]
            away_out[:, columns] = piece[rows : rows + size]

        columns = core_columns(place, shard)
        out[:, columns] = piece[rows : rows + size]
        extra[:, columns] = piece[rows + size :]


def slots_kernel(info, *refs):
    pieces, (chosen, pads) = refs[:8], refs[8:]
    first_expert = info[1]
    place_x, place_z, sign = info[8], info[9], info[10]
    shape = (2 * HALF, EXTRA)
    lanes = lax.broadcasted_iota(jnp.int32, shape, 1)
    rows = lax.broadcasted_iota(jnp.int32, shape, 0)
    earlier = (lanes < rows).astype(bf16)
    pad_total = jnp.zeros((1, EXTRA), f32)
    for ix in range(SIDE):
        for iz in range(SIDE):
            marks = join([pieces[ix][iz], pieces[4 + iz][ix]]).astype(f32)
            pad_total += jnp.sum(marks, axis=0, keepdims=True)
            named = jnp.zeros(shape, f32)
            for e in range(EXTRA // SLOTS):
                hit = jnp.where((lanes < 8) & (marks == (first_expert + e).astype(f32)), 1.0, 0.0)
                hit = jnp.max(hit, axis=-1, keepdims=True)
                named = jnp.where(lanes // SLOTS == e, hit, named)
            ranks = dot_nn(earlier, named.astype(bf16))
            match = (named > 0.0) & (ranks == (lanes % SLOTS).astype(f32))
            place = ((place_x + sign * ix) % SIDE) * SIDE + (place_z + sign * iz) % SIDE
            chosen[place] = jnp.where(match, 1.0, 0.0).astype(bf16)
    pads[...] = jnp.broadcast_to(pad_total, pads.shape)


def write_slots(result, place, columns, slots):
    for e in range(EXTRA // SLOTS):
        target = pl.ds(pl.multiple_of(place * SLOTS, SLOTS), SLOTS)
        result[e, target, columns] = slots[e * SLOTS : (e + 1) * SLOTS]


def read_slots(source, place, columns):
    target = pl.ds(pl.multiple_of(place * SLOTS, SLOTS), SLOTS)
    return join([source[e, target, columns] for e in range(EXTRA // SLOTS)])


def pick_rows_kernel(info, chosen, *refs):
    own, other, (result, extra) = refs[:8], refs[8:16], refs[16:]
    core, place_x, place_z, sign = info[0], info[8], info[9], info[10]
    half = result.shape[-1] // 2
    own_columns = core_columns(core, half)
    other_columns = core_columns(1 - core, half)
    for ix in range(SIDE):
        for iz in range(SIDE):
            place = ((place_x + sign * ix) % SIDE) * SIDE + (place_z + sign * iz) % SIDE
            matrix = chosen[place]
            rows = join([own[ix][iz], own[4 + iz][ix]])
            slots = dot_tn(matrix, rows).astype(bf16)
            write_slots(result, place, own_columns, slots[:, :half])
            write_slots(extra, place, slice(None), slots[:, half:])
            jx, jz = -ix % SIDE, -iz % SIDE
            rows = join([other[jx][jz, :, :half], other[4 + jz][jx, :, :half]])
            write_slots(result, place, other_columns, dot_tn(matrix, rows).astype(bf16))


def pick_spans_kernel(info, chosen, own, other, result):
    core = info[0]
    half = own.shape[-1]
    for place in range(SIDE * SIDE):
        matrix = chosen[place]
        write_slots(result, place, core_columns(core, half), dot_tn(matrix, own[place]).astype(bf16))
        write_slots(result, place, core_columns(1 - core, half), dot_tn(matrix, other[place]).astype(bf16))


def put_rows_kernel(info, chosen, own, came, extra, *pieces):
    place_x, place_z, sign = info[8], info[9], info[10]
    half = own.shape[-1]
    for ix in range(SIDE):
        for iz in range(SIDE):
            place = ((place_x + sign * ix) % SIDE) * SIDE + (place_z + sign * iz) % SIDE
            matrix = chosen[place]
            rows = read_slots(own, place, slice(None)).astype(f32) + read_slots(came, place, slice(None)).astype(f32)
            rows = dot_nn(matrix, rows.astype(bf16)).astype(bf16)
            marks = dot_nn(matrix, read_slots(extra, place, slice(None))).astype(bf16)
            pieces[ix][iz, :, :half] = rows[:HALF]
            pieces[4 + iz][ix, :, :half] = rows[HALF:]
            pieces[ix][iz, :, half:] = marks[:HALF]
            pieces[4 + iz][ix, :, half:] = marks[HALF:]


def put_sums_kernel(info, chosen, own, came, *pieces):
    place_x, place_z, sign = info[8], info[9], info[10]
    for ix in range(SIDE):
        for iz in range(SIDE):
            place = ((place_x + sign * ix) % SIDE) * SIDE + (place_z + sign * iz) % SIDE
            rows = read_slots(own, place, slice(None)).astype(f32) + read_slots(came, place, slice(None)).astype(f32)
            rows = dot_nn(chosen[place], rows.astype(bf16)).astype(bf16)
            pieces[ix][iz] = rows[:HALF]
            pieces[4 + iz][ix] = rows[HALF:]


def span_of(info, ix, iz):
    return ((info[8] + info[10] * ix) % SIDE) * SIDE + (info[9] + info[10] * iz) % SIDE


def piece_parts(info, i):
    for j in range(SIDE):
        if i < SIDE:
            yield j, span_of(info, i, j), slice(0, HALF)
        else:
            yield j, span_of(info, j, i - SIDE), slice(HALF, 2 * HALF)


def project_kernel(info, gain, own, came, *refs):
    pieces, (own_out, other_out, normed_out) = refs[:8], refs[8:]
    half = gain.shape[1]
    wide = own_out.shape[-1]
    count = SIDE * HALF
    lanes = lax.broadcasted_iota(jnp.int32, (count, EXTRA), 1)
    for i, piece in enumerate(pieces):
        rows = piece[...].reshape(count, half + EXTRA)
        marks = jnp.where((lanes >= 9) & (lanes < 12), rows[:, half:].astype(f32), 0.0)
        inverse = jnp.sum(marks, axis=-1, keepdims=True)
        normed = (rows[:, :half].astype(f32) * inverse * gain[...]).astype(bf16)
        own_rows = dot_nt(normed, own[...])
        other_rows = dot_nt(normed, came[...])
        for j, span, part in piece_parts(info, i):
            cut = slice(j * HALF, (j + 1) * HALF)
            normed_out[span, part] = normed[cut]
            own_out[span, part] = own_rows[cut]
            other_out[span, part] = other_rows[cut]


def turn(value, cosine, sine):
    return value * cosine + pltpu.roll(value, 64, 1) * sine


def block_mask(doc_rows, doc_columns, real, query_start, key_start, query_count, key_count):
    rows = lax.broadcasted_iota(jnp.int32, (query_count, key_count), 0)
    columns = lax.broadcasted_iota(jnp.int32, (query_count, key_count), 1)
    distance = rows - columns + (query_start - key_start)
    positions = lax.broadcasted_iota(jnp.int32, (1, key_count), 1) + key_start
    doc_columns = jnp.where(positions < real, doc_columns, -1)
    inside = (distance >= 0) & (distance < WINDOW) & (doc_rows == doc_columns)
    return inside | (distance == 0)


def real_count(pads, count):
    return (count - pads[0:1, 8:9]).astype(jnp.int32)


def attend_kernel(
    own, came, cosine, sine, gains, doc_rows, doc_columns, pads,
    mixed, raw, queries, keys, values, log_totals,
):
    count = queries.shape[0]
    size = queries.shape[1]
    span = mixed.shape[1]
    scale = size ** (-0.5)

    def prepare(j, carry):
        rows = pl.ds(pl.multiple_of(j * span, span), span)
        block = own[j] + came[j]
        raw[rows, :] = block[:, : 2 * size]
        cos_rows = cosine[rows, :]
        sin_rows = sine[rows, :]
        for part, target in ((0, queries), (1, keys)):
            piece = block[:, part * size : (part + 1) * size]
            inverse = lax.rsqrt(jnp.mean(piece * piece, axis=-1, keepdims=True) + epsilon)
            normed = piece * inverse * gains[part : part + 1, :]
            target[rows, :] = turn(normed, cos_rows, sin_rows).astype(bf16)
        values[rows, :] = block[:, 2 * size :].astype(bf16)
        return carry

    lax.fori_loop(0, count // span, prepare, 0)
    real = real_count(pads, float(count))
    for start in range(0, count, QUERY_BLOCK):
        low = max(0, start - WINDOW)
        high = start + QUERY_BLOCK
        scores = dot_nt(queries[start:high, :], keys[low:high, :]) * scale
        allowed = block_mask(
            doc_rows[start:high, :], doc_columns[:, low:high], real, start, low, QUERY_BLOCK, high - low
        )
        scores = jnp.where(allowed, scores, negative)
        peak = jnp.max(scores, axis=-1, keepdims=True)
        exponent = jnp.exp(scores - peak)
        total = jnp.sum(exponent, axis=-1, keepdims=True)
        weights = (exponent * (1.0 / total)).astype(bf16)
        rows = dot_nn(weights, values[low:high, :]).astype(bf16)
        mixed[start // span : high // span] = rows.reshape(QUERY_BLOCK // span, span, size)
        log_totals[start:high, :] = peak + jnp.log(total)


def attend_back_kernel(
    grad_mixed, raw, queries, keys, values, log_totals, cosine, sine, gains, doc_rows, doc_columns, pads,
    grads, gain_grads, grad_queries, grad_keys, grad_values,
):
    count = queries.shape[0]
    size = queries.shape[1]
    span = grads.shape[1]
    scale = size ** (-0.5)
    grad_keys[...] = jnp.zeros_like(grad_keys)
    grad_values[...] = jnp.zeros_like(grad_values)
    real = real_count(pads, float(count))
    for start in range(0, count, QUERY_BLOCK):
        low = max(0, start - WINDOW)
        high = start + QUERY_BLOCK
        query_rows = queries[start:high, :]
        key_rows = keys[low:high, :]
        grad_rows = grad_mixed[start:high, :]
        scores = dot_nt(query_rows, key_rows) * scale
        allowed = block_mask(
            doc_rows[start:high, :], doc_columns[:, low:high], real, start, low, QUERY_BLOCK, high - low
        )
        soft = jnp.where(allowed, jnp.exp(scores - log_totals[start:high, :]), 0.0)
        grad_soft = dot_nt(grad_rows, values[low:high, :])
        row_dot = jnp.sum(soft * grad_soft, axis=-1, keepdims=True)
        grad_scores = (soft * (grad_soft - row_dot)).astype(bf16)
        grad_queries[start:high, :] = dot_nn(grad_scores, key_rows) * scale
        grad_keys[low:high, :] += dot_tn(grad_scores, query_rows) * scale
        grad_values[low:high, :] += dot_tn(soft.astype(bf16), grad_rows)
    gain_grads[...] = jnp.zeros_like(gain_grads)

    def finish(j, carry):
        rows = pl.ds(pl.multiple_of(j * span, span), span)
        cos_rows = cosine[rows, :]
        sin_rows = sine[rows, :]
        parts = []
        for part, source in ((0, grad_queries), (1, grad_keys)):
            piece = raw[rows, part * size : (part + 1) * size]
            inverse = lax.rsqrt(jnp.mean(piece * piece, axis=-1, keepdims=True) + epsilon)
            back = turn(source[rows, :], cos_rows, -sin_rows)
            gain_grads[part : part + 1, :] += jnp.sum(back * piece * inverse, axis=0, keepdims=True)
            scaled = back * gains[part : part + 1, :]
            mean = jnp.mean(scaled * piece, axis=-1, keepdims=True)
            parts.append((inverse * scaled - piece * (inverse * inverse * inverse * mean)).astype(bf16))
        parts.append(grad_values[rows, :].astype(bf16))
        grads[j] = join(parts, 1)
        return carry

    lax.fori_loop(0, count // span, finish, 0)


def out_kernel(info, mixed, came_mixed, own, came, *pieces):
    for i, piece in enumerate(pieces):
        parts = list(piece_parts(info, i))
        left = join([mixed[span, part] for _, span, part in parts])
        right = join([came_mixed[span, part] for _, span, part in parts])
        rows = dot_nn(left, own[...]) + dot_nn(right, came[...])
        piece[...] = rows.astype(bf16).reshape(piece.shape)


def heads_back_kernel(rows, weight, result):
    for i in range(weight.shape[0]):
        result[i] = dot_nt(rows[...], weight[i]).astype(bf16)


def out_grad_kernel(mixed, came_mixed, rows, own_out, away_out):
    size = mixed.shape[-1]
    count = mixed.shape[0] * mixed.shape[1]
    grads = rows[...].reshape(count, rows.shape[-1])
    own_out[...] = dot_tn(mixed[...].reshape(count, size), grads).astype(bf16)
    away_out[...] = dot_tn(came_mixed[...].reshape(count, size), grads).astype(bf16)


def input_back_kernel(info, grads, came_grads, own, came, *refs):
    tokens, mixture, pieces, gain_grad = refs[:8], refs[8:16], refs[16:24], refs[24]
    half = own.shape[1]
    count = SIDE * HALF
    lanes = lax.broadcasted_iota(jnp.int32, (count, EXTRA), 1)
    total = jnp.zeros((1, half), f32)
    for i, piece in enumerate(pieces):
        parts = list(piece_parts(info, i))
        left = join([grads[span, part] for _, span, part in parts])
        right = join([came_grads[span, part] for _, span, part in parts])
        rows = dot_nn(left, own[...]) + dot_nn(right, came[...])
        piece[:, :, :half] = rows.astype(bf16).reshape(SIDE, HALF, half)
        piece[:, :, half:] = mixture[i][...]
        source = tokens[i][...].reshape(count, half + EXTRA)
        marks = jnp.where((lanes >= 9) & (lanes < 12), source[:, half:].astype(f32), 0.0)
        inverse = jnp.sum(marks, axis=-1, keepdims=True)
        total += jnp.sum(rows * (source[:, :half].astype(f32) * inverse), axis=0, keepdims=True)
    gain_grad[...] = jnp.broadcast_to(total, gain_grad.shape)


def project_grad_kernel(grads, came_grads, normed, own_out, away_out):
    count = normed.shape[0] * normed.shape[1]
    wide = grads.shape[-1]
    rows = normed[...].reshape(count, normed.shape[-1])
    own_out[...] = dot_tn(grads[...].reshape(count, wide), rows).astype(bf16)
    away_out[...] = dot_tn(came_grads[...].reshape(count, wide), rows).astype(bf16)


def halves(core, own, came):
    return join([jnp.where(core == 0, own, came), jnp.where(core == 0, came, own)], 1)


def chosen_experts(ids, count):
    lanes = lax.broadcasted_iota(jnp.int32, (ids.shape[0], count), 1)
    chosen = jnp.zeros((ids.shape[0], count), f32)
    for k in range(8):
        chosen = jnp.where(lanes == ids[:, k : k + 1], 1.0, chosen)
    return chosen


def router_kernel(
    info, tokens, own, came, ids, extra, residual_out, inverse_out, normed_out, probs_out, gates_out, total_out, first, second
):
    core = info[0]
    half = tokens.shape[1] // 2
    experts = probs_out.shape[1]
    residual = tokens[...].astype(f32) + halves(core, own[...], came[...])
    residual_out[...] = residual
    inverse = lax.rsqrt(jnp.mean(residual * residual, axis=-1, keepdims=True) + epsilon)
    inverse_out[...] = inverse
    gain = extra[experts + 1 : experts + 2, :].astype(f32)
    normed = (residual * inverse * gain).astype(bf16)
    normed_out[...] = normed
    logits = dot_nt(normed, extra[:experts, :])
    exponent = jnp.exp(logits - jnp.max(logits, axis=-1, keepdims=True))
    probs = exponent / jnp.sum(exponent, axis=-1, keepdims=True)
    probs_out[...] = probs
    chosen = chosen_experts(ids, experts)
    picked = probs * chosen
    total = jnp.sum(picked, axis=-1, keepdims=True)
    total_out[...] = total
    gates = picked / total
    gates_out[...] = gates
    marks = join(split_low(gates, 2), 1)
    mine = normed_out[:, core_columns(core, half)]
    first[:, :half] = mine[:HALF]
    first[:, half:] = marks[:HALF]
    second[:, :half] = mine[HALF:]
    second[:, half:] = marks[HALF:]


def router_back_kernel(
    info, own, came, residual_ref, inverse_ref, normed, probs_ref, gates_ref, total, ids, padding, cotangent, extra,
    grad_low, grad_half, grad_out, rows_out,
):
    core = info[0]
    half = cotangent.shape[1] // 2
    experts = probs_ref.shape[1]
    probs = probs_ref[...]
    gates = gates_ref[...]
    residual = residual_ref[...]
    inverse = inverse_ref[...]
    marks = own[:, half:] + came[:, half:]
    gate_grads = marks[:, :experts] + marks[:, experts:]
    chosen = chosen_experts(ids, experts)
    grad_picked = (gate_grads - jnp.sum(gate_grads * gates, axis=-1, keepdims=True)) / total[...]
    grad_probs = chosen * grad_picked
    grad_logits = (probs * (grad_probs - jnp.sum(grad_probs * probs, axis=-1, keepdims=True))).astype(bf16)
    grad_normed = halves(core, own[:, :half], came[:, :half]) + dot_nn(grad_logits, extra[:experts, :])
    scaled = grad_normed * extra[experts + 1 : experts + 2, :].astype(f32)
    mean = jnp.mean(scaled * residual, axis=-1, keepdims=True)
    grad = cotangent[...].astype(f32) + inverse * scaled - residual * (inverse * inverse * inverse * mean)
    grad_out[...] = grad
    grad_low[...] = grad.astype(bf16)
    grad_half[...] = grad_low[:, core_columns(core, half)]
    gain_grad = jnp.sum(grad_normed * residual * inverse, axis=0, keepdims=True)
    rows_out[:experts] = dot_tn(grad_logits, normed[...]).astype(bf16)
    kept = 1.0 - padding[...].astype(f32)
    shard = 4 * EXTRA
    rest = jnp.zeros((1, shard - experts), f32)

    def row(values):
        return join([values, rest] * SIDE, 1)

    counted = chosen * kept
    probs_sum = jnp.sum(probs * kept, axis=0, keepdims=True)
    probs_high = probs_sum.astype(bf16).astype(f32)
    kept_sum = jnp.broadcast_to(jnp.sum(kept, axis=0, keepdims=True), (1, experts))
    rows = (
        gain_grad,
        row(jnp.sum(counted[:HALF], axis=0, keepdims=True)),
        row(jnp.sum(counted[HALF:], axis=0, keepdims=True)),
        row(probs_high),
        row(probs_sum - probs_high),
        row(kept_sum),
    )
    numbers = lax.broadcasted_iota(jnp.int32, (SMALL, 2 * half), 0)
    small = jnp.zeros((SMALL, 2 * half), f32)
    for i, values in enumerate(rows):
        small = jnp.where(numbers == i, values, small)
    rows_out[experts:] = small.astype(bf16)


def final_rows_kernel(info, own, came, tokens, inverse_ref, extra, grad_residual, residual, grad_input, result):
    core = info[0]
    half = own.shape[1] // 2
    base = extra.shape[0] - SMALL
    rows = tokens[...].astype(f32)
    inverse = inverse_ref[...]
    scaled = halves(core, own[:, :half], came[:, :half]) * extra[base : base + 1, :].astype(f32)
    mean = jnp.mean(scaled * rows, axis=-1, keepdims=True)
    grad_input[...] = grad_residual[...] + inverse * scaled - rows * (inverse * inverse * inverse * mean)
    result[...] = residual[...] + halves(core, own[:, half:], came[:, half:])


def expert_kernel(info, rows, marks, grads, pairs_w, downs_w, back_own, back_other, back_marks, hidden_out, pairs_out):
    core = info[0]
    expert = info[1] + pl.program_id(0)
    shard = pairs_w.shape[2]
    count = rows.shape[1]
    units = hidden_out.shape[2]
    pairs = grad_raw = 0.0
    for place in range(SIDE):
        columns = slice(place * shard, (place + 1) * shard)
        pairs += dot_nn(rows[0, :, columns], pairs_w[place, 0])
        grad_raw += dot_nt(grads[0, :, columns], downs_w[place, 0])
    gate_pre = pairs[:, :units]
    up_pre = pairs[:, units:]
    lanes = lax.broadcasted_iota(jnp.int32, (count, EXTRA), 1)
    high_lane = lanes == expert
    low_lane = lanes == expert + EXTRA // 2
    gates = jnp.sum(jnp.where(high_lane | low_lane, marks[0].astype(f32), 0.0), axis=-1, keepdims=True)
    sigmoid = jax.nn.sigmoid(gate_pre)
    activated = gate_pre * sigmoid
    hidden = (activated * up_pre).astype(bf16).astype(f32)
    gate_grads = jnp.sum(hidden * grad_raw, axis=-1, keepdims=True)
    grad_hidden = gates * grad_raw
    gate_low = (grad_hidden * up_pre * sigmoid * (1.0 + gate_pre * (1.0 - sigmoid))).astype(bf16)
    up_low = (grad_hidden * activated).astype(bf16)
    hidden_out[0] = (gates * hidden).astype(bf16)
    pairs_low = join([gate_low, up_low], 1)
    pairs_out[0] = pairs_low
    for place in range(SIDE):
        near = slice((place % 2) * shard, (place % 2 + 1) * shard)
        result = dot_nt(pairs_low, pairs_w[place, 0]).astype(bf16)

        @pl.when(place // 2 == core)
        def _():
            back_own[0, :, near] = result

        @pl.when(place // 2 != core)
        def _():
            back_other[0, :, near] = result

    high = gate_grads.astype(bf16).astype(f32)
    low = gate_grads - high
    back_marks[0] = (jnp.where(high_lane, high, 0.0) + jnp.where(low_lane, low, 0.0)).astype(bf16)


def expert_grad_kernel(info, rows, pairs, *refs):
    gate_grads, up_grads = refs[:4], refs[4:]
    shard, units = gate_grads[0].shape[1:]
    for i in range(SIDE):
        result = dot_tn(rows[0, :, core_columns(info[4 + i], shard)], pairs[0]).astype(bf16)
        gate_grads[i][0] = result[:, :units]
        up_grads[i][0] = result[:, units:]


def expert_out_kernel(info, grads, hidden, downs_w, out_own, out_other, *down_grads):
    core = info[0]
    shard = downs_w.shape[3]
    for i in range(SIDE):
        place = info[4 + i]
        down_grads[i][0] = dot_tn(hidden[0], grads[0, :, core_columns(place, shard)]).astype(bf16)
        result = dot_nn(hidden[0], downs_w[place, 0]).astype(bf16)
        near = core_columns(place % 2, shard)

        @pl.when(place // 2 == core)
        def _():
            out_own[0, :, near] = result

        @pl.when(place // 2 != core)
        def _():
            out_other[0, :, near] = result


def by_expert(shape):
    if len(shape) == 4:
        return pl.BlockSpec((shape[0], 1) + tuple(shape[2:]), lambda e: (0, e, 0, 0))
    return pl.BlockSpec((1,) + tuple(shape[1:]), lambda e: (e, 0, 0))


def per_expert(kernel, info, arrays, out_shapes, flops, moved):
    return call(
        kernel,
        [scalars] + [by_expert(array.shape) for array in arrays],
        [(shape, bf16) for shape in out_shapes],
        flops=flops,
        moved=moved,
        out_specs=[by_expert(shape) for shape in out_shapes],
        grid=(arrays[0].shape[0],),
    )(info, *arrays)


def project_chunk_kernel(info, own, came, gain, gain_came, heads, heads_came, out, out_came, extra, *pieces):
    core = info[0]
    shard = pieces[0].shape[1]
    size = out.shape[0]
    numbers = lax.broadcasted_iota(jnp.int32, (SMALL, shard), 0)
    both = heads[...] + heads_came[...]
    rest = jnp.zeros((1, shard - 2 * size), f32)
    head_row = join([both[0:1], both[1:2], rest], 1)
    for i in range(SIDE):
        place = info[4 + i]
        columns = core_columns(place % 2, shard)
        near = place // 2 == core
        block = jnp.where(near, own[:, columns], came[:, columns])
        pieces[i][:size] = block[:size]
        pieces[SIDE + i][...] = block[size:]
        gain_row = jnp.where(near, gain[0:1, columns], gain_came[0:1, columns])
        small = jnp.where(numbers == 0, gain_row, jnp.where(numbers == 1, head_row, 0.0))
        pieces[i][size : 2 * size] = jnp.where(near, out[:, columns], out_came[:, columns])
        pieces[i][2 * size : 2 * size + extra.shape[0]] = extra[:, core_columns(place, shard)]
        pieces[i][2 * size + extra.shape[0] :] = small.astype(bf16)


def project_final_kernel(info, parts, query, out_grad, router, gain1, gain2, head_gains, load, loss, total):
    step = pl.program_id(0)
    size = out_grad.shape[0] // parts.shape[0]
    rest = 0.0
    for i in range(parts.shape[0]):
        block = parts[i].astype(f32)
        query[:, i * size : (i + 1) * size] = block[:size].T
        out_grad[i * size : (i + 1) * size] = block[size : 2 * size]
        rest += block[2 * size :]

    @pl.when(step == 0)
    def _():
        total[...] = rest

    @pl.when(step > 0)
    def _():
        total[...] += rest

    @pl.when(step == pl.num_programs(0) - 1)
    def _():
        experts = router.shape[0]
        router[...] = total[:experts]

        def row(i):
            return total[experts + i : experts + i + 1, :]

        gain2[...] = row(0)
        counts = row(1)[:, :experts] + row(2)[:, :experts]
        probs = row(3)[:, :experts] + row(4)[:, :experts]
        kept = row(5)[:, :experts]
        share = counts / (kept * 8.0)
        load[...] = share * float(experts)
        loss[...] = float(experts) * jnp.sum(share * (probs / kept), axis=-1, keepdims=True)
        gain1[...] = row(SMALL)
        count = head_gains.shape[1]
        for part in range(2):
            sums = row(SMALL + 1)[:, part * size : (part + 1) * size]
            sums = pltpu.roll(jnp.broadcast_to(sums, (8, size)), (size - info[2] * count) % size, 1)
            head_gains[part : part + 1] = sums[:1, :count]


def key_value_kernel(info, mine, other, key, value):
    size = key.shape[1] // 2
    for group in range(2):
        cut = slice(group * size, (group + 1) * size)
        block = jnp.where(info[11] == group, mine[...].astype(f32), other[...].astype(f32))
        key[:, cut] = block[:size].T
        value[:, cut] = block[size:].T


def body(
    tokens,
    cotangent,
    doc_lengths,
    padding,
    expert_ids,
    norm1_gain,
    w_query,
    key_weight,
    value_weight,
    q_gain,
    k_gain,
    w_out,
    norm2_gain,
    w_router,
    w_gate,
    w_up,
    w_down,
):
    core = lax.axis_index("tensor")
    context = lax.axis_index("context")
    mine = lax.axis_index("fsdp")
    place_x = context // SIDE
    place_z = context % SIDE
    sign = 1 - 2 * core
    span, width = tokens.shape[1:]
    half = width // 2
    size = 4 * q_gain.shape[0]
    expert_count = w_router.shape[1]
    local_experts, shard, hidden_units = w_gate.shape
    spans = SIDE * SIDE
    count = span * spans
    info = jnp.stack(
        [core, context * local_experts, mine, context]
        + [(mine + sign * i) % SIDE for i in range(SIDE)]
        + [place_x, place_z, sign, context // (spans // 2)]
    ).astype(jnp.int32)
    token_rows = tokens[0]
    cot_rows = cotangent[0]
    ids = expert_ids[0]
    pad_column = padding[0][:, None]

    first, second, inverse1 = call(
        token_message_kernel,
        [scalars] + [whole] * 3,
        [((HALF, half + EXTRA), bf16), ((HALF, half + EXTRA), bf16), ((span, 1), f32)],
    )(info, token_rows, ids, pad_column)

    positions = jnp.arange(count, dtype=jnp.int32)
    ends = jnp.cumsum(doc_lengths[0])
    passed = positions[:, None] >= ends[None, :]
    doc_index = jnp.sum(passed.astype(jnp.int32), axis=-1)
    starts = jnp.sum(jnp.where(passed, doc_lengths, 0), axis=-1)
    doc_rows = doc_index[:, None]
    doc_columns = doc_index[None, :]
    offsets = (positions - starts).astype(f32)
    frequency = theta_base ** (-jnp.arange(size // 2, dtype=f32) * 2.0 / size)
    angles = offsets[:, None] * frequency[None, :]
    cosine = jnp.cos(angles)
    sine = jnp.sin(angles)
    cosine = join([cosine, cosine], 1)
    sine = join([-sine, sine], 1)
    dense = call(
        dense_message_kernel,
        None,
        [((4 * size + expert_count + SMALL, shard), bf16)],
        grid_spec=pltpu.PrefetchScalarGridSpec(
            num_scalar_prefetch=1,
            grid=(1,),
            in_specs=[
                pl.BlockSpec((shard, size), lambda i, info: (0, info[3])),
                pl.BlockSpec((shard, size), lambda i, info: (0, info[11])),
                pl.BlockSpec((shard, size), lambda i, info: (0, info[11])),
                pl.BlockSpec((size, shard), lambda i, info: (info[3], 0)),
            ]
            + [whole] * 5,
            out_specs=[whole],
        ),
    )(
        after(info, first), w_query, key_weight, value_weight, w_out, w_router.T,
        norm1_gain[None], norm2_gain[None], q_gain[None], k_gain[None],
    )[0]
    dense_pieces = ring_gather(dense, moves_y())
    cot_half = lax.dynamic_slice_in_dim(cot_rows, core * half, half, axis=1)
    cot_all = lax.all_gather(cot_half, "context", axis=0)
    pairs_all = lax.all_gather(after(join([w_gate, w_up], 2), first), "fsdp", axis=0)
    first_near, second_near = two_gathers(
        first, second, moves_z(), moves_x(), (dense_pieces[3],), (dense_pieces[1],)
    )
    first_pieces, second_pieces = two_gathers(
        stack(first_near),
        stack(second_near),
        moves_x(),
        moves_z(),
        (dense_pieces[2], cosine, sine, doc_rows),
    )
    token_pieces = first_pieces + second_pieces
    extra_rows = expert_count + SMALL
    dense_own, dense_away, out_own_rows, out_away_rows, dense_out, extra = call(
        dense_split_kernel,
        [scalars] + [whole] * 4,
        [
            ((3 * size, half), bf16),
            ((3 * size, half), bf16),
            ((size, half), bf16),
            ((size, half), bf16),
            ((size, width), bf16),
            ((extra_rows, width), bf16),
        ],
    )(info, *dense_pieces)
    dense_came = other_core(dense_away)
    out_came_rows = other_core(out_away_rows)
    gain1 = lax.dynamic_slice(extra, (expert_count, core * half), (1, half)).astype(f32)
    gain_rows = extra[expert_count + 2 : expert_count + 4].reshape(2, SIDE, shard)[:, :, : size // SIDE]
    head_gains = jnp.pad(gain_rows.reshape(2, size).astype(f32), ((0, 6), (0, 0)))

    mark_spec = pl.BlockSpec((SIDE, HALF, EXTRA), lambda i: (0, 0, half // EXTRA))
    chosen, pads = call(
        slots_kernel,
        [scalars] + [mark_spec] * 8,
        [((spans, span, EXTRA), bf16), ((8, EXTRA), f32)],
        grid=(1,),
        out_specs=[whole, whole],
    )(info, *token_pieces)

    head_shape = (spans, span, size)
    own_part, away_part, normed1 = call(
        project_kernel,
        [scalars] + [whole] * 11,
        [((spans, span, 3 * size), f32), ((spans, span, 3 * size), f32), ((spans, span, half), bf16)],
        flops=4 * count * half * 3 * size,
        moved=2 * 10**7,
    )(info, gain1, after(dense_own, cot_all), dense_came, *token_pieces)
    down_all = lax.all_gather(after(w_down, token_pieces[0]), "fsdp", axis=0)
    mixed, raw, queries, keys, values, log_totals = call(
        attend_kernel,
        [whole] * 8,
        [
            (head_shape, bf16),
            ((count, 2 * size), f32),
            ((count, size), bf16),
            ((count, size), bf16),
            ((count, size), bf16),
            ((count, 1), f32),
        ],
        flops=4 * 10**9,
        moved=3 * 10**7,
    )(own_part, other_core(away_part), cosine, sine, head_gains, doc_rows, doc_columns, pads)
    mixed_came = other_core(mixed)
    piece_shape = (SIDE, HALF, half)
    branch_pieces = call(
        out_kernel, [scalars] + [whole] * 4, [(piece_shape, bf16)] * 8, flops=4 * count * size * half, moved=10**7
    )(info, mixed, mixed_came, out_own_rows, out_came_rows)
    branch = plane_scatter(branch_pieces)

    residual2, inverse2, normed2, probs, gates, picked_total, first, second = call(
        router_kernel,
        [scalars] + [whole] * 5,
        [
            ((span, width), f32),
            ((span, 1), f32),
            ((span, width), bf16),
            ((span, expert_count), f32),
            ((span, expert_count), f32),
            ((span, 1), f32),
            ((HALF, half + EXTRA), bf16),
            ((HALF, half + EXTRA), bf16),
        ],
    )(info, token_rows, branch, other_core(branch), ids, extra)
    cot_other = other_core(after(cot_all, first))
    slot_count = spans * SLOTS
    slot_grads = call(
        pick_spans_kernel,
        [scalars] + [whole] * 3,
        [((local_experts, slot_count, width), bf16)],
        flops=4 * 10**9,
        moved=2 * 10**7,
    )(info, chosen, cot_all, cot_other)[0]
    row_pieces = plane_gather(
        first, second, ((), (), (pairs_all,), (slot_grads,))
    )
    away_pieces = [other_core(piece) for piece in row_pieces]

    slot_rows, slot_marks = call(
        pick_rows_kernel,
        [scalars] + [whole] * 17,
        [((local_experts, slot_count, width), bf16), ((local_experts, slot_count, EXTRA), bf16)],
        flops=4 * 10**9,
        moved=2 * 10**7,
    )(info, chosen, *row_pieces, *away_pieces)
    expert_flops = 2 * local_experts * slot_count * width * hidden_units
    slot_half = (local_experts, slot_count, half)
    slot_hidden = (local_experts, slot_count, hidden_units)
    back_own, back_other, back_marks, hidden, pairs = per_expert(
        expert_kernel,
        info,
        [slot_rows, slot_marks, slot_grads, pairs_all, down_all],
        [slot_half, slot_half, (local_experts, slot_count, EXTRA), slot_hidden, slot_hidden[:2] + (2 * hidden_units,)],
        5 * expert_flops,
        5 * 10**7,
    )
    back_came = other_core(back_other)
    expert_grads = per_expert(
        expert_grad_kernel,
        info,
        [slot_rows, pairs],
        [(local_experts, shard, hidden_units)] * 8,
        2 * expert_flops,
        3 * 10**7,
    )
    gate_grads, up_grads = expert_grads[:4], expert_grads[4:]
    out_all = lax.all_gather(after(dense_out, slot_rows), "context", axis=0)
    grad_pieces = call(
        put_rows_kernel,
        [scalars] + [whole] * 4,
        [((SIDE, HALF, half + EXTRA), bf16)] * 8,
        flops=2 * 10**9,
        moved=2 * 10**7,
    )(info, chosen, back_own, after(back_came, gate_grads[0]), back_marks)
    out_own, out_other, *down_grads = per_expert(
        expert_out_kernel,
        info,
        [slot_grads, after(hidden, grad_pieces[0]), down_all],
        [slot_half, slot_half] + [(local_experts, hidden_units, shard)] * 4,
        2 * expert_flops,
        3 * 10**7,
    )
    mixture_pieces = call(
        put_sums_kernel,
        [scalars] + [whole] * 3,
        [(piece_shape, bf16)] * 8,
        flops=2 * 10**9,
        moved=2 * 10**7,
    )(info, chosen, out_own, other_core(out_other))
    gate_steps, up_steps, down_steps = scatter_chain([gate_grads, up_grads, down_grads], moves_y())
    grad_message = plane_scatter(grad_pieces, ((out_own, *gate_steps[:2]), (), (), (gate_steps[2], up_steps[0], mixture_pieces[0])))

    grad_low, grad_half, grad_residual2, router_rows = call(
        router_back_kernel,
        [scalars] + [whole] * 12,
        [
            ((span, width), bf16),
            ((span, half), bf16),
            ((span, width), f32),
            ((extra_rows, width), bf16),
        ],
    )(
        info, grad_message, other_core(grad_message), residual2, inverse2, normed2, probs, gates, picked_total,
        ids, pad_column, cot_rows, extra,
    )

    four_heads = pl.BlockSpec((SIDE, span, size), lambda i: (i, 0, 0))
    four_weights = pl.BlockSpec((SIDE, size, width), lambda i: (i, 0, 0))
    out_grads_all = lax.all_gather(grad_half, "context", axis=0)
    heads_back = call(
        heads_back_kernel,
        [whole, four_weights],
        [(head_shape, bf16)],
        flops=2 * span * width * width,
        moved=10**7,
        grid=(SIDE,),
        out_specs=[four_heads],
    )(grad_low, out_all)[0]
    heads_grad = lax.all_to_all(heads_back, "context", split_axis=0, concat_axis=0, tiled=True)
    grads, gain_grads = call(
        attend_back_kernel,
        [whole] * 12,
        [((spans, span, 3 * size), bf16), ((8, size), f32)],
        flops=8 * 10**9,
        moved=3 * 10**7,
        scratch_shapes=[pltpu.VMEM((count, size), f32)] * 3,
    )(
        heads_grad.reshape(count, size), raw, queries, keys, values, log_totals,
        cosine, sine, head_gains, doc_rows, doc_columns, pads,
    )
    grads_came = other_core(grads)
    project_own, project_away = call(
        project_grad_kernel,
        [whole] * 3,
        [((3 * size, half), bf16)] * 2,
        flops=4 * count * half * 3 * size,
        moved=2 * 10**7,
    )(grads, grads_came, normed1)
    out_grad_own, out_grad_away = call(
        out_grad_kernel, [whole] * 3, [((size, half), bf16)] * 2, flops=4 * count * size * half, moved=10**7
    )(after(mixed, project_own), mixed_came, out_grads_all)
    project_came = other_core(project_away)
    *input_pieces, gain1_part = call(
        input_back_kernel,
        [scalars] + [whole] * 20,
        [((SIDE, HALF, width), bf16)] * 8 + [((8, half), f32)],
        flops=4 * count * half * 3 * size,
        moved=3 * 10**7,
    )(info, grads, after(grads_came, project_own, up_steps[1], up_steps[2]), dense_own, dense_came, *token_pieces, *mixture_pieces)

    query_shape = (2 * size + SMALL + extra_rows, shard)
    key_value_shape = (2 * size, shard)
    project_pieces = call(
        project_chunk_kernel, [scalars] + [whole] * 9, [(query_shape, bf16)] * 4 + [(key_value_shape, bf16)] * 4
    )(
        info, project_own, project_came, gain1_part, other_core(gain1_part), gain_grads, other_core(gain_grads),
        out_grad_own, other_core(out_grad_away), router_rows,
    )
    query_terms = ring_scatter(project_pieces[:4], moves_y())
    key_passing = moves_y()[0](project_pieces[6])
    key_ahead = moves_y()[1](project_pieces[7])
    first, second, (key_passing, key_ahead, *query_terms), (key_ahead,) = two_scatters(
        input_pieces[:4],
        input_pieces[4:],
        moves_x(),
        moves_z(),
        (key_passing, key_ahead, *query_terms, *down_steps[:2]),
        (key_ahead,),
    )
    query_mine = low_sum(query_terms[:3])
    query_all = lax.all_gather(query_mine, "context", axis=0)
    key_behind = moves_y()[0](add_low(project_pieces[5], key_passing))
    first, second, (key_behind,), key_terms = two_scatters(
        unstack(first), unstack(second), moves_z(), moves_x(), (key_behind,), (down_steps[2],)
    )
    key_value = low_sum((project_pieces[4], key_behind, key_ahead))
    key_value = low_sum([key_value] + [along_z(key_value, step) for step in range(1, SIDE)])
    final_rows = call(total_kernel, [whole] * 6, [((span, width), f32)])(*first, *second)[0]
    key_value = low_sum([key_value, across(key_value, 1)])
    final_key, final_value = call(
        key_value_kernel, [scalars] + [whole] * 2, [((shard, 2 * size), f32)] * 2
    )(info, key_value, across(key_value, 2))
    grad_input, result = call(final_rows_kernel, [scalars] + [whole] * 7, [((span, width), f32)] * 2)(
        info, final_rows, other_core(final_rows), token_rows, inverse1, extra, grad_residual2, residual2
    )
    (
        final_query, final_out, final_router, final_gain1, final_gain2, final_head_gains, expert_load, balance_loss
    ) = call(
        project_final_kernel,
        [scalars, pl.BlockSpec((SIDE,) + query_shape, lambda i: (i, 0, 0))],
        [
            ((shard, spans * size), f32),
            ((spans * size, shard), f32),
            ((expert_count, shard), f32),
            ((1, shard), f32),
            ((1, shard), f32),
            ((2, size // SIDE), f32),
            ((1, expert_count), f32),
            ((1, 1), f32),
        ],
        grid=(SIDE,),
        out_specs=[
            pl.BlockSpec((shard, SIDE * size), lambda i: (0, i)),
            pl.BlockSpec((SIDE * size, shard), lambda i: (i, 0)),
        ]
        + [whole] * 6,
        scratch_shapes=[pltpu.VMEM((SMALL + extra_rows, shard), f32)],
    )(info, after(query_all, grad_input))

    def finished(parts, steps):
        return parts[0].astype(f32) + steps[1].astype(f32) + steps[2].astype(f32)

    final_gate = finished(gate_grads, gate_steps)
    final_up = finished(up_grads, up_steps)
    final_down = finished(down_grads, down_steps)

    return (
        result[None],
        balance_loss.reshape(()),
        expert_load.reshape(expert_count),
        grad_input[None],
        final_gain1.reshape(shard),
        final_query,
        final_key,
        final_value,
        final_head_gains[0],
        final_head_gains[1],
        final_out,
        final_gain2.reshape(shard),
        final_router.T,
        final_gate,
        final_up,
        final_down,
    )


def solution(mesh):
    in_specs = (
        P("fsdp", "context", None),
        P("fsdp", "context", None),
        P("fsdp", None),
        P("fsdp", "context"),
        P("fsdp", "context", None),
        P("fsdp"),
        P("fsdp", "tensor"),
        P("fsdp", "tensor"),
        P("fsdp", "tensor"),
        P("fsdp"),
        P("fsdp"),
        P("tensor", "fsdp"),
        P("fsdp"),
        P("fsdp", None),
        P("context", "fsdp", "tensor"),
        P("context", "fsdp", "tensor"),
        P("context", "tensor", "fsdp"),
    )
    out_specs = (
        P("fsdp", "context", None),
        P(),
        P(),
        P("fsdp", "context", None),
        P("fsdp"),
        P("fsdp", "tensor"),
        P("fsdp", "tensor"),
        P("fsdp", "tensor"),
        P("fsdp"),
        P("fsdp"),
        P("tensor", "fsdp"),
        P("fsdp"),
        P("fsdp", None),
        P("context", "fsdp", "tensor"),
        P("context", "fsdp", "tensor"),
        P("context", "tensor", "fsdp"),
    )
    return jax.shard_map(body, mesh=mesh, in_specs=in_specs, out_specs=out_specs, check_vma=False)
```

```python
import jax
import jax.numpy as jnp
from jax import lax
from jax.experimental import pallas as pl
from jax.experimental.pallas import tpu as pltpu
from jax.sharding import PartitionSpec as P

WINDOW = 1024
SIDE = 4
HALF = 64
QUERY_BLOCK = 256
SLOTS = 32
EXTRA = 128
SMALL = 16

epsilon = 1e-06
theta_base = 1000000.0
negative = -1e30
f32 = jnp.float32
bf16 = jnp.bfloat16
vmem_limit = 56 * 1024 * 1024
whole = pl.BlockSpec(memory_space=pltpu.VMEM)
scalars = pl.BlockSpec(memory_space=pltpu.SMEM)


def call(kernel, in_specs, out_shape, flops=10**6, moved=10**6, **rest):
    if in_specs is not None:
        rest["in_specs"] = in_specs
    return pl.pallas_call(
        kernel,
        out_shape=[jax.ShapeDtypeStruct(shape, kind) for shape, kind in out_shape],
        compiler_params=pltpu.CompilerParams(vmem_limit_bytes=vmem_limit),
        cost_estimate=pl.CostEstimate(flops=flops, bytes_accessed=moved, transcendentals=0),
        **rest,
    )


def dot_nt(left, right):
    return lax.dot_general(left, right, (((1,), (1,)), ((), ())), preferred_element_type=f32)


def dot_tn(left, right):
    return lax.dot_general(left, right, (((0,), (0,)), ((), ())), preferred_element_type=f32)


def dot_nn(left, right):
    return jnp.dot(left, right, preferred_element_type=f32)


def join(parts, axis=0):
    return jnp.concatenate(parts, axis=axis)


def ring_moves(axis, target):
    forward = []
    backward = []
    count = lax.axis_size(axis)
    for i in range(count):
        for core, sign in ((0, 1), (1, -1)):
            forward.append((2 * i + core, 2 * target(i, sign) + core))
            backward.append((2 * i + core, 2 * target(i, -sign) + core))

    def move(pairs):
        return lambda value: lax.ppermute(value, (axis, "tensor"), pairs)

    return move(forward), move(backward)


def moves_z():
    return ring_moves("context", lambda i, step: (i // SIDE) * SIDE + (i + step) % SIDE)


def moves_x():
    return ring_moves("context", lambda i, step: (i + SIDE * step) % (SIDE * SIDE))


def moves_y():
    return ring_moves("fsdp", lambda i, step: (i + step) % SIDE)


def other_core(value):
    return lax.ppermute(value, "tensor", [(0, 1), (1, 0)])


def after(value, *events):
    return lax.optimization_barrier((value, *events))[0]


def ring_gather(value, moves):
    behind = moves[0](value)
    ahead = moves[1](value)
    far = moves[0](behind)
    return [value, ahead, far, behind]


def add_low(left, right):
    return (left.astype(f32) + right.astype(f32)).astype(bf16)


def low_sum(terms):
    return sum(term.astype(f32) for term in terms).astype(bf16)


def across(value, step):
    pairs = [(i, i ^ (SIDE * step)) for i in range(SIDE * SIDE)]
    return lax.ppermute(value, "context", pairs)


def along_x(value, step):
    pairs = [(i, (i + SIDE * step) % (SIDE * SIDE)) for i in range(SIDE * SIDE)]
    return lax.ppermute(value, "context", pairs)


def along_z(value, step):
    pairs = [(i, (i // SIDE) * SIDE + (i + step) % SIDE) for i in range(SIDE * SIDE)]
    return lax.ppermute(value, "context", pairs)


def ring_scatter(parts, moves):
    passing = moves[0](parts[2])
    from_ahead = moves[1](parts[3])
    from_behind = moves[0](add_low(parts[1], passing))
    return parts[0], from_behind, from_ahead


def together(*values):
    return lax.optimization_barrier(values)


def stack_kernel(a, b, c, d, result):
    for i, part in enumerate((a, b, c, d)):
        result[i] = part[...]


def stack(parts):
    shape = parts[0].shape
    return call(stack_kernel, [whole] * 4, [((4,) + shape, bf16)])(*parts)[0]


def two_gathers(left, right, left_moves, right_moves, events=(), last=()):
    left_behind = left_moves[0](left)
    left_ahead = left_moves[1](left)
    right_behind = right_moves[0](right)
    right_ahead = right_moves[1](right)
    left_behind, left_ahead, right_behind, right_ahead = together(
        left_behind, left_ahead, right_behind, right_ahead, *events
    )[:4]
    left_far = left_moves[0](left_behind)
    right_far = right_moves[0](right_behind)
    left_far, right_far = together(left_far, right_far, *last)[:2]
    return [left, left_ahead, left_far, left_behind], [right, right_ahead, right_far, right_behind]


def two_short_gathers(left, right, events=()):
    left_moves, right_moves = moves_z(), moves_x()
    values = (
        left_moves[1](left),
        along_z(left, 2),
        left_moves[0](left),
        right_moves[1](right),
        along_x(right, 2),
        right_moves[0](right),
    )
    values = together(*values, *events)[:6]
    return [left, *values[:3]], [right, *values[3:]]


def two_short_scatters(left, right, events=()):
    left_moves, right_moves = moves_z(), moves_x()
    values = (
        left_moves[1](left[3]),
        along_z(left[2], 2),
        left_moves[0](left[1]),
        right_moves[1](right[3]),
        along_x(right[2], 2),
        right_moves[0](right[1]),
    )
    values = together(*values, *events)[:6]
    return (left[0], *values[:3]), (right[0], *values[3:])


def plane_gather(first, second, events=((), (), (), ())):
    first_near, second_near = two_short_gathers(first, second, events[0])
    first_pieces, second_pieces = two_gathers(
        stack(first_near), stack(second_near), moves_x(), moves_z(), *events[2:]
    )
    return first_pieces + second_pieces


def unstack_kernel(a, b, c, r0, r1, r2, r3):
    for i, part in enumerate((r0, r1, r2, r3)):
        part[...] = (a[i].astype(f32) + b[i].astype(f32) + c[i].astype(f32)).astype(bf16)


def unstack(terms):
    shape = terms[0].shape[1:]
    return call(unstack_kernel, [whole] * 3, [(shape, bf16)] * 4)(*terms)


def total_kernel(*refs):
    result = refs[8]
    for i in range(2):
        a, b, c, d = (part[...].astype(f32) for part in refs[4 * i : 4 * i + 4])
        result[i * HALF : (i + 1) * HALF] = (a + b) + (c + d)


def two_scatters(left, right, left_moves, right_moves, events=(), last=()):
    left_passing = left_moves[0](left[2])
    left_from_ahead = left_moves[1](left[3])
    right_passing = right_moves[0](right[2])
    right_from_ahead = right_moves[1](right[3])
    left_passing, left_from_ahead, right_passing, right_from_ahead, *events = together(
        left_passing, left_from_ahead, right_passing, right_from_ahead, *events
    )
    left_from_behind = left_moves[0](add_low(left[1], left_passing))
    right_from_behind = right_moves[0](add_low(right[1], right_passing))
    left_from_behind, right_from_behind, *last = together(left_from_behind, right_from_behind, *last)
    left_terms = (left[0], left_from_behind, left_from_ahead)
    right_terms = (right[0], right_from_behind, right_from_ahead)
    return left_terms, right_terms, events, last


def plane_scatter(pieces, events=((), (), ())):
    first, second, *_ = two_scatters(pieces[:4], pieces[4:], moves_x(), moves_z(), *events[:2])
    first, second = two_short_scatters(unstack(first), unstack(second), events[2])
    return total(first, second)


def total(first, second):
    width = first[0].shape[-1]
    return call(total_kernel, [whole] * 8, [((2 * HALF, width), f32)])(*first, *second)[0]


def split_low(value, count):
    parts = []
    rest = value
    for _ in range(count):
        part = rest.astype(bf16)
        parts.append(part)
        rest = rest - part.astype(f32)
    return parts


def core_columns(core, width):
    return pl.ds(pl.multiple_of(core * width, width), width)


def token_message_kernel(info, tokens, ids, padding, first, second, inverse_out):
    width = tokens.shape[1]
    half = width // 2
    rows = tokens[...].astype(f32)
    inverse = lax.rsqrt(jnp.mean(rows * rows, axis=-1, keepdims=True) + epsilon)
    inverse_out[...] = inverse
    lanes = lax.broadcasted_iota(jnp.int32, (rows.shape[0], EXTRA), 1)
    marks = jnp.zeros((rows.shape[0], EXTRA), f32)
    for k in range(8):
        marks = jnp.where(lanes == k, ids[:, k : k + 1].astype(f32), marks)
    marks = jnp.where(lanes == 8, padding[...].astype(f32), marks)
    for k, part in enumerate(split_low(inverse, 3)):
        marks = jnp.where(lanes == 9 + k, part.astype(f32), marks)
    marks = marks.astype(bf16)
    own = tokens[:, core_columns(info[0], half)]
    first[:, :half] = own[:HALF]
    first[:, half:] = marks[:HALF]
    second[:, :half] = own[HALF:]
    second[:, half:] = marks[HALF:]


def dense_message_kernel(info, query, key, value, out, router, gain1, gain2, q_gain, k_gain, result):
    size = query.shape[1]
    experts = router.shape[0]
    result[:size] = query[...].T
    result[size : 2 * size] = key[...].T
    result[2 * size : 3 * size] = value[...].T
    result[3 * size : 4 * size] = out[...]
    result[4 * size : 4 * size + experts] = router[...]
    base = 4 * size + experts
    rows = lax.broadcasted_iota(jnp.int32, (SMALL, result.shape[1]), 0)
    gains = jnp.where(rows == 0, gain1[...].astype(f32), 0.0)
    gains = jnp.where(rows == 1, gain2[...].astype(f32), gains)
    rest = jnp.zeros((1, result.shape[1] - q_gain.shape[1]), f32)
    gains = jnp.where(rows == 2, join([q_gain[...].astype(f32), rest], 1), gains)
    gains = jnp.where(rows == 3, join([k_gain[...].astype(f32), rest], 1), gains)
    result[base:] = gains.astype(bf16)


def dense_split_kernel(info, a, b, c, d, own, away, own_out, away_out, extra):
    shard = a.shape[1]
    rows = own.shape[0]
    size = own_out.shape[0]
    core = info[0]
    for i, piece in enumerate((a, b, c, d)):
        place = info[4 + i]
        columns = core_columns(place % 2, shard)

        @pl.when(place // 2 == core)
        def _():
            own[:, columns] = piece[:rows]
            own_out[:, columns] = piece[rows : rows + size]

        @pl.when(place // 2 != core)
        def _():
            away[:, columns] = piece[:rows]
            away_out[:, columns] = piece[rows : rows + size]

        extra[:, core_columns(place, shard)] = piece[rows + size :]


def slots_kernel(info, *refs):
    pieces, (chosen, pads) = refs[:8], refs[8:]
    first_expert = info[1]
    place_x, place_z, sign = info[8], info[9], info[10]
    shape = (2 * HALF, EXTRA)
    lanes = lax.broadcasted_iota(jnp.int32, shape, 1)
    rows = lax.broadcasted_iota(jnp.int32, shape, 0)
    earlier = (lanes < rows).astype(bf16)
    pad_total = jnp.zeros((1, EXTRA), f32)
    for ix in range(SIDE):
        for iz in range(SIDE):
            marks = join([pieces[ix][iz], pieces[4 + iz][ix]]).astype(f32)
            pad_total += jnp.sum(marks, axis=0, keepdims=True)
            named = jnp.zeros(shape, f32)
            for e in range(EXTRA // SLOTS):
                hit = jnp.where((lanes < 8) & (marks == (first_expert + e).astype(f32)), 1.0, 0.0)
                hit = jnp.max(hit, axis=-1, keepdims=True)
                named = jnp.where(lanes // SLOTS == e, hit, named)
            ranks = dot_nn(earlier, named.astype(bf16))
            match = (named > 0.0) & (ranks == (lanes % SLOTS).astype(f32))
            place = ((place_x + sign * ix) % SIDE) * SIDE + (place_z + sign * iz) % SIDE
            chosen[place] = jnp.where(match, 1.0, 0.0).astype(bf16)
    pads[...] = jnp.broadcast_to(pad_total, pads.shape)


def write_slots(result, place, columns, slots):
    for e in range(EXTRA // SLOTS):
        target = pl.ds(pl.multiple_of(place * SLOTS, SLOTS), SLOTS)
        result[e, target, columns] = slots[e * SLOTS : (e + 1) * SLOTS]


def read_slots(source, place, columns):
    target = pl.ds(pl.multiple_of(place * SLOTS, SLOTS), SLOTS)
    return join([source[e, target, columns] for e in range(EXTRA // SLOTS)])


def pick_rows_kernel(info, chosen, *refs):
    own, other, (result, extra) = refs[:8], refs[8:16], refs[16:]
    core, place_x, place_z, sign = info[0], info[8], info[9], info[10]
    half = result.shape[-1] // 2
    own_columns = core_columns(core, half)
    other_columns = core_columns(1 - core, half)
    for ix in range(SIDE):
        for iz in range(SIDE):
            place = ((place_x + sign * ix) % SIDE) * SIDE + (place_z + sign * iz) % SIDE
            matrix = chosen[place]
            rows = join([own[ix][iz], own[4 + iz][ix]])
            slots = dot_tn(matrix, rows).astype(bf16)
            write_slots(result, place, own_columns, slots[:, :half])
            write_slots(extra, place, slice(None), slots[:, half:])
            jx, jz = -ix % SIDE, -iz % SIDE
            rows = join([other[jx][jz, :, :half], other[4 + jz][jx, :, :half]])
            write_slots(result, place, other_columns, dot_tn(matrix, rows).astype(bf16))


def pick_spans_kernel(info, chosen, own, other, result):
    core = info[0]
    half = own.shape[-1]
    for place in range(SIDE * SIDE):
        matrix = chosen[place]
        write_slots(result, place, core_columns(core, half), dot_tn(matrix, own[place]).astype(bf16))
        write_slots(result, place, core_columns(1 - core, half), dot_tn(matrix, other[place]).astype(bf16))


def put_rows_kernel(info, chosen, own, came, extra, *pieces):
    place_x, place_z, sign = info[8], info[9], info[10]
    half = own.shape[-1]
    for ix in range(SIDE):
        for iz in range(SIDE):
            place = ((place_x + sign * ix) % SIDE) * SIDE + (place_z + sign * iz) % SIDE
            matrix = chosen[place]
            rows = read_slots(own, place, slice(None)).astype(f32) + read_slots(came, place, slice(None)).astype(f32)
            rows = dot_nn(matrix, rows.astype(bf16)).astype(bf16)
            marks = dot_nn(matrix, read_slots(extra, place, slice(None))).astype(bf16)
            pieces[ix][iz, :, :half] = rows[:HALF]
            pieces[4 + iz][ix, :, :half] = rows[HALF:]
            pieces[ix][iz, :, half:] = marks[:HALF]
            pieces[4 + iz][ix, :, half:] = marks[HALF:]


def put_spans_kernel(chosen, own, came, result):
    for place in range(SIDE * SIDE):
        rows = read_slots(own, place, slice(None)).astype(f32) + read_slots(came, place, slice(None)).astype(f32)
        result[place] = dot_nn(chosen[place], rows.astype(bf16)).astype(bf16)


def span_of(info, ix, iz):
    return ((info[8] + info[10] * ix) % SIDE) * SIDE + (info[9] + info[10] * iz) % SIDE


def piece_parts(info, i):
    for j in range(SIDE):
        if i < SIDE:
            yield j, span_of(info, i, j), slice(0, HALF)
        else:
            yield j, span_of(info, j, i - SIDE), slice(HALF, 2 * HALF)


def project_kernel(info, gain, own, came, *refs):
    pieces, (own_out, other_out, normed_out) = refs[:8], refs[8:]
    half = gain.shape[1]
    wide = own_out.shape[-1]
    count = SIDE * HALF
    lanes = lax.broadcasted_iota(jnp.int32, (count, EXTRA), 1)
    for i, piece in enumerate(pieces):
        rows = piece[...].reshape(count, half + EXTRA)
        marks = jnp.where((lanes >= 9) & (lanes < 12), rows[:, half:].astype(f32), 0.0)
        inverse = jnp.sum(marks, axis=-1, keepdims=True)
        normed = (rows[:, :half].astype(f32) * inverse * gain[...]).astype(bf16)
        own_rows = dot_nt(normed, own[...])
        other_rows = dot_nt(normed, came[...])
        for j, span, part in piece_parts(info, i):
            cut = slice(j * HALF, (j + 1) * HALF)
            normed_out[span, part] = normed[cut]
            own_out[span, part] = own_rows[cut]
            other_out[span, part] = other_rows[cut].astype(bf16)


def turn(value, cosine, sine):
    return value * cosine + pltpu.roll(value, 64, 1) * sine


def block_mask(doc_rows, doc_columns, real, query_start, key_start, query_count, key_count):
    rows = lax.broadcasted_iota(jnp.int32, (query_count, key_count), 0)
    columns = lax.broadcasted_iota(jnp.int32, (query_count, key_count), 1)
    distance = rows - columns + (query_start - key_start)
    positions = lax.broadcasted_iota(jnp.int32, (1, key_count), 1) + key_start
    doc_columns = jnp.where(positions < real, doc_columns, -1)
    inside = (distance >= 0) & (distance < WINDOW) & (doc_rows == doc_columns)
    return inside | (distance == 0)


def real_count(pads, count):
    return (count - pads[0:1, 8:9]).astype(jnp.int32)


def attend_kernel(
    own, came, cosine, sine, gains, doc_rows, doc_columns, pads,
    mixed, raw, queries, keys, values, log_totals,
):
    count = queries.shape[0]
    size = queries.shape[1]
    span = mixed.shape[1]
    scale = size ** (-0.5)

    def prepare(j, carry):
        rows = pl.ds(pl.multiple_of(j * span, span), span)
        block = own[j] + came[j].astype(f32)
        raw[rows, :] = block[:, : 2 * size]
        cos_rows = cosine[rows, :]
        sin_rows = sine[rows, :]
        for part, target in ((0, queries), (1, keys)):
            piece = block[:, part * size : (part + 1) * size]
            inverse = lax.rsqrt(jnp.mean(piece * piece, axis=-1, keepdims=True) + epsilon)
            normed = piece * inverse * gains[part : part + 1, :]
            target[rows, :] = turn(normed, cos_rows, sin_rows).astype(bf16)
        values[rows, :] = block[:, 2 * size :].astype(bf16)
        return carry

    lax.fori_loop(0, count // span, prepare, 0)
    real = real_count(pads, float(count))
    for start in range(0, count, QUERY_BLOCK):
        low = max(0, start - WINDOW)
        high = start + QUERY_BLOCK
        scores = dot_nt(queries[start:high, :], keys[low:high, :]) * scale
        allowed = block_mask(
            doc_rows[start:high, :], doc_columns[:, low:high], real, start, low, QUERY_BLOCK, high - low
        )
        scores = jnp.where(allowed, scores, negative)
        peak = jnp.max(scores, axis=-1, keepdims=True)
        exponent = jnp.exp(scores - peak)
        total = jnp.sum(exponent, axis=-1, keepdims=True)
        weights = (exponent * (1.0 / total)).astype(bf16)
        rows = dot_nn(weights, values[low:high, :]).astype(bf16)
        mixed[start // span : high // span] = rows.reshape(QUERY_BLOCK // span, span, size)
        log_totals[start:high, :] = peak + jnp.log(total)


def attend_back_kernel(
    own, came, raw, queries, keys, values, log_totals, cosine, sine, gains, doc_rows, doc_columns, pads,
    grads, gain_grads, grad_mixed, grad_queries, grad_keys, grad_values,
):
    count = queries.shape[0]
    size = queries.shape[1]
    span = grads.shape[1]
    scale = size ** (-0.5)
    grad_mixed[...] = (own[...] + came[...]).astype(bf16).reshape(count, size)
    grad_keys[...] = jnp.zeros_like(grad_keys)
    grad_values[...] = jnp.zeros_like(grad_values)
    real = real_count(pads, float(count))
    for start in range(0, count, QUERY_BLOCK):
        low = max(0, start - WINDOW)
        high = start + QUERY_BLOCK
        query_rows = queries[start:high, :]
        key_rows = keys[low:high, :]
        grad_rows = grad_mixed[start:high, :]
        scores = dot_nt(query_rows, key_rows) * scale
        allowed = block_mask(
            doc_rows[start:high, :], doc_columns[:, low:high], real, start, low, QUERY_BLOCK, high - low
        )
        soft = jnp.where(allowed, jnp.exp(scores - log_totals[start:high, :]), 0.0)
        grad_soft = dot_nt(grad_rows, values[low:high, :])
        row_dot = jnp.sum(soft * grad_soft, axis=-1, keepdims=True)
        grad_scores = (soft * (grad_soft - row_dot)).astype(bf16)
        grad_queries[start:high, :] = dot_nn(grad_scores, key_rows) * scale
        grad_keys[low:high, :] += dot_tn(grad_scores, query_rows) * scale
        grad_values[low:high, :] += dot_tn(soft.astype(bf16), grad_rows)
    gain_grads[...] = jnp.zeros_like(gain_grads)

    def finish(j, carry):
        rows = pl.ds(pl.multiple_of(j * span, span), span)
        cos_rows = cosine[rows, :]
        sin_rows = sine[rows, :]
        parts = []
        for part, source in ((0, grad_queries), (1, grad_keys)):
            piece = raw[rows, part * size : (part + 1) * size]
            inverse = lax.rsqrt(jnp.mean(piece * piece, axis=-1, keepdims=True) + epsilon)
            back = turn(source[rows, :], cos_rows, -sin_rows)
            gain_grads[part : part + 1, :] += jnp.sum(back * piece * inverse, axis=0, keepdims=True)
            scaled = back * gains[part : part + 1, :]
            mean = jnp.mean(scaled * piece, axis=-1, keepdims=True)
            parts.append((inverse * scaled - piece * (inverse * inverse * inverse * mean)).astype(bf16))
        parts.append(grad_values[rows, :].astype(bf16))
        grads[j] = join(parts, 1)
        return carry

    lax.fori_loop(0, count // span, finish, 0)


def out_kernel(info, mixed, came_mixed, own, came, *pieces):
    for i, piece in enumerate(pieces):
        parts = list(piece_parts(info, i))
        left = join([mixed[span, part] for _, span, part in parts])
        right = join([came_mixed[span, part] for _, span, part in parts])
        rows = dot_nn(left, own[...]) + dot_nn(right, came[...])
        piece[...] = rows.astype(bf16).reshape(piece.shape)


def heads_back_kernel(info, own, came, *refs):
    pieces, (own_out, other_out) = refs[:8], refs[8:]
    for i, piece in enumerate(pieces):
        rows = piece[...].reshape(SIDE * HALF, piece.shape[-1])
        own_rows = dot_nt(rows, own[...])
        other_rows = dot_nt(rows, came[...])
        for j, span, part in piece_parts(info, i):
            cut = slice(j * HALF, (j + 1) * HALF)
            own_out[span, part] = own_rows[cut]
            other_out[span, part] = other_rows[cut]


def out_grad_kernel(info, mixed, came_mixed, *refs):
    pieces, (own_out, away_out) = refs[:8], refs[8:]
    own_total = away_total = 0.0
    for i, piece in enumerate(pieces):
        rows = piece[...].reshape(SIDE * HALF, piece.shape[-1])
        parts = list(piece_parts(info, i))
        own_total += dot_tn(join([mixed[span, part] for _, span, part in parts]), rows)
        away_total += dot_tn(join([came_mixed[span, part] for _, span, part in parts]), rows)
    own_out[...] = own_total.astype(bf16)
    away_out[...] = away_total.astype(bf16)


def input_back_kernel(info, grads, came_grads, own, came, *pieces):
    for i, piece in enumerate(pieces):
        parts = list(piece_parts(info, i))
        left = join([grads[span, part] for _, span, part in parts])
        right = join([came_grads[span, part] for _, span, part in parts])
        rows = dot_nn(left, own[...]) + dot_nn(right, came[...])
        piece[...] = rows.astype(bf16).reshape(piece.shape)


def project_grad_kernel(grads, came_grads, normed, own, came, gain, own_out, away_out, gain_grad):
    count = normed.shape[0] * normed.shape[1]
    wide = grads.shape[-1]
    rows = normed[...].reshape(count, normed.shape[-1])
    total = 0.0
    for source, weight, target in ((grads, own, own_out), (came_grads, came, away_out)):
        result = dot_tn(source[...].reshape(count, wide), rows)
        target[...] = result.astype(bf16)
        total += jnp.sum(result * weight[...].astype(f32), axis=0, keepdims=True)
    gain_grad[...] = jnp.broadcast_to(total / gain[...], gain_grad.shape)


def halves(core, own, came):
    return join([jnp.where(core == 0, own, came), jnp.where(core == 0, came, own)], 1)


def chosen_experts(ids, count):
    lanes = lax.broadcasted_iota(jnp.int32, (ids.shape[0], count), 1)
    chosen = jnp.zeros((ids.shape[0], count), f32)
    for k in range(8):
        chosen = jnp.where(lanes == ids[:, k : k + 1], 1.0, chosen)
    return chosen


def router_kernel(
    info, tokens, own, came, ids, extra, residual_out, inverse_out, normed_out, probs_out, gates_out, total_out, first, second
):
    core = info[0]
    half = tokens.shape[1] // 2
    experts = probs_out.shape[1]
    residual = tokens[...].astype(f32) + halves(core, own[...], came[...])
    residual_out[...] = residual
    inverse = lax.rsqrt(jnp.mean(residual * residual, axis=-1, keepdims=True) + epsilon)
    inverse_out[...] = inverse
    gain = extra[experts + 1 : experts + 2, :].astype(f32)
    normed = (residual * inverse * gain).astype(bf16)
    normed_out[...] = normed
    logits = dot_nt(normed, extra[:experts, :])
    exponent = jnp.exp(logits - jnp.max(logits, axis=-1, keepdims=True))
    probs = exponent / jnp.sum(exponent, axis=-1, keepdims=True)
    probs_out[...] = probs
    chosen = chosen_experts(ids, experts)
    picked = probs * chosen
    total = jnp.sum(picked, axis=-1, keepdims=True)
    total_out[...] = total
    gates = picked / total
    gates_out[...] = gates
    marks = join(split_low(gates, 2), 1)
    mine = normed_out[:, core_columns(core, half)]
    first[:, :half] = mine[:HALF]
    first[:, half:] = marks[:HALF]
    second[:, :half] = mine[HALF:]
    second[:, half:] = marks[HALF:]


def router_back_kernel(
    info, own, came, residual_ref, inverse_ref, normed, probs_ref, gates_ref, total, ids, padding, cotangent, extra,
    first, second, grad_out, rows_out, scratch,
):
    core = info[0]
    half = cotangent.shape[1] // 2
    experts = probs_ref.shape[1]
    probs = probs_ref[...]
    gates = gates_ref[...]
    residual = residual_ref[...]
    inverse = inverse_ref[...]
    marks = own[:, half:] + came[:, half:]
    gate_grads = marks[:, :experts] + marks[:, experts:]
    chosen = chosen_experts(ids, experts)
    grad_picked = (gate_grads - jnp.sum(gate_grads * gates, axis=-1, keepdims=True)) / total[...]
    grad_probs = chosen * grad_picked
    grad_logits = (probs * (grad_probs - jnp.sum(grad_probs * probs, axis=-1, keepdims=True))).astype(bf16)
    grad_normed = halves(core, own[:, :half], came[:, :half]) + dot_nn(grad_logits, extra[:experts, :])
    scaled = grad_normed * extra[experts + 1 : experts + 2, :].astype(f32)
    mean = jnp.mean(scaled * residual, axis=-1, keepdims=True)
    grad = cotangent[...].astype(f32) + inverse * scaled - residual * (inverse * inverse * inverse * mean)
    grad_out[...] = grad
    scratch[...] = grad.astype(bf16)
    mine = scratch[:, core_columns(core, half)]
    first[...] = mine[:HALF]
    second[...] = mine[HALF:]
    gain_grad = jnp.sum(grad_normed * residual * inverse, axis=0, keepdims=True)
    rows_out[:experts] = dot_tn(grad_logits, normed[...]).astype(bf16)
    kept = 1.0 - padding[...].astype(f32)
    shard = 4 * EXTRA
    rest = jnp.zeros((1, shard - experts), f32)

    def row(values):
        return join([values, rest] * SIDE, 1)

    counted = chosen * kept
    probs_sum = jnp.sum(probs * kept, axis=0, keepdims=True)
    probs_high = probs_sum.astype(bf16).astype(f32)
    kept_sum = jnp.broadcast_to(jnp.sum(kept, axis=0, keepdims=True), (1, experts))
    rows = (
        gain_grad,
        row(jnp.sum(counted[:HALF], axis=0, keepdims=True)),
        row(jnp.sum(counted[HALF:], axis=0, keepdims=True)),
        row(probs_high),
        row(probs_sum - probs_high),
        row(kept_sum),
    )
    numbers = lax.broadcasted_iota(jnp.int32, (SMALL, 2 * half), 0)
    small = jnp.zeros((SMALL, 2 * half), f32)
    for i, values in enumerate(rows):
        small = jnp.where(numbers == i, values, small)
    rows_out[experts:] = small.astype(bf16)


def final_rows_kernel(info, own, came, tokens, inverse_ref, extra, grad_residual, grad_input):
    core = info[0]
    base = extra.shape[0] - SMALL
    rows = tokens[...].astype(f32)
    inverse = inverse_ref[...]
    scaled = halves(core, own[...], came[...]) * extra[base : base + 1, :].astype(f32)
    mean = jnp.mean(scaled * rows, axis=-1, keepdims=True)
    grad_input[...] = grad_residual[...] + inverse * scaled - rows * (inverse * inverse * inverse * mean)


def result_kernel(info, own, came, residual, result):
    result[...] = residual[...] + halves(info[0], own[...].astype(f32), came[...].astype(f32))


def expert_kernel(info, rows, marks, grads, pairs_w, downs_w, back_own, back_other, back_marks, hidden_out, pairs_out):
    core = info[0]
    expert = info[1] + pl.program_id(0)
    shard = pairs_w.shape[2]
    count = rows.shape[1]
    units = hidden_out.shape[2]
    pairs = grad_raw = 0.0
    for place in range(SIDE):
        columns = slice(place * shard, (place + 1) * shard)
        pairs += dot_nn(rows[0, :, columns], pairs_w[place, 0])
        grad_raw += dot_nt(grads[0, :, columns], downs_w[place, 0])
    gate_pre = pairs[:, :units]
    up_pre = pairs[:, units:]
    lanes = lax.broadcasted_iota(jnp.int32, (count, EXTRA), 1)
    high_lane = lanes == expert
    low_lane = lanes == expert + EXTRA // 2
    gates = jnp.sum(jnp.where(high_lane | low_lane, marks[0].astype(f32), 0.0), axis=-1, keepdims=True)
    sigmoid = jax.nn.sigmoid(gate_pre)
    activated = gate_pre * sigmoid
    hidden = (activated * up_pre).astype(bf16).astype(f32)
    gate_grads = jnp.sum(hidden * grad_raw, axis=-1, keepdims=True)
    grad_hidden = gates * grad_raw
    gate_low = (grad_hidden * up_pre * sigmoid * (1.0 + gate_pre * (1.0 - sigmoid))).astype(bf16)
    up_low = (grad_hidden * activated).astype(bf16)
    hidden_out[0] = (gates * hidden).astype(bf16)
    pairs_low = join([gate_low, up_low], 1)
    pairs_out[0] = pairs_low
    for place in range(SIDE):
        near = slice((place % 2) * shard, (place % 2 + 1) * shard)
        result = dot_nt(pairs_low, pairs_w[place, 0]).astype(bf16)

        @pl.when(place // 2 == core)
        def _():
            back_own[0, :, near] = result

        @pl.when(place // 2 != core)
        def _():
            back_other[0, :, near] = result

    high = gate_grads.astype(bf16).astype(f32)
    low = gate_grads - high
    back_marks[0] = (jnp.where(high_lane, high, 0.0) + jnp.where(low_lane, low, 0.0)).astype(bf16)


def expert_grad_kernel(info, rows, pairs, gate_grads, up_grads):
    shard, units = up_grads.shape[2:]
    for i in range(SIDE):
        result = dot_tn(rows[0, :, i * shard : (i + 1) * shard], pairs[0]).astype(bf16)
        gate_grads[i, 0] = result[:, :units]
        up_grads[i, 0] = result[:, units:]


def expert_out_kernel(info, grads, hidden, downs_w, out_own, out_other, *down_grads):
    core = info[0]
    shard = downs_w.shape[3]
    for i in range(SIDE):
        place = info[4 + i]
        down_grads[i][0] = dot_tn(hidden[0], grads[0, :, core_columns(place, shard)]).astype(bf16)
        result = dot_nn(hidden[0], downs_w[place, 0]).astype(bf16)
        near = core_columns(place % 2, shard)

        @pl.when(place // 2 == core)
        def _():
            out_own[0, :, near] = result

        @pl.when(place // 2 != core)
        def _():
            out_other[0, :, near] = result


def by_expert(shape):
    if len(shape) == 4:
        return pl.BlockSpec((shape[0], 1) + tuple(shape[2:]), lambda e: (0, e, 0, 0))
    return pl.BlockSpec((1,) + tuple(shape[1:]), lambda e: (e, 0, 0))


def per_expert(kernel, info, arrays, out_shapes, flops, moved):
    return call(
        kernel,
        [scalars] + [by_expert(array.shape) for array in arrays],
        [(shape, bf16) for shape in out_shapes],
        flops=flops,
        moved=moved,
        out_specs=[by_expert(shape) for shape in out_shapes],
        grid=(arrays[0].shape[0],),
    )(info, *arrays)


def project_chunk_kernel(info, own, came, gain, gain_came, heads, heads_came, out, out_came, extra, *pieces):
    core = info[0]
    shard = pieces[0].shape[1]
    size = out.shape[0]
    base = 2 * size + extra.shape[0]
    numbers = lax.broadcasted_iota(jnp.int32, (SMALL, shard), 0)
    both = heads[...] + heads_came[...]
    rest = jnp.zeros((1, shard - 2 * size), f32)
    head_row = join([both[0:1], both[1:2], rest], 1)
    for i, piece in enumerate(pieces):
        place = info[4 + i]
        columns = core_columns(place % 2, shard)
        near = place // 2 == core
        block = jnp.where(near, own[:, columns], came[:, columns])
        piece[:size] = block[:size]
        piece[size : 2 * size] = jnp.where(near, out[:, columns], out_came[:, columns])
        piece[2 * size : base] = extra[:, core_columns(place, shard)]
        gain_row = jnp.where(near, gain[0:1, columns], gain_came[0:1, columns])
        small = jnp.where(numbers == 0, gain_row, jnp.where(numbers == 1, head_row, 0.0))
        piece[base : base + SMALL] = small.astype(bf16)
        piece[base + SMALL :] = block[size:]


def project_final_kernel(
    info, parts, query, out_grad, key, value, router, gain1, gain2, head_gains, load, loss, total, key_value
):
    step = pl.program_id(0)
    size = out_grad.shape[0] // parts.shape[0]
    base = 2 * size + total.shape[0]
    rest = pair = 0.0
    for i in range(parts.shape[0]):
        block = parts[i].astype(f32)
        query[:, i * size : (i + 1) * size] = block[:size].T
        out_grad[i * size : (i + 1) * size] = block[size : 2 * size]
        rest += block[2 * size : base]
        pair += block[base:]

    @pl.when(step == 0)
    def _():
        total[...] = rest

    @pl.when(step > 0)
    def _():
        total[...] += rest

    @pl.when(step % 2 == 0)
    def _():
        key_value[...] = pair

    @pl.when(step % 2 == 1)
    def _():
        both = key_value[...] + pair
        key[...] = both[:size].T
        value[...] = both[size:].T

    @pl.when(step == pl.num_programs(0) - 1)
    def _():
        experts = router.shape[0]
        router[...] = total[:experts]

        def row(i):
            return total[experts + i : experts + i + 1, :]

        gain2[...] = row(0)
        counts = row(1)[:, :experts] + row(2)[:, :experts]
        probs = row(3)[:, :experts] + row(4)[:, :experts]
        kept = row(5)[:, :experts]
        share = counts / (kept * 8.0)
        load[...] = share * float(experts)
        loss[...] = float(experts) * jnp.sum(share * (probs / kept), axis=-1, keepdims=True)
        gain1[...] = row(SMALL)
        count = head_gains.shape[1]
        for part in range(2):
            sums = row(SMALL + 1)[:, part * size : (part + 1) * size]
            sums = pltpu.roll(jnp.broadcast_to(sums, (8, size)), (size - info[2] * count) % size, 1)
            head_gains[part : part + 1] = sums[:1, :count]


def body(
    tokens,
    cotangent,
    doc_lengths,
    padding,
    expert_ids,
    norm1_gain,
    w_query,
    key_weight,
    value_weight,
    q_gain,
    k_gain,
    w_out,
    norm2_gain,
    w_router,
    w_gate,
    w_up,
    w_down,
):
    core = lax.axis_index("tensor")
    context = lax.axis_index("context")
    mine = lax.axis_index("fsdp")
    place_x = context // SIDE
    place_z = context % SIDE
    sign = 1 - 2 * core
    span, width = tokens.shape[1:]
    half = width // 2
    size = 4 * q_gain.shape[0]
    expert_count = w_router.shape[1]
    local_experts, shard, hidden_units = w_gate.shape
    spans = SIDE * SIDE
    count = span * spans
    info = jnp.stack(
        [core, context * local_experts, mine, context]
        + [(mine + sign * i) % SIDE for i in range(SIDE)]
        + [place_x, place_z, sign, context // (spans // 2)]
    ).astype(jnp.int32)
    token_rows = tokens[0]
    cot_rows = cotangent[0]
    ids = expert_ids[0]
    pad_column = padding[0][:, None]

    first, second, inverse1 = call(
        token_message_kernel,
        [scalars] + [whole] * 3,
        [((HALF, half + EXTRA), bf16), ((HALF, half + EXTRA), bf16), ((span, 1), f32)],
    )(info, token_rows, ids, pad_column)

    positions = jnp.arange(count, dtype=jnp.int32)
    ends = jnp.cumsum(doc_lengths[0])
    passed = positions[:, None] >= ends[None, :]
    doc_index = jnp.sum(passed.astype(jnp.int32), axis=-1)
    starts = jnp.sum(jnp.where(passed, doc_lengths, 0), axis=-1)
    doc_rows = doc_index[:, None]
    doc_columns = doc_index[None, :]
    offsets = (positions - starts).astype(f32)
    frequency = theta_base ** (-jnp.arange(size // 2, dtype=f32) * 2.0 / size)
    angles = offsets[:, None] * frequency[None, :]
    cosine = jnp.cos(angles)
    sine = jnp.sin(angles)
    cosine = join([cosine, cosine], 1)
    sine = join([-sine, sine], 1)
    dense = call(
        dense_message_kernel,
        None,
        [((4 * size + expert_count + SMALL, shard), bf16)],
        grid_spec=pltpu.PrefetchScalarGridSpec(
            num_scalar_prefetch=1,
            grid=(1,),
            in_specs=[
                pl.BlockSpec((shard, size), lambda i, info: (0, info[3])),
                pl.BlockSpec((shard, size), lambda i, info: (0, info[11])),
                pl.BlockSpec((shard, size), lambda i, info: (0, info[11])),
                pl.BlockSpec((size, shard), lambda i, info: (info[3], 0)),
            ]
            + [whole] * 5,
            out_specs=[whole],
        ),
    )(
        after(info, first), w_query, key_weight, value_weight, w_out, w_router.T,
        norm1_gain[None], norm2_gain[None], q_gain[None], k_gain[None],
    )[0]
    dense_pieces = ring_gather(dense, moves_y())
    first_near, second_near = two_gathers(
        first, second, moves_z(), moves_x(), (dense_pieces[3],), (dense_pieces[1],)
    )
    pairs = join([w_gate, after(w_up, first_near[2])], 2)
    cot_half = lax.dynamic_slice_in_dim(cot_rows, core * half, half, axis=1)
    cot_all = lax.all_gather(cot_half, "context", axis=0)
    pairs_all = lax.all_gather(pairs, "fsdp", axis=0)
    first_pieces, second_pieces = two_gathers(
        stack(first_near),
        stack(second_near),
        moves_x(),
        moves_z(),
        (dense_pieces[2], cosine, sine, doc_rows),
    )
    token_pieces = first_pieces + second_pieces
    extra_rows = expert_count + SMALL
    dense_own, dense_away, out_own_rows, out_away_rows, extra = call(
        dense_split_kernel,
        [scalars] + [whole] * 4,
        [
            ((3 * size, half), bf16),
            ((3 * size, half), bf16),
            ((size, half), bf16),
            ((size, half), bf16),
            ((extra_rows, width), bf16),
        ],
    )(info, *dense_pieces)
    dense_came = other_core(dense_away)
    out_came_rows = other_core(out_away_rows)
    gain1 = lax.dynamic_slice(extra, (expert_count, core * half), (1, half)).astype(f32)
    gain_rows = extra[expert_count + 2 : expert_count + 4].reshape(2, SIDE, shard)[:, :, : size // SIDE]
    head_gains = jnp.pad(gain_rows.reshape(2, size).astype(f32), ((0, 6), (0, 0)))

    mark_spec = pl.BlockSpec((SIDE, HALF, EXTRA), lambda i: (0, 0, half // EXTRA))
    chosen, pads = call(
        slots_kernel,
        [scalars] + [mark_spec] * 8,
        [((spans, span, EXTRA), bf16), ((8, EXTRA), f32)],
        grid=(1,),
        out_specs=[whole, whole],
    )(info, *token_pieces)

    head_shape = (spans, span, size)
    own_part, away_part, normed1 = call(
        project_kernel,
        [scalars] + [whole] * 11,
        [((spans, span, 3 * size), f32), ((spans, span, 3 * size), bf16), ((spans, span, half), bf16)],
        flops=4 * count * half * 3 * size,
        moved=2 * 10**7,
    )(info, gain1, after(dense_own, cot_all), dense_came, *token_pieces)
    down_all = lax.all_gather(after(w_down, own_part), "fsdp", axis=0)
    mixed, raw, queries, keys, values, log_totals = call(
        attend_kernel,
        [whole] * 8,
        [
            (head_shape, bf16),
            ((count, 2 * size), f32),
            ((count, size), bf16),
            ((count, size), bf16),
            ((count, size), bf16),
            ((count, 1), f32),
        ],
        flops=4 * 10**9,
        moved=3 * 10**7,
    )(own_part, other_core(away_part), cosine, sine, head_gains, doc_rows, doc_columns, pads)
    mixed_came = other_core(mixed)
    piece_shape = (SIDE, HALF, half)
    branch_pieces = call(
        out_kernel, [scalars] + [whole] * 4, [(piece_shape, bf16)] * 8, flops=4 * count * size * half, moved=10**7
    )(info, mixed, mixed_came, out_own_rows, out_came_rows)
    branch = plane_scatter(branch_pieces)

    residual2, inverse2, normed2, probs, gates, picked_total, first, second = call(
        router_kernel,
        [scalars] + [whole] * 5,
        [
            ((span, width), f32),
            ((span, 1), f32),
            ((span, width), bf16),
            ((span, expert_count), f32),
            ((span, expert_count), f32),
            ((span, 1), f32),
            ((HALF, half + EXTRA), bf16),
            ((HALF, half + EXTRA), bf16),
        ],
    )(info, token_rows, branch, other_core(branch), ids, extra)
    cot_other = other_core(after(cot_all, first))
    slot_count = spans * SLOTS
    slot_grads = call(
        pick_spans_kernel,
        [scalars] + [whole] * 3,
        [((local_experts, slot_count, width), bf16)],
        flops=4 * 10**9,
        moved=2 * 10**7,
    )(info, chosen, cot_all, cot_other)[0]
    row_pieces = plane_gather(
        first, second, ((), (), (pairs_all,), (slot_grads,))
    )
    away_pieces = [other_core(piece) for piece in row_pieces]

    slot_rows, slot_marks = call(
        pick_rows_kernel,
        [scalars] + [whole] * 17,
        [((local_experts, slot_count, width), bf16), ((local_experts, slot_count, EXTRA), bf16)],
        flops=4 * 10**9,
        moved=2 * 10**7,
    )(info, chosen, *row_pieces, *away_pieces)
    expert_flops = 2 * local_experts * slot_count * width * hidden_units
    slot_half = (local_experts, slot_count, half)
    slot_hidden = (local_experts, slot_count, hidden_units)
    back_own, back_other, back_marks, hidden, pair_grads = per_expert(
        expert_kernel,
        info,
        [slot_rows, slot_marks, slot_grads, pairs_all, down_all],
        [slot_half, slot_half, (local_experts, slot_count, EXTRA), slot_hidden, slot_hidden[:2] + (2 * hidden_units,)],
        5 * expert_flops,
        5 * 10**7,
    )
    back_came = other_core(back_other)
    gate_grads, up_grads = per_expert(
        expert_grad_kernel,
        info,
        [slot_rows, pair_grads],
        [(SIDE, local_experts, shard, hidden_units)] * 2,
        2 * expert_flops,
        3 * 10**7,
    )
    grad_pieces = call(
        put_rows_kernel,
        [scalars] + [whole] * 4,
        [((SIDE, HALF, half + EXTRA), bf16)] * 8,
        flops=2 * 10**9,
        moved=2 * 10**7,
    )(info, chosen, back_own, after(back_came, gate_grads), back_marks)
    out_own, out_other, *down_grads = per_expert(
        expert_out_kernel,
        info,
        [slot_grads, after(hidden, grad_pieces[0]), down_all],
        [slot_half, slot_half] + [(local_experts, hidden_units, shard)] * 4,
        2 * expert_flops,
        3 * 10**7,
    )
    mixture_spans = call(
        put_spans_kernel,
        [whole] * 3,
        [((spans, span, half), bf16)],
        flops=2 * 10**9,
        moved=2 * 10**7,
    )(chosen, out_own, other_core(out_other))[0]
    gate_mine = lax.psum_scatter(gate_grads, "fsdp", scatter_dimension=0, tiled=False)
    grad_message = plane_scatter(grad_pieces, ((out_own,), (), ()))
    up_mine = lax.psum_scatter(up_grads, "fsdp", scatter_dimension=0, tiled=False)

    first, second, grad_residual2, router_rows = call(
        router_back_kernel,
        [scalars] + [whole] * 12,
        [
            ((HALF, half), bf16),
            ((HALF, half), bf16),
            ((span, width), f32),
            ((extra_rows, width), bf16),
        ],
        scratch_shapes=[pltpu.VMEM((span, width), bf16)],
    )(
        info, grad_message, other_core(grad_message), residual2, inverse2, normed2, probs, gates, picked_total,
        ids, pad_column, cot_rows, extra,
    )

    out_pieces = plane_gather(first, second, ((), (), (), (mixture_spans,)))
    heads_own, heads_away = call(
        heads_back_kernel,
        [scalars] + [whole] * 10,
        [((spans, span, size), f32)] * 2,
        flops=4 * count * size * half,
        moved=10**7,
    )(info, out_own_rows, out_came_rows, *out_pieces)
    mixture = lax.psum_scatter(mixture_spans, "context", scatter_dimension=0, tiled=False)
    result = call(result_kernel, [scalars] + [whole] * 3, [((span, width), f32)])(
        info, mixture, other_core(mixture), residual2
    )[0]
    heads_came, gate_mine, up_mine = together(other_core(heads_away), gate_mine, up_mine)
    grads, gain_grads = call(
        attend_back_kernel,
        [whole] * 13,
        [((spans, span, 3 * size), bf16), ((8, size), f32)],
        flops=8 * 10**9,
        moved=3 * 10**7,
        scratch_shapes=[pltpu.VMEM((count, size), bf16)] + [pltpu.VMEM((count, size), f32)] * 3,
    )(
        heads_own, heads_came, raw, queries, keys, values, log_totals,
        cosine, sine, head_gains, doc_rows, doc_columns, pads,
    )
    grads_came = other_core(grads)
    down_passing = moves_y()[0](down_grads[2])
    down_ahead = moves_y()[1](after(down_grads[3], down_passing))
    project_own, project_away, gain1_part = call(
        project_grad_kernel,
        [whole] * 6,
        [((3 * size, half), bf16)] * 2 + [((8, half), f32)],
        flops=4 * count * half * 3 * size,
        moved=2 * 10**7,
    )(grads, after(grads_came, down_passing), normed1, dense_own, dense_came, gain1)
    out_grad_own, out_grad_away = call(
        out_grad_kernel,
        [scalars] + [whole] * 10,
        [((size, half), bf16)] * 2,
        flops=4 * count * size * half,
        moved=10**7,
    )(info, after(mixed, heads_own), mixed_came, *out_pieces)
    project_came = other_core(project_away)
    message_shape = (4 * size + SMALL + extra_rows, shard)
    project_pieces = call(
        project_chunk_kernel, [scalars] + [whole] * 9, [(message_shape, bf16)] * 4
    )(
        info, project_own, project_came, gain1_part, other_core(gain1_part), gain_grads, other_core(gain_grads),
        out_grad_own, after(other_core(out_grad_away), down_ahead), router_rows,
    )
    passing = moves_y()[0](project_pieces[2])
    from_ahead = moves_y()[1](project_pieces[3])
    input_pieces = call(
        input_back_kernel,
        [scalars] + [whole] * 4,
        [(piece_shape, bf16)] * 8,
        flops=4 * count * half * 3 * size,
        moved=3 * 10**7,
    )(info, grads, after(grads_came, project_pieces[0]), dense_own, dense_came)
    from_behind = moves_y()[0](add_low(project_pieces[1], after(passing, input_pieces[0])))
    message = after(low_sum((project_pieces[0], from_behind, from_ahead)), result)
    message_all = lax.all_gather(message, "context", axis=0)
    down_behind = moves_y()[0](add_low(down_grads[1], down_passing))
    final_rows = plane_scatter(input_pieces, ((), (down_behind,), ()))
    grad_input = call(final_rows_kernel, [scalars] + [whole] * 6, [((span, width), f32)])(
        info, final_rows, other_core(final_rows), token_rows, inverse1, extra, grad_residual2
    )[0]
    final_gate = gate_mine.astype(f32)
    final_up = up_mine.astype(f32)
    final_down = down_grads[0].astype(f32) + down_ahead.astype(f32) + down_behind.astype(f32)
    (
        final_query, final_out, final_key, final_value, final_router, final_gain1, final_gain2, final_head_gains,
        expert_load, balance_loss,
    ) = call(
        project_final_kernel,
        [scalars, pl.BlockSpec((SIDE,) + message_shape, lambda i: (i, 0, 0))],
        [
            ((shard, spans * size), f32),
            ((spans * size, shard), f32),
            ((shard, 2 * size), f32),
            ((shard, 2 * size), f32),
            ((expert_count, shard), f32),
            ((1, shard), f32),
            ((1, shard), f32),
            ((2, size // SIDE), f32),
            ((1, expert_count), f32),
            ((1, 1), f32),
        ],
        grid=(SIDE,),
        out_specs=[
            pl.BlockSpec((shard, SIDE * size), lambda i: (0, i)),
            pl.BlockSpec((SIDE * size, shard), lambda i: (i, 0)),
            pl.BlockSpec((shard, size), lambda i: (0, i // 2)),
            pl.BlockSpec((shard, size), lambda i: (0, i // 2)),
        ]
        + [whole] * 6,
        scratch_shapes=[pltpu.VMEM((SMALL + extra_rows, shard), f32), pltpu.VMEM((2 * size, shard), f32)],
    )(info, after(message_all, grad_input, final_gate, final_up, final_down))

    return (
        result[None],
        balance_loss.reshape(()),
        expert_load.reshape(expert_count),
        grad_input[None],
        final_gain1.reshape(shard),
        final_query,
        final_key,
        final_value,
        final_head_gains[0],
        final_head_gains[1],
        final_out,
        final_gain2.reshape(shard),
        final_router.T,
        final_gate,
        final_up,
        final_down,
    )


def solution(mesh):
    in_specs = (
        P("fsdp", "context", None),
        P("fsdp", "context", None),
        P("fsdp", None),
        P("fsdp", "context"),
        P("fsdp", "context", None),
        P("fsdp"),
        P("fsdp", "tensor"),
        P("fsdp", "tensor"),
        P("fsdp", "tensor"),
        P("fsdp"),
        P("fsdp"),
        P("tensor", "fsdp"),
        P("fsdp"),
        P("fsdp", None),
        P("context", "fsdp", "tensor"),
        P("context", "fsdp", "tensor"),
        P("context", "tensor", "fsdp"),
    )
    out_specs = (
        P("fsdp", "context", None),
        P(),
        P(),
        P("fsdp", "context", None),
        P("fsdp"),
        P("fsdp", "tensor"),
        P("fsdp", "tensor"),
        P("fsdp", "tensor"),
        P("fsdp"),
        P("fsdp"),
        P("tensor", "fsdp"),
        P("fsdp"),
        P("fsdp", None),
        P("context", "fsdp", "tensor"),
        P("context", "fsdp", "tensor"),
        P("context", "tensor", "fsdp"),
    )
    return jax.shard_map(body, mesh=mesh, in_specs=in_specs, out_specs=out_specs, check_vma=False)
```

```python
import jax
import jax.numpy as jnp
from jax import lax
from jax.experimental import pallas as pl
from jax.experimental.pallas import tpu as pltpu
from jax.sharding import PartitionSpec as P

WINDOW = 1024
SIDE = 4
HALF = 64
QUERY_BLOCK = 256
SLOTS = 32
EXTRA = 128
SMALL = 16

epsilon = 1e-06
theta_base = 1000000.0
negative = -1e30
f32 = jnp.float32
bf16 = jnp.bfloat16
vmem_limit = 56 * 1024 * 1024
whole = pl.BlockSpec(memory_space=pltpu.VMEM)
scalars = pl.BlockSpec(memory_space=pltpu.SMEM)


def call(kernel, in_specs, out_shape, flops=10**6, moved=10**6, **rest):
    if in_specs is not None:
        rest["in_specs"] = in_specs
    return pl.pallas_call(
        kernel,
        out_shape=[jax.ShapeDtypeStruct(shape, kind) for shape, kind in out_shape],
        compiler_params=pltpu.CompilerParams(vmem_limit_bytes=vmem_limit),
        cost_estimate=pl.CostEstimate(flops=flops, bytes_accessed=moved, transcendentals=0),
        **rest,
    )


def dot_nt(left, right):
    return lax.dot_general(left, right, (((1,), (1,)), ((), ())), preferred_element_type=f32)


def dot_tn(left, right):
    return lax.dot_general(left, right, (((0,), (0,)), ((), ())), preferred_element_type=f32)


def dot_nn(left, right):
    return jnp.dot(left, right, preferred_element_type=f32)


def join(parts, axis=0):
    return jnp.concatenate(parts, axis=axis)


def ring_moves(axis, target):
    forward = []
    backward = []
    count = lax.axis_size(axis)
    for i in range(count):
        for core, sign in ((0, 1), (1, -1)):
            forward.append((2 * i + core, 2 * target(i, sign) + core))
            backward.append((2 * i + core, 2 * target(i, -sign) + core))

    def move(pairs):
        return lambda value: lax.ppermute(value, (axis, "tensor"), pairs)

    return move(forward), move(backward)


def moves_z():
    return ring_moves("context", lambda i, step: (i // SIDE) * SIDE + (i + step) % SIDE)


def moves_x():
    return ring_moves("context", lambda i, step: (i + SIDE * step) % (SIDE * SIDE))


def moves_y():
    return ring_moves("fsdp", lambda i, step: (i + step) % SIDE)


def other_core(value):
    return lax.ppermute(value, "tensor", [(0, 1), (1, 0)])


def after(value, *events):
    return lax.optimization_barrier((value, *events))[0]


def ring_gather(value, moves):
    behind = moves[0](value)
    ahead = moves[1](value)
    far = moves[0](behind)
    return [value, ahead, far, behind]


def add_low(left, right):
    return (left.astype(f32) + right.astype(f32)).astype(bf16)


def low_sum(terms):
    return sum(term.astype(f32) for term in terms).astype(bf16)


def across(value, step):
    pairs = [(i, i ^ (SIDE * step)) for i in range(SIDE * SIDE)]
    return lax.ppermute(value, "context", pairs)


def along_x(value, step):
    pairs = [(i, (i + SIDE * step) % (SIDE * SIDE)) for i in range(SIDE * SIDE)]
    return lax.ppermute(value, "context", pairs)


def along_z(value, step):
    pairs = [(i, (i // SIDE) * SIDE + (i + step) % SIDE) for i in range(SIDE * SIDE)]
    return lax.ppermute(value, "context", pairs)


def ring_scatter(parts, moves):
    passing = moves[0](parts[2])
    from_ahead = moves[1](parts[3])
    from_behind = moves[0](add_low(parts[1], passing))
    return parts[0], from_behind, from_ahead


def together(*values):
    return lax.optimization_barrier(values)


def stack_kernel(a, b, c, d, result):
    for i, part in enumerate((a, b, c, d)):
        result[i] = part[...]


def stack(parts):
    shape = parts[0].shape
    return call(stack_kernel, [whole] * 4, [((4,) + shape, bf16)])(*parts)[0]


def two_gathers(left, right, left_moves, right_moves, events=(), last=()):
    left_behind = left_moves[0](left)
    left_ahead = left_moves[1](left)
    right_behind = right_moves[0](right)
    right_ahead = right_moves[1](right)
    left_behind, left_ahead, right_behind, right_ahead = together(
        left_behind, left_ahead, right_behind, right_ahead, *events
    )[:4]
    left_far = left_moves[0](left_behind)
    right_far = right_moves[0](right_behind)
    left_far, right_far = together(left_far, right_far, *last)[:2]
    return [left, left_ahead, left_far, left_behind], [right, right_ahead, right_far, right_behind]


def two_short_gathers(left, right, events=()):
    left_moves, right_moves = moves_z(), moves_x()
    values = (
        left_moves[1](left),
        along_z(left, 2),
        left_moves[0](left),
        right_moves[1](right),
        along_x(right, 2),
        right_moves[0](right),
    )
    values = together(*values, *events)[:6]
    return [left, *values[:3]], [right, *values[3:]]


def two_short_scatters(left, right, events=()):
    left_moves, right_moves = moves_z(), moves_x()
    values = (
        left_moves[1](left[3]),
        along_z(left[2], 2),
        left_moves[0](left[1]),
        right_moves[1](right[3]),
        along_x(right[2], 2),
        right_moves[0](right[1]),
    )
    values = together(*values, *events)[:6]
    return (left[0], *values[:3]), (right[0], *values[3:])


def plane_gather(first, second, events=((), (), (), ())):
    first_near, second_near = two_short_gathers(first, second, events[0])
    first_pieces, second_pieces = two_gathers(
        stack(first_near), stack(second_near), moves_x(), moves_z(), *events[2:]
    )
    return first_pieces + second_pieces


def unstack_kernel(a, b, c, r0, r1, r2, r3):
    for i, part in enumerate((r0, r1, r2, r3)):
        part[...] = (a[i].astype(f32) + b[i].astype(f32) + c[i].astype(f32)).astype(bf16)


def unstack(terms):
    shape = terms[0].shape[1:]
    return call(unstack_kernel, [whole] * 3, [(shape, bf16)] * 4)(*terms)


def total_kernel(*refs):
    result = refs[8]
    for i in range(2):
        a, b, c, d = (part[...].astype(f32) for part in refs[4 * i : 4 * i + 4])
        result[i * HALF : (i + 1) * HALF] = (a + b) + (c + d)


def two_scatters(left, right, left_moves, right_moves, events=(), last=()):
    left_passing = left_moves[0](left[2])
    left_from_ahead = left_moves[1](left[3])
    right_passing = right_moves[0](right[2])
    right_from_ahead = right_moves[1](right[3])
    left_passing, left_from_ahead, right_passing, right_from_ahead, *events = together(
        left_passing, left_from_ahead, right_passing, right_from_ahead, *events
    )
    left_from_behind = left_moves[0](add_low(left[1], left_passing))
    right_from_behind = right_moves[0](add_low(right[1], right_passing))
    left_from_behind, right_from_behind, *last = together(left_from_behind, right_from_behind, *last)
    left_terms = (left[0], left_from_behind, left_from_ahead)
    right_terms = (right[0], right_from_behind, right_from_ahead)
    return left_terms, right_terms, events, last


def plane_scatter(pieces, events=((), (), ())):
    first, second, *_ = two_scatters(pieces[:4], pieces[4:], moves_x(), moves_z(), *events[:2])
    first, second = two_short_scatters(unstack(first), unstack(second), events[2])
    return total(first, second)


def total(first, second):
    width = first[0].shape[-1]
    return call(total_kernel, [whole] * 8, [((2 * HALF, width), f32)])(*first, *second)[0]


def split_low(value, count):
    parts = []
    rest = value
    for _ in range(count):
        part = rest.astype(bf16)
        parts.append(part)
        rest = rest - part.astype(f32)
    return parts


def core_columns(core, width):
    return pl.ds(pl.multiple_of(core * width, width), width)


def token_message_kernel(info, tokens, ids, padding, first, second, inverse_out):
    width = tokens.shape[1]
    half = width // 2
    rows = tokens[...].astype(f32)
    inverse = lax.rsqrt(jnp.mean(rows * rows, axis=-1, keepdims=True) + epsilon)
    inverse_out[...] = inverse
    lanes = lax.broadcasted_iota(jnp.int32, (rows.shape[0], EXTRA), 1)
    marks = jnp.zeros((rows.shape[0], EXTRA), f32)
    for k in range(8):
        marks = jnp.where(lanes == k, ids[:, k : k + 1].astype(f32), marks)
    marks = jnp.where(lanes == 8, padding[...].astype(f32), marks)
    for k, part in enumerate(split_low(inverse, 3)):
        marks = jnp.where(lanes == 9 + k, part.astype(f32), marks)
    marks = marks.astype(bf16)
    own = tokens[:, core_columns(info[0], half)]
    first[:, :half] = own[:HALF]
    first[:, half:] = marks[:HALF]
    second[:, :half] = own[HALF:]
    second[:, half:] = marks[HALF:]


def dense_message_kernel(info, query, key, value, out, router, gain1, gain2, q_gain, k_gain, result):
    size = query.shape[1]
    experts = router.shape[0]
    result[:size] = query[...].T
    result[size : 2 * size] = key[...].T
    result[2 * size : 3 * size] = value[...].T
    result[3 * size : 4 * size] = out[...]
    result[4 * size : 4 * size + experts] = router[...]
    base = 4 * size + experts
    rows = lax.broadcasted_iota(jnp.int32, (SMALL, result.shape[1]), 0)
    gains = jnp.where(rows == 0, gain1[...].astype(f32), 0.0)
    gains = jnp.where(rows == 1, gain2[...].astype(f32), gains)
    rest = jnp.zeros((1, result.shape[1] - q_gain.shape[1]), f32)
    gains = jnp.where(rows == 2, join([q_gain[...].astype(f32), rest], 1), gains)
    gains = jnp.where(rows == 3, join([k_gain[...].astype(f32), rest], 1), gains)
    result[base:] = gains.astype(bf16)


def dense_split_kernel(info, a, b, c, d, own, away, own_out, away_out, extra):
    shard = a.shape[1]
    rows = own.shape[0]
    size = own_out.shape[0]
    core = info[0]
    for i, piece in enumerate((a, b, c, d)):
        place = info[4 + i]
        columns = core_columns(place % 2, shard)

        @pl.when(place // 2 == core)
        def _():
            own[:, columns] = piece[:rows]
            own_out[:, columns] = piece[rows : rows + size]

        @pl.when(place // 2 != core)
        def _():
            away[:, columns] = piece[:rows]
            away_out[:, columns] = piece[rows : rows + size]

        extra[:, core_columns(place, shard)] = piece[rows + size :]


def slots_kernel(info, *refs):
    pieces, (chosen, pads) = refs[:8], refs[8:]
    first_expert = info[1]
    place_x, place_z, sign = info[8], info[9], info[10]
    shape = (2 * HALF, EXTRA)
    lanes = lax.broadcasted_iota(jnp.int32, shape, 1)
    rows = lax.broadcasted_iota(jnp.int32, shape, 0)
    earlier = (lanes < rows).astype(bf16)
    pad_total = jnp.zeros((1, EXTRA), f32)
    for ix in range(SIDE):
        for iz in range(SIDE):
            marks = join([pieces[ix][iz], pieces[4 + iz][ix]]).astype(f32)
            pad_total += jnp.sum(marks, axis=0, keepdims=True)
            named = jnp.zeros(shape, f32)
            for e in range(EXTRA // SLOTS):
                hit = jnp.where((lanes < 8) & (marks == (first_expert + e).astype(f32)), 1.0, 0.0)
                hit = jnp.max(hit, axis=-1, keepdims=True)
                named = jnp.where(lanes // SLOTS == e, hit, named)
            ranks = dot_nn(earlier, named.astype(bf16))
            match = (named > 0.0) & (ranks == (lanes % SLOTS).astype(f32))
            place = ((place_x + sign * ix) % SIDE) * SIDE + (place_z + sign * iz) % SIDE
            chosen[place] = jnp.where(match, 1.0, 0.0).astype(bf16)
    pads[...] = jnp.broadcast_to(pad_total, pads.shape)


def write_slots(result, place, columns, slots):
    for e in range(EXTRA // SLOTS):
        target = pl.ds(pl.multiple_of(place * SLOTS, SLOTS), SLOTS)
        result[e, target, columns] = slots[e * SLOTS : (e + 1) * SLOTS]


def read_slots(source, place, columns):
    target = pl.ds(pl.multiple_of(place * SLOTS, SLOTS), SLOTS)
    return join([source[e, target, columns] for e in range(EXTRA // SLOTS)])


def pick_rows_kernel(info, chosen, *refs):
    own, other, (result, extra) = refs[:8], refs[8:16], refs[16:]
    core, place_x, place_z, sign = info[0], info[8], info[9], info[10]
    half = result.shape[-1] // 2
    own_columns = core_columns(core, half)
    other_columns = core_columns(1 - core, half)
    for ix in range(SIDE):
        for iz in range(SIDE):
            place = ((place_x + sign * ix) % SIDE) * SIDE + (place_z + sign * iz) % SIDE
            matrix = chosen[place]
            rows = join([own[ix][iz], own[4 + iz][ix]])
            slots = dot_tn(matrix, rows).astype(bf16)
            write_slots(result, place, own_columns, slots[:, :half])
            write_slots(extra, place, slice(None), slots[:, half:])
            jx, jz = -ix % SIDE, -iz % SIDE
            rows = join([other[jx][jz, :, :half], other[4 + jz][jx, :, :half]])
            write_slots(result, place, other_columns, dot_tn(matrix, rows).astype(bf16))


def pick_spans_kernel(info, chosen, own, other, result):
    core = info[0]
    half = own.shape[-1]
    for place in range(SIDE * SIDE):
        matrix = chosen[place]
        write_slots(result, place, core_columns(core, half), dot_tn(matrix, own[place]).astype(bf16))
        write_slots(result, place, core_columns(1 - core, half), dot_tn(matrix, other[place]).astype(bf16))


def put_rows_kernel(info, chosen, own, came, extra, *pieces):
    place_x, place_z, sign = info[8], info[9], info[10]
    half = own.shape[-1]
    for ix in range(SIDE):
        for iz in range(SIDE):
            place = ((place_x + sign * ix) % SIDE) * SIDE + (place_z + sign * iz) % SIDE
            matrix = chosen[place]
            rows = read_slots(own, place, slice(None)).astype(f32) + read_slots(came, place, slice(None)).astype(f32)
            rows = dot_nn(matrix, rows.astype(bf16)).astype(bf16)
            marks = dot_nn(matrix, read_slots(extra, place, slice(None))).astype(bf16)
            pieces[ix][iz, :, :half] = rows[:HALF]
            pieces[4 + iz][ix, :, :half] = rows[HALF:]
            pieces[ix][iz, :, half:] = marks[:HALF]
            pieces[4 + iz][ix, :, half:] = marks[HALF:]


def put_spans_kernel(chosen, own, came, result):
    for place in range(SIDE * SIDE):
        rows = read_slots(own, place, slice(None)).astype(f32) + read_slots(came, place, slice(None)).astype(f32)
        result[place] = dot_nn(chosen[place], rows.astype(bf16)).astype(bf16)


def span_of(info, ix, iz):
    return ((info[8] + info[10] * ix) % SIDE) * SIDE + (info[9] + info[10] * iz) % SIDE


def piece_parts(info, i):
    for j in range(SIDE):
        if i < SIDE:
            yield j, span_of(info, i, j), slice(0, HALF)
        else:
            yield j, span_of(info, j, i - SIDE), slice(HALF, 2 * HALF)


def project_kernel(info, gain, own, came, *refs):
    pieces, (own_out, other_out, normed_out) = refs[:8], refs[8:]
    half = gain.shape[1]
    wide = own_out.shape[-1]
    count = SIDE * HALF
    lanes = lax.broadcasted_iota(jnp.int32, (count, EXTRA), 1)
    for i, piece in enumerate(pieces):
        rows = piece[...].reshape(count, half + EXTRA)
        marks = jnp.where((lanes >= 9) & (lanes < 12), rows[:, half:].astype(f32), 0.0)
        inverse = jnp.sum(marks, axis=-1, keepdims=True)
        normed = (rows[:, :half].astype(f32) * inverse * gain[...]).astype(bf16)
        own_rows = dot_nt(normed, own[...])
        other_rows = dot_nt(normed, came[...])
        for j, span, part in piece_parts(info, i):
            cut = slice(j * HALF, (j + 1) * HALF)
            normed_out[span, part] = normed[cut]
            own_out[span, part] = own_rows[cut]
            other_out[span, part] = other_rows[cut].astype(bf16)


def turn(value, cosine, sine):
    return value * cosine + pltpu.roll(value, 64, 1) * sine


def block_mask(doc_rows, doc_columns, real, query_start, key_start, query_count, key_count):
    positions = lax.broadcasted_iota(jnp.int32, (1, key_count), 1) + key_start
    doc_columns = jnp.where(positions < real, doc_columns, -1)
    offsets = lax.broadcasted_iota(jnp.int32, (query_count, query_count), 0) - lax.broadcasted_iota(
        jnp.int32, (query_count, query_count), 1
    )
    same = doc_rows == doc_columns[:, key_count - query_count :]
    parts = [((offsets >= 0) & same) | (offsets == 0)]
    begin = 0
    if query_start - key_start == WINDOW:
        begin = query_count
        parts.insert(0, (offsets < 0) & (doc_rows == doc_columns[:, :begin]))
    if begin < key_count - query_count:
        parts.insert(-1, doc_rows == doc_columns[:, begin : key_count - query_count])
    return parts


def keep(parts, values, other):
    result = []
    begin = 0
    for part in parts:
        end = begin + part.shape[1]
        result.append(jnp.where(part, values[:, begin:end], other))
        begin = end
    return result[0] if len(result) == 1 else join(result, 1)


def real_count(pads, count):
    return (count - pads[0:1, 8:9]).astype(jnp.int32)


def attend_kernel(
    own, came, cosine, sine, gains, doc_rows, doc_columns, pads,
    mixed, raw, queries, keys, values, log_totals,
):
    count = queries.shape[0]
    size = queries.shape[1]
    span = mixed.shape[1]
    scale = size ** (-0.5)

    def prepare(j, carry):
        rows = pl.ds(pl.multiple_of(j * span, span), span)
        block = own[j] + came[j].astype(f32)
        raw[rows, :] = block[:, : 2 * size]
        cos_rows = cosine[rows, :]
        sin_rows = sine[rows, :]
        for part, target in ((0, queries), (1, keys)):
            piece = block[:, part * size : (part + 1) * size]
            inverse = lax.rsqrt(jnp.mean(piece * piece, axis=-1, keepdims=True) + epsilon)
            normed = piece * inverse * gains[part : part + 1, :]
            target[rows, :] = turn(normed, cos_rows, sin_rows).astype(bf16)
        values[rows, :] = block[:, 2 * size :].astype(bf16)
        return carry

    lax.fori_loop(0, count // span, prepare, 0)
    real = real_count(pads, float(count))
    for start in range(0, count, QUERY_BLOCK):
        low = max(0, start - WINDOW)
        high = start + QUERY_BLOCK
        scores = dot_nt(queries[start:high, :], keys[low:high, :]) * scale
        allowed = block_mask(
            doc_rows[start:high, :], doc_columns[:, low:high], real, start, low, QUERY_BLOCK, high - low
        )
        scores = keep(allowed, scores, negative)
        peak = jnp.max(scores, axis=-1, keepdims=True)
        exponent = jnp.exp(scores - peak)
        total = jnp.sum(exponent, axis=-1, keepdims=True)
        weights = (exponent * (1.0 / total)).astype(bf16)
        rows = dot_nn(weights, values[low:high, :]).astype(bf16)
        mixed[start // span : high // span] = rows.reshape(QUERY_BLOCK // span, span, size)
        log_totals[start:high, :] = peak + jnp.log(total)


def attend_back_kernel(
    own, came, raw, queries, keys, values, log_totals, cosine, sine, gains, doc_rows, doc_columns, pads,
    grads, gain_grads, grad_mixed, grad_queries, grad_keys, grad_values,
):
    count = queries.shape[0]
    size = queries.shape[1]
    span = grads.shape[1]
    scale = size ** (-0.5)
    grad_mixed[...] = (own[...] + came[...]).astype(bf16).reshape(count, size)
    grad_keys[...] = jnp.zeros_like(grad_keys)
    grad_values[...] = jnp.zeros_like(grad_values)
    real = real_count(pads, float(count))
    for start in range(0, count, QUERY_BLOCK):
        low = max(0, start - WINDOW)
        high = start + QUERY_BLOCK
        query_rows = queries[start:high, :]
        key_rows = keys[low:high, :]
        grad_rows = grad_mixed[start:high, :]
        scores = dot_nt(query_rows, key_rows) * scale
        allowed = block_mask(
            doc_rows[start:high, :], doc_columns[:, low:high], real, start, low, QUERY_BLOCK, high - low
        )
        soft = keep(allowed, jnp.exp(scores - log_totals[start:high, :]), 0.0)
        grad_soft = dot_nt(grad_rows, values[low:high, :])
        row_dot = jnp.sum(soft * grad_soft, axis=-1, keepdims=True)
        grad_scores = (soft * (grad_soft - row_dot)).astype(bf16)
        grad_queries[start:high, :] = dot_nn(grad_scores, key_rows) * scale
        grad_keys[low:high, :] += dot_tn(grad_scores, query_rows) * scale
        grad_values[low:high, :] += dot_tn(soft.astype(bf16), grad_rows)
    gain_grads[...] = jnp.zeros_like(gain_grads)

    def finish(j, carry):
        rows = pl.ds(pl.multiple_of(j * span, span), span)
        cos_rows = cosine[rows, :]
        sin_rows = sine[rows, :]
        parts = []
        for part, source in ((0, grad_queries), (1, grad_keys)):
            piece = raw[rows, part * size : (part + 1) * size]
            inverse = lax.rsqrt(jnp.mean(piece * piece, axis=-1, keepdims=True) + epsilon)
            back = turn(source[rows, :], cos_rows, -sin_rows)
            gain_grads[part : part + 1, :] += jnp.sum(back * piece * inverse, axis=0, keepdims=True)
            scaled = back * gains[part : part + 1, :]
            mean = jnp.mean(scaled * piece, axis=-1, keepdims=True)
            parts.append((inverse * scaled - piece * (inverse * inverse * inverse * mean)).astype(bf16))
        parts.append(grad_values[rows, :].astype(bf16))
        grads[j] = join(parts, 1)
        return carry

    lax.fori_loop(0, count // span, finish, 0)


def out_kernel(info, mixed, came_mixed, own, came, *pieces):
    for i, piece in enumerate(pieces):
        parts = list(piece_parts(info, i))
        left = join([mixed[span, part] for _, span, part in parts])
        right = join([came_mixed[span, part] for _, span, part in parts])
        rows = dot_nn(left, own[...]) + dot_nn(right, came[...])
        piece[...] = rows.astype(bf16).reshape(piece.shape)


def heads_back_kernel(info, own, came, *refs):
    pieces, (own_out, other_out) = refs[:8], refs[8:]
    for i, piece in enumerate(pieces):
        rows = piece[...].reshape(SIDE * HALF, piece.shape[-1])
        own_rows = dot_nt(rows, own[...])
        other_rows = dot_nt(rows, came[...])
        for j, span, part in piece_parts(info, i):
            cut = slice(j * HALF, (j + 1) * HALF)
            own_out[span, part] = own_rows[cut]
            other_out[span, part] = other_rows[cut]


def out_grad_kernel(info, mixed, came_mixed, *refs):
    pieces, (own_out, away_out) = refs[:8], refs[8:]
    own_total = away_total = 0.0
    for i, piece in enumerate(pieces):
        rows = piece[...].reshape(SIDE * HALF, piece.shape[-1])
        parts = list(piece_parts(info, i))
        own_total += dot_tn(join([mixed[span, part] for _, span, part in parts]), rows)
        away_total += dot_tn(join([came_mixed[span, part] for _, span, part in parts]), rows)
    own_out[...] = own_total.astype(bf16)
    away_out[...] = away_total.astype(bf16)


def input_back_kernel(info, grads, came_grads, own, came, *pieces):
    for i, piece in enumerate(pieces):
        parts = list(piece_parts(info, i))
        left = join([grads[span, part] for _, span, part in parts])
        right = join([came_grads[span, part] for _, span, part in parts])
        rows = dot_nn(left, own[...]) + dot_nn(right, came[...])
        piece[...] = rows.astype(bf16).reshape(piece.shape)


def project_grad_kernel(grads, came_grads, normed, own, came, gain, own_out, away_out, gain_grad):
    count = normed.shape[0] * normed.shape[1]
    wide = grads.shape[-1]
    rows = normed[...].reshape(count, normed.shape[-1])
    total = 0.0
    for source, weight, target in ((grads, own, own_out), (came_grads, came, away_out)):
        result = dot_tn(source[...].reshape(count, wide), rows)
        target[...] = result.astype(bf16)
        total += jnp.sum(result * weight[...].astype(f32), axis=0, keepdims=True)
    gain_grad[...] = jnp.broadcast_to(total / gain[...], gain_grad.shape)


def halves(core, own, came):
    return join([jnp.where(core == 0, own, came), jnp.where(core == 0, came, own)], 1)


def chosen_experts(ids, count):
    lanes = lax.broadcasted_iota(jnp.int32, (ids.shape[0], count), 1)
    chosen = jnp.zeros((ids.shape[0], count), f32)
    for k in range(8):
        chosen = jnp.where(lanes == ids[:, k : k + 1], 1.0, chosen)
    return chosen


def router_kernel(
    info, tokens, own, came, ids, extra, residual_out, inverse_out, normed_out, probs_out, gates_out, total_out, first, second
):
    core = info[0]
    half = tokens.shape[1] // 2
    experts = probs_out.shape[1]
    residual = tokens[...].astype(f32) + halves(core, own[...], came[...])
    residual_out[...] = residual
    inverse = lax.rsqrt(jnp.mean(residual * residual, axis=-1, keepdims=True) + epsilon)
    inverse_out[...] = inverse
    gain = extra[experts + 1 : experts + 2, :].astype(f32)
    normed = (residual * inverse * gain).astype(bf16)
    normed_out[...] = normed
    logits = dot_nt(normed, extra[:experts, :])
    exponent = jnp.exp(logits - jnp.max(logits, axis=-1, keepdims=True))
    probs = exponent / jnp.sum(exponent, axis=-1, keepdims=True)
    probs_out[...] = probs
    chosen = chosen_experts(ids, experts)
    picked = probs * chosen
    total = jnp.sum(picked, axis=-1, keepdims=True)
    total_out[...] = total
    gates = picked / total
    gates_out[...] = gates
    marks = join(split_low(gates, 2), 1)
    mine = normed_out[:, core_columns(core, half)]
    first[:, :half] = mine[:HALF]
    first[:, half:] = marks[:HALF]
    second[:, :half] = mine[HALF:]
    second[:, half:] = marks[HALF:]


def router_back_kernel(
    info, own, came, residual_ref, inverse_ref, normed, probs_ref, gates_ref, total, ids, padding, cotangent, extra,
    first, second, grad_out, rows_out, scratch,
):
    core = info[0]
    half = cotangent.shape[1] // 2
    experts = probs_ref.shape[1]
    probs = probs_ref[...]
    gates = gates_ref[...]
    residual = residual_ref[...]
    inverse = inverse_ref[...]
    marks = own[:, half:] + came[:, half:]
    gate_grads = marks[:, :experts] + marks[:, experts:]
    chosen = chosen_experts(ids, experts)
    grad_picked = (gate_grads - jnp.sum(gate_grads * gates, axis=-1, keepdims=True)) / total[...]
    grad_probs = chosen * grad_picked
    grad_logits = (probs * (grad_probs - jnp.sum(grad_probs * probs, axis=-1, keepdims=True))).astype(bf16)
    grad_normed = halves(core, own[:, :half], came[:, :half]) + dot_nn(grad_logits, extra[:experts, :])
    scaled = grad_normed * extra[experts + 1 : experts + 2, :].astype(f32)
    mean = jnp.mean(scaled * residual, axis=-1, keepdims=True)
    grad = cotangent[...].astype(f32) + inverse * scaled - residual * (inverse * inverse * inverse * mean)
    grad_out[...] = grad
    scratch[...] = grad.astype(bf16)
    mine = scratch[:, core_columns(core, half)]
    first[...] = mine[:HALF]
    second[...] = mine[HALF:]
    gain_grad = jnp.sum(grad_normed * residual * inverse, axis=0, keepdims=True)
    rows_out[:experts] = dot_tn(grad_logits, normed[...]).astype(bf16)
    kept = 1.0 - padding[...].astype(f32)
    shard = 4 * EXTRA
    rest = jnp.zeros((1, shard - experts), f32)

    def row(values):
        return join([values, rest] * SIDE, 1)

    counted = chosen * kept
    probs_sum = jnp.sum(probs * kept, axis=0, keepdims=True)
    probs_high = probs_sum.astype(bf16).astype(f32)
    kept_sum = jnp.broadcast_to(jnp.sum(kept, axis=0, keepdims=True), (1, experts))
    rows = (
        gain_grad,
        row(jnp.sum(counted[:HALF], axis=0, keepdims=True)),
        row(jnp.sum(counted[HALF:], axis=0, keepdims=True)),
        row(probs_high),
        row(probs_sum - probs_high),
        row(kept_sum),
    )
    numbers = lax.broadcasted_iota(jnp.int32, (SMALL, 2 * half), 0)
    small = jnp.zeros((SMALL, 2 * half), f32)
    for i, values in enumerate(rows):
        small = jnp.where(numbers == i, values, small)
    rows_out[experts:] = small.astype(bf16)


def final_rows_kernel(info, own, came, tokens, inverse_ref, extra, grad_residual, grad_input):
    core = info[0]
    base = extra.shape[0] - SMALL
    rows = tokens[...].astype(f32)
    inverse = inverse_ref[...]
    scaled = halves(core, own[...], came[...]) * extra[base : base + 1, :].astype(f32)
    mean = jnp.mean(scaled * rows, axis=-1, keepdims=True)
    grad_input[...] = grad_residual[...] + inverse * scaled - rows * (inverse * inverse * inverse * mean)


def result_kernel(info, own, came, residual, result):
    result[...] = residual[...] + halves(info[0], own[...].astype(f32), came[...].astype(f32))


def expert_kernel(info, rows, marks, grads, pairs_w, downs_w, back_own, back_other, back_marks, hidden_out, pairs_out):
    core = info[0]
    expert = info[1] + pl.program_id(0)
    shard = pairs_w.shape[2]
    count = rows.shape[1]
    units = hidden_out.shape[2]
    pairs = grad_raw = 0.0
    for place in range(SIDE):
        columns = slice(place * shard, (place + 1) * shard)
        pairs += dot_nn(rows[0, :, columns], pairs_w[place, 0])
        grad_raw += dot_nt(grads[0, :, columns], downs_w[place, 0])
    gate_pre = pairs[:, :units]
    up_pre = pairs[:, units:]
    lanes = lax.broadcasted_iota(jnp.int32, (count, EXTRA), 1)
    high_lane = lanes == expert
    low_lane = lanes == expert + EXTRA // 2
    gates = jnp.sum(jnp.where(high_lane | low_lane, marks[0].astype(f32), 0.0), axis=-1, keepdims=True)
    sigmoid = jax.nn.sigmoid(gate_pre)
    activated = gate_pre * sigmoid
    hidden = (activated * up_pre).astype(bf16).astype(f32)
    gate_grads = jnp.sum(hidden * grad_raw, axis=-1, keepdims=True)
    grad_hidden = gates * grad_raw
    gate_low = (grad_hidden * up_pre * sigmoid * (1.0 + gate_pre * (1.0 - sigmoid))).astype(bf16)
    up_low = (grad_hidden * activated).astype(bf16)
    hidden_out[0] = (gates * hidden).astype(bf16)
    pairs_low = join([gate_low, up_low], 1)
    pairs_out[0] = pairs_low
    for place in range(SIDE):
        near = slice((place % 2) * shard, (place % 2 + 1) * shard)
        result = dot_nt(pairs_low, pairs_w[place, 0]).astype(bf16)

        @pl.when(place // 2 == core)
        def _():
            back_own[0, :, near] = result

        @pl.when(place // 2 != core)
        def _():
            back_other[0, :, near] = result

    high = gate_grads.astype(bf16).astype(f32)
    low = gate_grads - high
    back_marks[0] = (jnp.where(high_lane, high, 0.0) + jnp.where(low_lane, low, 0.0)).astype(bf16)


def expert_grad_kernel(info, rows, pairs, gate_grads, up_grads):
    shard, units = up_grads.shape[2:]
    for i in range(SIDE):
        result = dot_tn(rows[0, :, i * shard : (i + 1) * shard], pairs[0]).astype(bf16)
        gate_grads[i, 0] = result[:, :units]
        up_grads[i, 0] = result[:, units:]


def expert_out_kernel(info, grads, hidden, downs_w, out_own, out_other, *down_grads):
    core = info[0]
    shard = downs_w.shape[3]
    for i in range(SIDE):
        place = info[4 + i]
        down_grads[i][0] = dot_tn(hidden[0], grads[0, :, core_columns(place, shard)]).astype(bf16)
        result = dot_nn(hidden[0], downs_w[place, 0]).astype(bf16)
        near = core_columns(place % 2, shard)

        @pl.when(place // 2 == core)
        def _():
            out_own[0, :, near] = result

        @pl.when(place // 2 != core)
        def _():
            out_other[0, :, near] = result


def by_expert(shape):
    if len(shape) == 4:
        return pl.BlockSpec((shape[0], 1) + tuple(shape[2:]), lambda e: (0, e, 0, 0))
    return pl.BlockSpec((1,) + tuple(shape[1:]), lambda e: (e, 0, 0))


def per_expert(kernel, info, arrays, out_shapes, flops, moved):
    return call(
        kernel,
        [scalars] + [by_expert(array.shape) for array in arrays],
        [(shape, bf16) for shape in out_shapes],
        flops=flops,
        moved=moved,
        out_specs=[by_expert(shape) for shape in out_shapes],
        grid=(arrays[0].shape[0],),
    )(info, *arrays)


def project_chunk_kernel(info, own, came, gain, gain_came, heads, heads_came, out, out_came, extra, *pieces):
    core = info[0]
    shard = pieces[0].shape[1]
    size = out.shape[0]
    base = 2 * size + extra.shape[0]
    numbers = lax.broadcasted_iota(jnp.int32, (SMALL, shard), 0)
    both = heads[...] + heads_came[...]
    rest = jnp.zeros((1, shard - 2 * size), f32)
    head_row = join([both[0:1], both[1:2], rest], 1)
    for i, piece in enumerate(pieces):
        place = info[4 + i]
        columns = core_columns(place % 2, shard)
        near = place // 2 == core
        block = jnp.where(near, own[:, columns], came[:, columns])
        piece[:size] = block[:size]
        piece[size : 2 * size] = jnp.where(near, out[:, columns], out_came[:, columns])
        piece[2 * size : base] = extra[:, core_columns(place, shard)]
        gain_row = jnp.where(near, gain[0:1, columns], gain_came[0:1, columns])
        small = jnp.where(numbers == 0, gain_row, jnp.where(numbers == 1, head_row, 0.0))
        piece[base : base + SMALL] = small.astype(bf16)
        piece[base + SMALL :] = block[size:]


def project_final_kernel(
    info, parts, query, out_grad, key, value, router, gain1, gain2, head_gains, load, loss, total, key_value
):
    step = pl.program_id(0)
    size = out_grad.shape[0] // parts.shape[0]
    base = 2 * size + total.shape[0]
    rest = pair = 0.0
    for i in range(parts.shape[0]):
        block = parts[i].astype(f32)
        query[:, i * size : (i + 1) * size] = block[:size].T
        out_grad[i * size : (i + 1) * size] = block[size : 2 * size]
        rest += block[2 * size : base]
        pair += block[base:]

    @pl.when(step == 0)
    def _():
        total[...] = rest

    @pl.when(step > 0)
    def _():
        total[...] += rest

    @pl.when(step % 2 == 0)
    def _():
        key_value[...] = pair

    @pl.when(step % 2 == 1)
    def _():
        both = key_value[...] + pair
        key[...] = both[:size].T
        value[...] = both[size:].T

    @pl.when(step == pl.num_programs(0) - 1)
    def _():
        experts = router.shape[0]
        router[...] = total[:experts]

        def row(i):
            return total[experts + i : experts + i + 1, :]

        gain2[...] = row(0)
        counts = row(1)[:, :experts] + row(2)[:, :experts]
        probs = row(3)[:, :experts] + row(4)[:, :experts]
        kept = row(5)[:, :experts]
        share = counts / (kept * 8.0)
        load[...] = share * float(experts)
        loss[...] = float(experts) * jnp.sum(share * (probs / kept), axis=-1, keepdims=True)
        gain1[...] = row(SMALL)
        count = head_gains.shape[1]
        for part in range(2):
            sums = row(SMALL + 1)[:, part * size : (part + 1) * size]
            sums = pltpu.roll(jnp.broadcast_to(sums, (8, size)), (size - info[2] * count) % size, 1)
            head_gains[part : part + 1] = sums[:1, :count]


def body(
    tokens,
    cotangent,
    doc_lengths,
    padding,
    expert_ids,
    norm1_gain,
    w_query,
    key_weight,
    value_weight,
    q_gain,
    k_gain,
    w_out,
    norm2_gain,
    w_router,
    w_gate,
    w_up,
    w_down,
):
    core = lax.axis_index("tensor")
    context = lax.axis_index("context")
    mine = lax.axis_index("fsdp")
    place_x = context // SIDE
    place_z = context % SIDE
    sign = 1 - 2 * core
    span, width = tokens.shape[1:]
    half = width // 2
    size = 4 * q_gain.shape[0]
    expert_count = w_router.shape[1]
    local_experts, shard, hidden_units = w_gate.shape
    spans = SIDE * SIDE
    count = span * spans
    info = jnp.stack(
        [core, context * local_experts, mine, context]
        + [(mine + sign * i) % SIDE for i in range(SIDE)]
        + [place_x, place_z, sign, context // (spans // 2)]
    ).astype(jnp.int32)
    token_rows = tokens[0]
    cot_rows = cotangent[0]
    ids = expert_ids[0]
    pad_column = padding[0][:, None]

    first, second, inverse1 = call(
        token_message_kernel,
        [scalars] + [whole] * 3,
        [((HALF, half + EXTRA), bf16), ((HALF, half + EXTRA), bf16), ((span, 1), f32)],
    )(info, token_rows, ids, pad_column)

    positions = jnp.arange(count, dtype=jnp.int32)
    ends = jnp.cumsum(doc_lengths[0])
    passed = positions[:, None] >= ends[None, :]
    doc_index = jnp.sum(passed.astype(jnp.int32), axis=-1)
    starts = jnp.sum(jnp.where(passed, doc_lengths, 0), axis=-1)
    doc_rows = doc_index[:, None]
    doc_columns = doc_index[None, :]
    offsets = (positions - starts).astype(f32)
    frequency = theta_base ** (-jnp.arange(size // 2, dtype=f32) * 2.0 / size)
    angles = offsets[:, None] * frequency[None, :]
    cosine = jnp.cos(angles)
    sine = jnp.sin(angles)
    cosine = join([cosine, cosine], 1)
    sine = join([-sine, sine], 1)
    dense = call(
        dense_message_kernel,
        None,
        [((4 * size + expert_count + SMALL, shard), bf16)],
        grid_spec=pltpu.PrefetchScalarGridSpec(
            num_scalar_prefetch=1,
            grid=(1,),
            in_specs=[
                pl.BlockSpec((shard, size), lambda i, info: (0, info[3])),
                pl.BlockSpec((shard, size), lambda i, info: (0, info[11])),
                pl.BlockSpec((shard, size), lambda i, info: (0, info[11])),
                pl.BlockSpec((size, shard), lambda i, info: (info[3], 0)),
            ]
            + [whole] * 5,
            out_specs=[whole],
        ),
    )(
        after(info, first), w_query, key_weight, value_weight, w_out, w_router.T,
        norm1_gain[None], norm2_gain[None], q_gain[None], k_gain[None],
    )[0]
    dense_pieces = ring_gather(dense, moves_y())
    first_near, second_near = two_gathers(
        first, second, moves_z(), moves_x(), (dense_pieces[3],), (dense_pieces[1],)
    )
    pairs = join([w_gate, after(w_up, first_near[2])], 2)
    cot_half = lax.dynamic_slice_in_dim(cot_rows, core * half, half, axis=1)
    cot_all = lax.all_gather(cot_half, "context", axis=0)
    pairs_all = lax.all_gather(pairs, "fsdp", axis=0)
    first_pieces, second_pieces = two_gathers(
        stack(first_near),
        stack(second_near),
        moves_x(),
        moves_z(),
        (dense_pieces[2], cosine, sine, doc_rows),
    )
    token_pieces = first_pieces + second_pieces
    extra_rows = expert_count + SMALL
    dense_own, dense_away, out_own_rows, out_away_rows, extra = call(
        dense_split_kernel,
        [scalars] + [whole] * 4,
        [
            ((3 * size, half), bf16),
            ((3 * size, half), bf16),
            ((size, half), bf16),
            ((size, half), bf16),
            ((extra_rows, width), bf16),
        ],
    )(info, *dense_pieces)
    dense_came = other_core(dense_away)
    out_came_rows = other_core(out_away_rows)
    gain1 = lax.dynamic_slice(extra, (expert_count, core * half), (1, half)).astype(f32)
    gain_rows = extra[expert_count + 2 : expert_count + 4].reshape(2, SIDE, shard)[:, :, : size // SIDE]
    head_gains = jnp.pad(gain_rows.reshape(2, size).astype(f32), ((0, 6), (0, 0)))

    mark_spec = pl.BlockSpec((SIDE, HALF, EXTRA), lambda i: (0, 0, half // EXTRA))
    chosen, pads = call(
        slots_kernel,
        [scalars] + [mark_spec] * 8,
        [((spans, span, EXTRA), bf16), ((8, EXTRA), f32)],
        grid=(1,),
        out_specs=[whole, whole],
    )(info, *token_pieces)

    head_shape = (spans, span, size)
    own_part, away_part, normed1 = call(
        project_kernel,
        [scalars] + [whole] * 11,
        [((spans, span, 3 * size), f32), ((spans, span, 3 * size), bf16), ((spans, span, half), bf16)],
        flops=4 * count * half * 3 * size,
        moved=2 * 10**7,
    )(info, gain1, after(dense_own, cot_all), dense_came, *token_pieces)
    down_all = lax.all_gather(after(w_down, own_part), "fsdp", axis=0)
    mixed, raw, queries, keys, values, log_totals = call(
        attend_kernel,
        [whole] * 8,
        [
            (head_shape, bf16),
            ((count, 2 * size), f32),
            ((count, size), bf16),
            ((count, size), bf16),
            ((count, size), bf16),
            ((count, 1), f32),
        ],
        flops=4 * 10**9,
        moved=3 * 10**7,
    )(own_part, other_core(away_part), cosine, sine, head_gains, doc_rows, doc_columns, pads)
    mixed_came = other_core(mixed)
    piece_shape = (SIDE, HALF, half)
    branch_pieces = call(
        out_kernel, [scalars] + [whole] * 4, [(piece_shape, bf16)] * 8, flops=4 * count * size * half, moved=10**7
    )(info, mixed, mixed_came, out_own_rows, out_came_rows)
    branch = plane_scatter(branch_pieces)

    residual2, inverse2, normed2, probs, gates, picked_total, first, second = call(
        router_kernel,
        [scalars] + [whole] * 5,
        [
            ((span, width), f32),
            ((span, 1), f32),
            ((span, width), bf16),
            ((span, expert_count), f32),
            ((span, expert_count), f32),
            ((span, 1), f32),
            ((HALF, half + EXTRA), bf16),
            ((HALF, half + EXTRA), bf16),
        ],
    )(info, token_rows, branch, other_core(branch), ids, extra)
    cot_other = other_core(after(cot_all, first))
    slot_count = spans * SLOTS
    slot_grads = call(
        pick_spans_kernel,
        [scalars] + [whole] * 3,
        [((local_experts, slot_count, width), bf16)],
        flops=4 * 10**9,
        moved=2 * 10**7,
    )(info, chosen, cot_all, cot_other)[0]
    row_pieces = plane_gather(
        first, second, ((), (), (pairs_all,), (slot_grads,))
    )
    away_pieces = [other_core(piece) for piece in row_pieces]

    slot_rows, slot_marks = call(
        pick_rows_kernel,
        [scalars] + [whole] * 17,
        [((local_experts, slot_count, width), bf16), ((local_experts, slot_count, EXTRA), bf16)],
        flops=4 * 10**9,
        moved=2 * 10**7,
    )(info, chosen, *row_pieces, *away_pieces)
    expert_flops = 2 * local_experts * slot_count * width * hidden_units
    slot_half = (local_experts, slot_count, half)
    slot_hidden = (local_experts, slot_count, hidden_units)
    back_own, back_other, back_marks, hidden, pair_grads = per_expert(
        expert_kernel,
        info,
        [slot_rows, slot_marks, slot_grads, pairs_all, down_all],
        [slot_half, slot_half, (local_experts, slot_count, EXTRA), slot_hidden, slot_hidden[:2] + (2 * hidden_units,)],
        5 * expert_flops,
        5 * 10**7,
    )
    back_came = other_core(back_other)
    gate_grads, up_grads = per_expert(
        expert_grad_kernel,
        info,
        [slot_rows, pair_grads],
        [(SIDE, local_experts, shard, hidden_units)] * 2,
        2 * expert_flops,
        3 * 10**7,
    )
    grad_pieces = call(
        put_rows_kernel,
        [scalars] + [whole] * 4,
        [((SIDE, HALF, half + EXTRA), bf16)] * 8,
        flops=2 * 10**9,
        moved=2 * 10**7,
    )(info, chosen, back_own, after(back_came, gate_grads), back_marks)
    out_own, out_other, *down_grads = per_expert(
        expert_out_kernel,
        info,
        [slot_grads, after(hidden, grad_pieces[0]), down_all],
        [slot_half, slot_half] + [(local_experts, hidden_units, shard)] * 4,
        2 * expert_flops,
        3 * 10**7,
    )
    mixture_spans = call(
        put_spans_kernel,
        [whole] * 3,
        [((spans, span, half), bf16)],
        flops=2 * 10**9,
        moved=2 * 10**7,
    )(chosen, out_own, other_core(out_other))[0]
    gate_mine = lax.psum_scatter(gate_grads, "fsdp", scatter_dimension=0, tiled=False)
    grad_message = plane_scatter(grad_pieces, ((out_own,), (), ()))
    up_mine = lax.psum_scatter(up_grads, "fsdp", scatter_dimension=0, tiled=False)

    first, second, grad_residual2, router_rows = call(
        router_back_kernel,
        [scalars] + [whole] * 12,
        [
            ((HALF, half), bf16),
            ((HALF, half), bf16),
            ((span, width), f32),
            ((extra_rows, width), bf16),
        ],
        scratch_shapes=[pltpu.VMEM((span, width), bf16)],
    )(
        info, grad_message, other_core(grad_message), residual2, inverse2, normed2, probs, gates, picked_total,
        ids, pad_column, cot_rows, extra,
    )

    out_pieces = plane_gather(first, second, ((), (), (), (mixture_spans,)))
    heads_own, heads_away = call(
        heads_back_kernel,
        [scalars] + [whole] * 10,
        [((spans, span, size), f32)] * 2,
        flops=4 * count * size * half,
        moved=10**7,
    )(info, out_own_rows, out_came_rows, *out_pieces)
    mixture = lax.psum_scatter(after(mixture_spans, heads_own), "context", scatter_dimension=0, tiled=False)
    result = call(result_kernel, [scalars] + [whole] * 3, [((span, width), f32)])(
        info, mixture, other_core(mixture), residual2
    )[0]
    heads_came, gate_mine, up_mine = together(other_core(heads_away), gate_mine, up_mine)
    grads, gain_grads = call(
        attend_back_kernel,
        [whole] * 13,
        [((spans, span, 3 * size), bf16), ((8, size), f32)],
        flops=8 * 10**9,
        moved=3 * 10**7,
        scratch_shapes=[pltpu.VMEM((count, size), bf16)] + [pltpu.VMEM((count, size), f32)] * 3,
    )(
        heads_own, heads_came, raw, queries, keys, values, log_totals,
        cosine, sine, head_gains, doc_rows, doc_columns, pads,
    )
    grads_came = other_core(grads)
    down_passing = moves_y()[0](down_grads[2])
    down_ahead = moves_y()[1](after(down_grads[3], down_passing))
    project_own, project_away, gain1_part = call(
        project_grad_kernel,
        [whole] * 6,
        [((3 * size, half), bf16)] * 2 + [((8, half), f32)],
        flops=4 * count * half * 3 * size,
        moved=2 * 10**7,
    )(grads, after(grads_came, down_passing), normed1, dense_own, dense_came, gain1)
    out_grad_own, out_grad_away = call(
        out_grad_kernel,
        [scalars] + [whole] * 10,
        [((size, half), bf16)] * 2,
        flops=4 * count * size * half,
        moved=10**7,
    )(info, after(mixed, heads_own), mixed_came, *out_pieces)
    project_came = other_core(project_away)
    message_shape = (4 * size + SMALL + extra_rows, shard)
    project_pieces = call(
        project_chunk_kernel, [scalars] + [whole] * 9, [(message_shape, bf16)] * 4
    )(
        info, project_own, project_came, gain1_part, other_core(gain1_part), gain_grads, other_core(gain_grads),
        out_grad_own, after(other_core(out_grad_away), down_ahead), router_rows,
    )
    passing = moves_y()[0](project_pieces[2])
    from_ahead = moves_y()[1](project_pieces[3])
    input_pieces = call(
        input_back_kernel,
        [scalars] + [whole] * 4,
        [(piece_shape, bf16)] * 8,
        flops=4 * count * half * 3 * size,
        moved=3 * 10**7,
    )(info, grads, after(grads_came, project_pieces[0]), dense_own, dense_came)
    from_behind = moves_y()[0](add_low(project_pieces[1], after(passing, input_pieces[0])))
    message = low_sum((project_pieces[0], from_behind, from_ahead))
    message_all = lax.all_gather(message, "context", axis=0)
    down_behind = moves_y()[0](add_low(down_grads[1], down_passing))
    final_rows = plane_scatter(input_pieces, ((), (down_behind,), ()))
    grad_input = call(final_rows_kernel, [scalars] + [whole] * 6, [((span, width), f32)])(
        info, final_rows, other_core(final_rows), token_rows, inverse1, extra, grad_residual2
    )[0]
    final_gate = gate_mine.astype(f32)
    final_up = up_mine.astype(f32)
    final_down = down_grads[0].astype(f32) + down_ahead.astype(f32) + down_behind.astype(f32)
    (
        final_query, final_out, final_key, final_value, final_router, final_gain1, final_gain2, final_head_gains,
        expert_load, balance_loss,
    ) = call(
        project_final_kernel,
        [scalars, pl.BlockSpec((SIDE,) + message_shape, lambda i: (i, 0, 0))],
        [
            ((shard, spans * size), f32),
            ((spans * size, shard), f32),
            ((shard, 2 * size), f32),
            ((shard, 2 * size), f32),
            ((expert_count, shard), f32),
            ((1, shard), f32),
            ((1, shard), f32),
            ((2, size // SIDE), f32),
            ((1, expert_count), f32),
            ((1, 1), f32),
        ],
        grid=(SIDE,),
        out_specs=[
            pl.BlockSpec((shard, SIDE * size), lambda i: (0, i)),
            pl.BlockSpec((SIDE * size, shard), lambda i: (i, 0)),
            pl.BlockSpec((shard, size), lambda i: (0, i // 2)),
            pl.BlockSpec((shard, size), lambda i: (0, i // 2)),
        ]
        + [whole] * 6,
        scratch_shapes=[pltpu.VMEM((SMALL + extra_rows, shard), f32), pltpu.VMEM((2 * size, shard), f32)],
    )(info, after(message_all, grad_input, final_gate, final_up, final_down, result))

    return (
        result[None],
        balance_loss.reshape(()),
        expert_load.reshape(expert_count),
        grad_input[None],
        final_gain1.reshape(shard),
        final_query,
        final_key,
        final_value,
        final_head_gains[0],
        final_head_gains[1],
        final_out,
        final_gain2.reshape(shard),
        final_router.T,
        final_gate,
        final_up,
        final_down,
    )


def solution(mesh):
    in_specs = (
        P("fsdp", "context", None),
        P("fsdp", "context", None),
        P("fsdp", None),
        P("fsdp", "context"),
        P("fsdp", "context", None),
        P("fsdp"),
        P("fsdp", "tensor"),
        P("fsdp", "tensor"),
        P("fsdp", "tensor"),
        P("fsdp"),
        P("fsdp"),
        P("tensor", "fsdp"),
        P("fsdp"),
        P("fsdp", None),
        P("context", "fsdp", "tensor"),
        P("context", "fsdp", "tensor"),
        P("context", "tensor", "fsdp"),
    )
    out_specs = (
        P("fsdp", "context", None),
        P(),
        P(),
        P("fsdp", "context", None),
        P("fsdp"),
        P("fsdp", "tensor"),
        P("fsdp", "tensor"),
        P("fsdp", "tensor"),
        P("fsdp"),
        P("fsdp"),
        P("tensor", "fsdp"),
        P("fsdp"),
        P("fsdp", None),
        P("context", "fsdp", "tensor"),
        P("context", "fsdp", "tensor"),
        P("context", "tensor", "fsdp"),
    )
    return jax.shard_map(body, mesh=mesh, in_specs=in_specs, out_specs=out_specs, check_vma=False)
```

```python
import jax
import jax.numpy as jnp
from jax import lax
from jax.experimental import pallas as pl
from jax.experimental.pallas import tpu as pltpu
from jax.sharding import PartitionSpec as P

WINDOW = 1024
SIDE = 4
HALF = 64
QUERY_BLOCK = 256
SLOTS = 32
EXTRA = 128
SMALL = 16

epsilon = 1e-06
theta_base = 1000000.0
negative = -1e30
f32 = jnp.float32
bf16 = jnp.bfloat16
vmem_limit = 56 * 1024 * 1024
whole = pl.BlockSpec(memory_space=pltpu.VMEM)
scalars = pl.BlockSpec(memory_space=pltpu.SMEM)


def call(kernel, in_specs, out_shape, flops=10**6, moved=10**6, **rest):
    if in_specs is not None:
        rest["in_specs"] = in_specs
    return pl.pallas_call(
        kernel,
        out_shape=[jax.ShapeDtypeStruct(shape, kind) for shape, kind in out_shape],
        compiler_params=pltpu.CompilerParams(vmem_limit_bytes=vmem_limit),
        cost_estimate=pl.CostEstimate(flops=flops, bytes_accessed=moved, transcendentals=0),
        **rest,
    )


def dot_nt(left, right):
    return lax.dot_general(left, right, (((1,), (1,)), ((), ())), preferred_element_type=f32)


def dot_tn(left, right):
    return lax.dot_general(left, right, (((0,), (0,)), ((), ())), preferred_element_type=f32)


def dot_nn(left, right):
    return jnp.dot(left, right, preferred_element_type=f32)


def join(parts, axis=0):
    return jnp.concatenate(parts, axis=axis)


def ring_moves(axis, target):
    forward = []
    backward = []
    count = lax.axis_size(axis)
    for i in range(count):
        for core, sign in ((0, 1), (1, -1)):
            forward.append((2 * i + core, 2 * target(i, sign) + core))
            backward.append((2 * i + core, 2 * target(i, -sign) + core))

    def move(pairs):
        return lambda value: lax.ppermute(value, (axis, "tensor"), pairs)

    return move(forward), move(backward)


def moves_z():
    return ring_moves("context", lambda i, step: (i // SIDE) * SIDE + (i + step) % SIDE)


def moves_x():
    return ring_moves("context", lambda i, step: (i + SIDE * step) % (SIDE * SIDE))


def moves_y():
    return ring_moves("fsdp", lambda i, step: (i + step) % SIDE)


def other_core(value):
    return lax.ppermute(value, "tensor", [(0, 1), (1, 0)])


def after(value, *events):
    return lax.optimization_barrier((value, *events))[0]


def ring_gather(value, moves):
    behind = moves[0](value)
    ahead = moves[1](value)
    far = moves[0](behind)
    return [value, ahead, far, behind]


def add_low(left, right):
    return (left.astype(f32) + right.astype(f32)).astype(bf16)


def low_sum(terms):
    return sum(term.astype(f32) for term in terms).astype(bf16)


def across(value, step):
    pairs = [(i, i ^ (SIDE * step)) for i in range(SIDE * SIDE)]
    return lax.ppermute(value, "context", pairs)


def along_x(value, step):
    pairs = [(i, (i + SIDE * step) % (SIDE * SIDE)) for i in range(SIDE * SIDE)]
    return lax.ppermute(value, "context", pairs)


def along_z(value, step):
    pairs = [(i, (i // SIDE) * SIDE + (i + step) % SIDE) for i in range(SIDE * SIDE)]
    return lax.ppermute(value, "context", pairs)


def ring_scatter(parts, moves):
    passing = moves[0](parts[2])
    from_ahead = moves[1](parts[3])
    from_behind = moves[0](add_low(parts[1], passing))
    return parts[0], from_behind, from_ahead


def together(*values):
    return lax.optimization_barrier(values)


def stack_kernel(a, b, c, d, result):
    for i, part in enumerate((a, b, c, d)):
        result[i] = part[...]


def stack(parts):
    shape = parts[0].shape
    return call(stack_kernel, [whole] * 4, [((4,) + shape, bf16)])(*parts)[0]


def two_gathers(left, right, left_moves, right_moves, events=(), last=()):
    left_behind = left_moves[0](left)
    left_ahead = left_moves[1](left)
    right_behind = right_moves[0](right)
    right_ahead = right_moves[1](right)
    left_behind, left_ahead, right_behind, right_ahead = together(
        left_behind, left_ahead, right_behind, right_ahead, *events
    )[:4]
    left_far = left_moves[0](left_behind)
    right_far = right_moves[0](right_behind)
    left_far, right_far = together(left_far, right_far, *last)[:2]
    return [left, left_ahead, left_far, left_behind], [right, right_ahead, right_far, right_behind]


def two_short_gathers(left, right, events=()):
    left_moves, right_moves = moves_z(), moves_x()
    values = (
        left_moves[1](left),
        along_z(left, 2),
        left_moves[0](left),
        right_moves[1](right),
        along_x(right, 2),
        right_moves[0](right),
    )
    values = together(*values, *events)[:6]
    return [left, *values[:3]], [right, *values[3:]]


def two_short_scatters(left, right, events=()):
    left_moves, right_moves = moves_z(), moves_x()
    values = (
        left_moves[1](left[3]),
        along_z(left[2], 2),
        left_moves[0](left[1]),
        right_moves[1](right[3]),
        along_x(right[2], 2),
        right_moves[0](right[1]),
    )
    values = together(*values, *events)[:6]
    return (left[0], *values[:3]), (right[0], *values[3:])


def plane_gather(first, second, events=((), (), (), ())):
    first_near, second_near = two_short_gathers(first, second, events[0])
    first_pieces, second_pieces = two_gathers(
        stack(first_near), stack(second_near), moves_x(), moves_z(), *events[2:]
    )
    return first_pieces + second_pieces


def unstack_kernel(a, b, c, r0, r1, r2, r3):
    for i, part in enumerate((r0, r1, r2, r3)):
        part[...] = (a[i].astype(f32) + b[i].astype(f32) + c[i].astype(f32)).astype(bf16)


def unstack(terms):
    shape = terms[0].shape[1:]
    return call(unstack_kernel, [whole] * 3, [(shape, bf16)] * 4)(*terms)


def total_kernel(*refs):
    result = refs[8]
    for i in range(2):
        a, b, c, d = (part[...].astype(f32) for part in refs[4 * i : 4 * i + 4])
        result[i * HALF : (i + 1) * HALF] = (a + b) + (c + d)


def two_scatters(left, right, left_moves, right_moves, events=(), last=()):
    left_passing = left_moves[0](left[2])
    left_from_ahead = left_moves[1](left[3])
    right_passing = right_moves[0](right[2])
    right_from_ahead = right_moves[1](right[3])
    left_passing, left_from_ahead, right_passing, right_from_ahead, *events = together(
        left_passing, left_from_ahead, right_passing, right_from_ahead, *events
    )
    left_from_behind = left_moves[0](add_low(left[1], left_passing))
    right_from_behind = right_moves[0](add_low(right[1], right_passing))
    left_from_behind, right_from_behind, *last = together(left_from_behind, right_from_behind, *last)
    left_terms = (left[0], left_from_behind, left_from_ahead)
    right_terms = (right[0], right_from_behind, right_from_ahead)
    return left_terms, right_terms, events, last


def plane_scatter(pieces, events=((), (), ())):
    first, second, *_ = two_scatters(pieces[:4], pieces[4:], moves_x(), moves_z(), *events[:2])
    first, second = two_short_scatters(unstack(first), unstack(second), events[2])
    return total(first, second)


def total(first, second):
    width = first[0].shape[-1]
    return call(total_kernel, [whole] * 8, [((2 * HALF, width), f32)])(*first, *second)[0]


def split_low(value, count):
    parts = []
    rest = value
    for _ in range(count):
        part = rest.astype(bf16)
        parts.append(part)
        rest = rest - part.astype(f32)
    return parts


def core_columns(core, width):
    return pl.ds(pl.multiple_of(core * width, width), width)


def token_message_kernel(info, tokens, ids, padding, first, second, inverse_out):
    width = tokens.shape[1]
    half = width // 2
    rows = tokens[...].astype(f32)
    inverse = lax.rsqrt(jnp.mean(rows * rows, axis=-1, keepdims=True) + epsilon)
    inverse_out[...] = inverse
    lanes = lax.broadcasted_iota(jnp.int32, (rows.shape[0], EXTRA), 1)
    marks = jnp.zeros((rows.shape[0], EXTRA), f32)
    for k in range(8):
        marks = jnp.where(lanes == k, ids[:, k : k + 1].astype(f32), marks)
    marks = jnp.where(lanes == 8, padding[...].astype(f32), marks)
    for k, part in enumerate(split_low(inverse, 3)):
        marks = jnp.where(lanes == 9 + k, part.astype(f32), marks)
    marks = marks.astype(bf16)
    own = tokens[:, core_columns(info[0], half)]
    first[:, :half] = own[:HALF]
    first[:, half:] = marks[:HALF]
    second[:, :half] = own[HALF:]
    second[:, half:] = marks[HALF:]


def dense_message_kernel(info, query, key, value, out, router, gain1, gain2, q_gain, k_gain, result):
    size = query.shape[1]
    experts = router.shape[0]
    result[:size] = query[...].T
    result[size : 2 * size] = key[...].T
    result[2 * size : 3 * size] = value[...].T
    result[3 * size : 4 * size] = out[...]
    result[4 * size : 4 * size + experts] = router[...]
    base = 4 * size + experts
    rows = lax.broadcasted_iota(jnp.int32, (SMALL, result.shape[1]), 0)
    gains = jnp.where(rows == 0, gain1[...].astype(f32), 0.0)
    gains = jnp.where(rows == 1, gain2[...].astype(f32), gains)
    rest = jnp.zeros((1, result.shape[1] - q_gain.shape[1]), f32)
    gains = jnp.where(rows == 2, join([q_gain[...].astype(f32), rest], 1), gains)
    gains = jnp.where(rows == 3, join([k_gain[...].astype(f32), rest], 1), gains)
    result[base:] = gains.astype(bf16)


def dense_split_kernel(info, a, b, c, d, own, away, own_out, away_out, extra):
    shard = a.shape[1]
    rows = own.shape[0]
    size = own_out.shape[0]
    core = info[0]
    for i, piece in enumerate((a, b, c, d)):
        place = info[4 + i]
        columns = core_columns(place % 2, shard)

        @pl.when(place // 2 == core)
        def _():
            own[:, columns] = piece[:rows]
            own_out[:, columns] = piece[rows : rows + size]

        @pl.when(place // 2 != core)
        def _():
            away[:, columns] = piece[:rows]
            away_out[:, columns] = piece[rows : rows + size]

        extra[:, core_columns(place, shard)] = piece[rows + size :]


def slots_kernel(info, *refs):
    pieces, (chosen, pads) = refs[:8], refs[8:]
    first_expert = info[1]
    place_x, place_z, sign = info[8], info[9], info[10]
    shape = (2 * HALF, EXTRA)
    lanes = lax.broadcasted_iota(jnp.int32, shape, 1)
    rows = lax.broadcasted_iota(jnp.int32, shape, 0)
    earlier = (lanes < rows).astype(bf16)
    pad_total = jnp.zeros((1, EXTRA), f32)
    for ix in range(SIDE):
        for iz in range(SIDE):
            marks = join([pieces[ix][iz], pieces[4 + iz][ix]]).astype(f32)
            pad_total += jnp.sum(marks, axis=0, keepdims=True)
            named = jnp.zeros(shape, f32)
            for e in range(EXTRA // SLOTS):
                hit = jnp.where((lanes < 8) & (marks == (first_expert + e).astype(f32)), 1.0, 0.0)
                hit = jnp.max(hit, axis=-1, keepdims=True)
                named = jnp.where(lanes // SLOTS == e, hit, named)
            ranks = dot_nn(earlier, named.astype(bf16))
            match = (named > 0.0) & (ranks == (lanes % SLOTS).astype(f32))
            place = ((place_x + sign * ix) % SIDE) * SIDE + (place_z + sign * iz) % SIDE
            chosen[place] = jnp.where(match, 1.0, 0.0).astype(bf16)
    pads[...] = jnp.broadcast_to(pad_total, pads.shape)


def write_slots(result, place, columns, slots):
    for e in range(EXTRA // SLOTS):
        target = pl.ds(pl.multiple_of(place * SLOTS, SLOTS), SLOTS)
        result[e, target, columns] = slots[e * SLOTS : (e + 1) * SLOTS]


def read_slots(source, place, columns):
    target = pl.ds(pl.multiple_of(place * SLOTS, SLOTS), SLOTS)
    return join([source[e, target, columns] for e in range(EXTRA // SLOTS)])


def pick_rows_kernel(info, chosen, *refs):
    own, other, (result, extra) = refs[:8], refs[8:16], refs[16:]
    core, place_x, place_z, sign = info[0], info[8], info[9], info[10]
    half = result.shape[-1] // 2
    own_columns = core_columns(core, half)
    other_columns = core_columns(1 - core, half)
    for ix in range(SIDE):
        for iz in range(SIDE):
            place = ((place_x + sign * ix) % SIDE) * SIDE + (place_z + sign * iz) % SIDE
            matrix = chosen[place]
            rows = join([own[ix][iz], own[4 + iz][ix]])
            slots = dot_tn(matrix, rows).astype(bf16)
            write_slots(result, place, own_columns, slots[:, :half])
            write_slots(extra, place, slice(None), slots[:, half:])
            jx, jz = -ix % SIDE, -iz % SIDE
            rows = join([other[jx][jz, :, :half], other[4 + jz][jx, :, :half]])
            write_slots(result, place, other_columns, dot_tn(matrix, rows).astype(bf16))


def pick_spans_kernel(info, chosen, own, other, result):
    core = info[0]
    half = own.shape[-1]
    for place in range(SIDE * SIDE):
        matrix = chosen[place]
        write_slots(result, place, core_columns(core, half), dot_tn(matrix, own[place]).astype(bf16))
        write_slots(result, place, core_columns(1 - core, half), dot_tn(matrix, other[place]).astype(bf16))


def put_rows_kernel(info, chosen, own, came, extra, *pieces):
    place_x, place_z, sign = info[8], info[9], info[10]
    half = own.shape[-1]
    for ix in range(SIDE):
        for iz in range(SIDE):
            place = ((place_x + sign * ix) % SIDE) * SIDE + (place_z + sign * iz) % SIDE
            matrix = chosen[place]
            rows = read_slots(own, place, slice(None)).astype(f32) + read_slots(came, place, slice(None)).astype(f32)
            rows = dot_nn(matrix, rows.astype(bf16)).astype(bf16)
            marks = dot_nn(matrix, read_slots(extra, place, slice(None))).astype(bf16)
            pieces[ix][iz, :, :half] = rows[:HALF]
            pieces[4 + iz][ix, :, :half] = rows[HALF:]
            pieces[ix][iz, :, half:] = marks[:HALF]
            pieces[4 + iz][ix, :, half:] = marks[HALF:]


def put_spans_kernel(chosen, own, came, result):
    for place in range(SIDE * SIDE):
        rows = read_slots(own, place, slice(None)).astype(f32) + read_slots(came, place, slice(None)).astype(f32)
        result[place] = dot_nn(chosen[place], rows.astype(bf16)).astype(bf16)


def span_of(info, ix, iz):
    return ((info[8] + info[10] * ix) % SIDE) * SIDE + (info[9] + info[10] * iz) % SIDE


def piece_parts(info, i):
    for j in range(SIDE):
        if i < SIDE:
            yield j, span_of(info, i, j), slice(0, HALF)
        else:
            yield j, span_of(info, j, i - SIDE), slice(HALF, 2 * HALF)


def project_kernel(info, gain, own, came, *refs):
    pieces, (own_out, other_out, normed_out) = refs[:8], refs[8:]
    half = gain.shape[1]
    wide = own_out.shape[-1]
    count = SIDE * HALF
    lanes = lax.broadcasted_iota(jnp.int32, (count, EXTRA), 1)
    for i, piece in enumerate(pieces):
        rows = piece[...].reshape(count, half + EXTRA)
        marks = jnp.where((lanes >= 9) & (lanes < 12), rows[:, half:].astype(f32), 0.0)
        inverse = jnp.sum(marks, axis=-1, keepdims=True)
        normed = (rows[:, :half].astype(f32) * inverse * gain[...]).astype(bf16)
        own_rows = dot_nt(normed, own[...])
        other_rows = dot_nt(normed, came[...])
        for j, span, part in piece_parts(info, i):
            cut = slice(j * HALF, (j + 1) * HALF)
            normed_out[span, part] = normed[cut]
            own_out[span, part] = own_rows[cut]
            other_out[span, part] = other_rows[cut].astype(bf16)


def turn(value, cosine, sine):
    return value * cosine + pltpu.roll(value, 64, 1) * sine


def block_mask(doc_rows, doc_columns, real, query_start, key_start, query_count, key_count):
    positions = lax.broadcasted_iota(jnp.int32, (1, key_count), 1) + key_start
    doc_columns = jnp.where(positions < real, doc_columns, -1)
    offsets = lax.broadcasted_iota(jnp.int32, (query_count, query_count), 0) - lax.broadcasted_iota(
        jnp.int32, (query_count, query_count), 1
    )
    same = doc_rows == doc_columns[:, key_count - query_count :]
    parts = [((offsets >= 0) & same) | (offsets == 0)]
    begin = 0
    if query_start - key_start == WINDOW:
        begin = query_count
        parts.insert(0, (offsets < 0) & (doc_rows == doc_columns[:, :begin]))
    if begin < key_count - query_count:
        parts.insert(-1, doc_rows == doc_columns[:, begin : key_count - query_count])
    return parts


def keep(parts, values, other):
    result = []
    begin = 0
    for part in parts:
        end = begin + part.shape[1]
        result.append(jnp.where(part, values[:, begin:end], other))
        begin = end
    return result[0] if len(result) == 1 else join(result, 1)


def real_count(pads, count):
    return (count - pads[0:1, 8:9]).astype(jnp.int32)


def attend_kernel(
    own, came, cosine, sine, gains, doc_rows, doc_columns, pads,
    mixed, raw, queries, keys, values, log_totals,
):
    count = queries.shape[0]
    size = queries.shape[1]
    span = mixed.shape[1]
    scale = size ** (-0.5)

    def prepare(j, carry):
        rows = pl.ds(pl.multiple_of(j * span, span), span)
        block = own[j] + came[j].astype(f32)
        raw[rows, :] = block[:, : 2 * size]
        cos_rows = cosine[rows, :]
        sin_rows = sine[rows, :]
        for part, target in ((0, queries), (1, keys)):
            piece = block[:, part * size : (part + 1) * size]
            inverse = lax.rsqrt(jnp.mean(piece * piece, axis=-1, keepdims=True) + epsilon)
            normed = piece * inverse * gains[part : part + 1, :]
            target[rows, :] = turn(normed, cos_rows, sin_rows).astype(bf16)
        values[rows, :] = block[:, 2 * size :].astype(bf16)
        return carry

    lax.fori_loop(0, count // span, prepare, 0)
    real = real_count(pads, float(count))
    for start in range(0, count, QUERY_BLOCK):
        low = max(0, start - WINDOW)
        high = start + QUERY_BLOCK
        scores = dot_nt(queries[start:high, :], keys[low:high, :]) * scale
        allowed = block_mask(
            doc_rows[start:high, :], doc_columns[:, low:high], real, start, low, QUERY_BLOCK, high - low
        )
        scores = keep(allowed, scores, negative)
        peak = jnp.max(scores, axis=-1, keepdims=True)
        exponent = jnp.exp(scores - peak)
        total = jnp.sum(exponent, axis=-1, keepdims=True)
        weights = (exponent * (1.0 / total)).astype(bf16)
        rows = dot_nn(weights, values[low:high, :]).astype(bf16)
        mixed[start // span : high // span] = rows.reshape(QUERY_BLOCK // span, span, size)
        log_totals[start:high, :] = peak + jnp.log(total)


def attend_back_kernel(
    own, came, raw, queries, keys, values, log_totals, cosine, sine, gains, doc_rows, doc_columns, pads,
    grads, gain_grads, grad_mixed, grad_queries, grad_keys, grad_values,
):
    count = queries.shape[0]
    size = queries.shape[1]
    span = grads.shape[1]
    scale = size ** (-0.5)
    grad_mixed[...] = (own[...] + came[...]).astype(bf16).reshape(count, size)
    grad_keys[...] = jnp.zeros_like(grad_keys)
    grad_values[...] = jnp.zeros_like(grad_values)
    real = real_count(pads, float(count))
    for start in range(0, count, QUERY_BLOCK):
        low = max(0, start - WINDOW)
        high = start + QUERY_BLOCK
        query_rows = queries[start:high, :]
        key_rows = keys[low:high, :]
        grad_rows = grad_mixed[start:high, :]
        scores = dot_nt(query_rows, key_rows) * scale
        allowed = block_mask(
            doc_rows[start:high, :], doc_columns[:, low:high], real, start, low, QUERY_BLOCK, high - low
        )
        soft = keep(allowed, jnp.exp(scores - log_totals[start:high, :]), 0.0)
        grad_soft = dot_nt(grad_rows, values[low:high, :])
        row_dot = jnp.sum(soft * grad_soft, axis=-1, keepdims=True)
        grad_scores = (soft * (grad_soft - row_dot)).astype(bf16)
        grad_queries[start:high, :] = dot_nn(grad_scores, key_rows) * scale
        grad_keys[low:high, :] += dot_tn(grad_scores, query_rows) * scale
        grad_values[low:high, :] += dot_tn(soft.astype(bf16), grad_rows)
    gain_grads[...] = jnp.zeros_like(gain_grads)

    def finish(j, carry):
        rows = pl.ds(pl.multiple_of(j * span, span), span)
        cos_rows = cosine[rows, :]
        sin_rows = sine[rows, :]
        parts = []
        for part, source in ((0, grad_queries), (1, grad_keys)):
            piece = raw[rows, part * size : (part + 1) * size]
            inverse = lax.rsqrt(jnp.mean(piece * piece, axis=-1, keepdims=True) + epsilon)
            back = turn(source[rows, :], cos_rows, -sin_rows)
            gain_grads[part : part + 1, :] += jnp.sum(back * piece * inverse, axis=0, keepdims=True)
            scaled = back * gains[part : part + 1, :]
            mean = jnp.mean(scaled * piece, axis=-1, keepdims=True)
            parts.append((inverse * scaled - piece * (inverse * inverse * inverse * mean)).astype(bf16))
        parts.append(grad_values[rows, :].astype(bf16))
        grads[j] = join(parts, 1)
        return carry

    lax.fori_loop(0, count // span, finish, 0)


def out_kernel(info, mixed, came_mixed, own, came, *pieces):
    for i, piece in enumerate(pieces):
        parts = list(piece_parts(info, i))
        left = join([mixed[span, part] for _, span, part in parts])
        right = join([came_mixed[span, part] for _, span, part in parts])
        rows = dot_nn(left, own[...]) + dot_nn(right, came[...])
        piece[...] = rows.astype(bf16).reshape(piece.shape)


def heads_back_kernel(info, own, came, *refs):
    pieces, (own_out, other_out) = refs[:8], refs[8:]
    for i, piece in enumerate(pieces):
        rows = piece[...].reshape(SIDE * HALF, piece.shape[-1])
        own_rows = dot_nt(rows, own[...])
        other_rows = dot_nt(rows, came[...])
        for j, span, part in piece_parts(info, i):
            cut = slice(j * HALF, (j + 1) * HALF)
            own_out[span, part] = own_rows[cut]
            other_out[span, part] = other_rows[cut]


def out_grad_kernel(info, mixed, came_mixed, *refs):
    pieces, (own_out, away_out) = refs[:8], refs[8:]
    own_total = away_total = 0.0
    for i, piece in enumerate(pieces):
        rows = piece[...].reshape(SIDE * HALF, piece.shape[-1])
        parts = list(piece_parts(info, i))
        own_total += dot_tn(join([mixed[span, part] for _, span, part in parts]), rows)
        away_total += dot_tn(join([came_mixed[span, part] for _, span, part in parts]), rows)
    own_out[...] = own_total.astype(bf16)
    away_out[...] = away_total.astype(bf16)


def input_back_kernel(info, grads, came_grads, own, came, *pieces):
    for i, piece in enumerate(pieces):
        parts = list(piece_parts(info, i))
        left = join([grads[span, part] for _, span, part in parts])
        right = join([came_grads[span, part] for _, span, part in parts])
        rows = dot_nn(left, own[...]) + dot_nn(right, came[...])
        piece[...] = rows.astype(bf16).reshape(piece.shape)


def project_grad_kernel(grads, came_grads, normed, own, came, gain, own_out, away_out, gain_grad):
    count = normed.shape[0] * normed.shape[1]
    wide = grads.shape[-1]
    rows = normed[...].reshape(count, normed.shape[-1])
    total = 0.0
    for source, weight, target in ((grads, own, own_out), (came_grads, came, away_out)):
        result = dot_tn(source[...].reshape(count, wide), rows)
        target[...] = result.astype(bf16)
        total += jnp.sum(result * weight[...].astype(f32), axis=0, keepdims=True)
    gain_grad[...] = jnp.broadcast_to(total / gain[...], gain_grad.shape)


def halves(core, own, came):
    return join([jnp.where(core == 0, own, came), jnp.where(core == 0, came, own)], 1)


def chosen_experts(ids, count):
    lanes = lax.broadcasted_iota(jnp.int32, (ids.shape[0], count), 1)
    chosen = jnp.zeros((ids.shape[0], count), f32)
    for k in range(8):
        chosen = jnp.where(lanes == ids[:, k : k + 1], 1.0, chosen)
    return chosen


def router_kernel(
    info, tokens, own, came, ids, extra, residual_out, inverse_out, normed_out, probs_out, gates_out, total_out, first, second
):
    core = info[0]
    half = tokens.shape[1] // 2
    experts = probs_out.shape[1]
    residual = tokens[...].astype(f32) + halves(core, own[...], came[...])
    residual_out[...] = residual
    inverse = lax.rsqrt(jnp.mean(residual * residual, axis=-1, keepdims=True) + epsilon)
    inverse_out[...] = inverse
    gain = extra[experts + 1 : experts + 2, :].astype(f32)
    normed = (residual * inverse * gain).astype(bf16)
    normed_out[...] = normed
    logits = dot_nt(normed, extra[:experts, :])
    exponent = jnp.exp(logits - jnp.max(logits, axis=-1, keepdims=True))
    probs = exponent / jnp.sum(exponent, axis=-1, keepdims=True)
    probs_out[...] = probs
    chosen = chosen_experts(ids, experts)
    picked = probs * chosen
    total = jnp.sum(picked, axis=-1, keepdims=True)
    total_out[...] = total
    gates = picked / total
    gates_out[...] = gates
    marks = join(split_low(gates, 2), 1)
    mine = normed_out[:, core_columns(core, half)]
    first[:, :half] = mine[:HALF]
    first[:, half:] = marks[:HALF]
    second[:, :half] = mine[HALF:]
    second[:, half:] = marks[HALF:]


def router_back_kernel(
    info, own, came, residual_ref, inverse_ref, normed, probs_ref, gates_ref, total, ids, padding, cotangent, extra,
    first, second, grad_out, rows_out, scratch,
):
    core = info[0]
    half = cotangent.shape[1] // 2
    experts = probs_ref.shape[1]
    probs = probs_ref[...]
    gates = gates_ref[...]
    residual = residual_ref[...]
    inverse = inverse_ref[...]
    marks = own[:, half:] + came[:, half:]
    gate_grads = marks[:, :experts] + marks[:, experts:]
    chosen = chosen_experts(ids, experts)
    grad_picked = (gate_grads - jnp.sum(gate_grads * gates, axis=-1, keepdims=True)) / total[...]
    grad_probs = chosen * grad_picked
    grad_logits = (probs * (grad_probs - jnp.sum(grad_probs * probs, axis=-1, keepdims=True))).astype(bf16)
    grad_normed = halves(core, own[:, :half], came[:, :half]) + dot_nn(grad_logits, extra[:experts, :])
    scaled = grad_normed * extra[experts + 1 : experts + 2, :].astype(f32)
    mean = jnp.mean(scaled * residual, axis=-1, keepdims=True)
    grad = cotangent[...].astype(f32) + inverse * scaled - residual * (inverse * inverse * inverse * mean)
    grad_out[...] = grad
    scratch[...] = grad.astype(bf16)
    mine = scratch[:, core_columns(core, half)]
    first[...] = mine[:HALF]
    second[...] = mine[HALF:]
    gain_grad = jnp.sum(grad_normed * residual * inverse, axis=0, keepdims=True)
    rows_out[:experts] = dot_tn(grad_logits, normed[...]).astype(bf16)
    kept = 1.0 - padding[...].astype(f32)
    shard = 4 * EXTRA
    rest = jnp.zeros((1, shard - experts), f32)

    def row(values):
        return join([values, rest] * SIDE, 1)

    counted = chosen * kept
    probs_sum = jnp.sum(probs * kept, axis=0, keepdims=True)
    probs_high = probs_sum.astype(bf16).astype(f32)
    kept_sum = jnp.broadcast_to(jnp.sum(kept, axis=0, keepdims=True), (1, experts))
    rows = (
        gain_grad,
        row(jnp.sum(counted[:HALF], axis=0, keepdims=True)),
        row(jnp.sum(counted[HALF:], axis=0, keepdims=True)),
        row(probs_high),
        row(probs_sum - probs_high),
        row(kept_sum),
    )
    numbers = lax.broadcasted_iota(jnp.int32, (SMALL, 2 * half), 0)
    small = jnp.zeros((SMALL, 2 * half), f32)
    for i, values in enumerate(rows):
        small = jnp.where(numbers == i, values, small)
    rows_out[experts:] = small.astype(bf16)


def final_rows_kernel(info, own, came, tokens, inverse_ref, extra, grad_residual, grad_input):
    core = info[0]
    base = extra.shape[0] - SMALL
    rows = tokens[...].astype(f32)
    inverse = inverse_ref[...]
    scaled = halves(core, own[...], came[...]) * extra[base : base + 1, :].astype(f32)
    mean = jnp.mean(scaled * rows, axis=-1, keepdims=True)
    grad_input[...] = grad_residual[...] + inverse * scaled - rows * (inverse * inverse * inverse * mean)


def result_kernel(info, own, came, residual, result):
    result[...] = residual[...] + halves(info[0], own[...].astype(f32), came[...].astype(f32))


def expert_kernel(info, rows, marks, grads, pairs_w, downs_w, back_own, back_other, back_marks, hidden_out, pairs_out):
    core = info[0]
    expert = info[1] + pl.program_id(0)
    shard = pairs_w.shape[2]
    count = rows.shape[1]
    units = hidden_out.shape[2]
    pairs = grad_raw = 0.0
    for place in range(SIDE):
        columns = slice(place * shard, (place + 1) * shard)
        pairs += dot_nn(rows[0, :, columns], pairs_w[place, 0])
        grad_raw += dot_nt(grads[0, :, columns], downs_w[place, 0])
    gate_pre = pairs[:, :units]
    up_pre = pairs[:, units:]
    lanes = lax.broadcasted_iota(jnp.int32, (count, EXTRA), 1)
    high_lane = lanes == expert
    low_lane = lanes == expert + EXTRA // 2
    gates = jnp.sum(jnp.where(high_lane | low_lane, marks[0].astype(f32), 0.0), axis=-1, keepdims=True)
    sigmoid = jax.nn.sigmoid(gate_pre)
    activated = gate_pre * sigmoid
    hidden = (activated * up_pre).astype(bf16).astype(f32)
    gate_grads = jnp.sum(hidden * grad_raw, axis=-1, keepdims=True)
    grad_hidden = gates * grad_raw
    gate_low = (grad_hidden * up_pre * sigmoid * (1.0 + gate_pre * (1.0 - sigmoid))).astype(bf16)
    up_low = (grad_hidden * activated).astype(bf16)
    hidden_out[0] = (gates * hidden).astype(bf16)
    pairs_low = join([gate_low, up_low], 1)
    pairs_out[0] = pairs_low
    for place in range(SIDE):
        near = slice((place % 2) * shard, (place % 2 + 1) * shard)
        result = dot_nt(pairs_low, pairs_w[place, 0]).astype(bf16)

        @pl.when(place // 2 == core)
        def _():
            back_own[0, :, near] = result

        @pl.when(place // 2 != core)
        def _():
            back_other[0, :, near] = result

    high = gate_grads.astype(bf16).astype(f32)
    low = gate_grads - high
    back_marks[0] = (jnp.where(high_lane, high, 0.0) + jnp.where(low_lane, low, 0.0)).astype(bf16)


def expert_grad_kernel(info, rows, pairs, gate_grads, up_grads):
    shard, units = up_grads.shape[2:]
    for i in range(SIDE):
        result = dot_tn(rows[0, :, i * shard : (i + 1) * shard], pairs[0]).astype(bf16)
        gate_grads[i, 0] = result[:, :units]
        up_grads[i, 0] = result[:, units:]


def expert_out_kernel(info, grads, hidden, downs_w, out_own, out_other, *down_grads):
    core = info[0]
    shard = downs_w.shape[3]
    for i in range(SIDE):
        place = info[4 + i]
        down_grads[i][0] = dot_tn(hidden[0], grads[0, :, core_columns(place, shard)]).astype(bf16)
        result = dot_nn(hidden[0], downs_w[place, 0]).astype(bf16)
        near = core_columns(place % 2, shard)

        @pl.when(place // 2 == core)
        def _():
            out_own[0, :, near] = result

        @pl.when(place // 2 != core)
        def _():
            out_other[0, :, near] = result


def by_expert(shape):
    if len(shape) == 4:
        return pl.BlockSpec((shape[0], 1) + tuple(shape[2:]), lambda e: (0, e, 0, 0))
    return pl.BlockSpec((1,) + tuple(shape[1:]), lambda e: (e, 0, 0))


def per_expert(kernel, info, arrays, out_shapes, flops, moved):
    return call(
        kernel,
        [scalars] + [by_expert(array.shape) for array in arrays],
        [(shape, bf16) for shape in out_shapes],
        flops=flops,
        moved=moved,
        out_specs=[by_expert(shape) for shape in out_shapes],
        grid=(arrays[0].shape[0],),
    )(info, *arrays)


def project_chunk_kernel(info, own, came, gain, gain_came, heads, heads_came, out, out_came, extra, *pieces):
    core = info[0]
    shard = pieces[0].shape[1]
    size = out.shape[0]
    base = 2 * size + extra.shape[0]
    numbers = lax.broadcasted_iota(jnp.int32, (SMALL, shard), 0)
    both = heads[...] + heads_came[...]
    rest = jnp.zeros((1, shard - 2 * size), f32)
    head_row = join([both[0:1], both[1:2], rest], 1)
    for i, piece in enumerate(pieces):
        place = info[4 + i]
        columns = core_columns(place % 2, shard)
        near = place // 2 == core
        block = jnp.where(near, own[:, columns], came[:, columns])
        piece[:size] = block[:size]
        piece[size : 2 * size] = jnp.where(near, out[:, columns], out_came[:, columns])
        piece[2 * size : base] = extra[:, core_columns(place, shard)]
        gain_row = jnp.where(near, gain[0:1, columns], gain_came[0:1, columns])
        small = jnp.where(numbers == 0, gain_row, jnp.where(numbers == 1, head_row, 0.0))
        piece[base : base + SMALL] = small.astype(bf16)
        piece[base + SMALL :] = block[size:]


def project_final_kernel(
    info, parts, query, out_grad, key, value, router, gain1, gain2, head_gains, load, loss, total, key_value
):
    step = pl.program_id(0)
    size = out_grad.shape[0] // parts.shape[0]
    base = 2 * size + total.shape[0]
    rest = pair = 0.0
    for i in range(parts.shape[0]):
        block = parts[i].astype(f32)
        query[:, i * size : (i + 1) * size] = block[:size].T
        out_grad[i * size : (i + 1) * size] = block[size : 2 * size]
        rest += block[2 * size : base]
        pair += block[base:]

    @pl.when(step == 0)
    def _():
        total[...] = rest

    @pl.when(step > 0)
    def _():
        total[...] += rest

    @pl.when(step % 2 == 0)
    def _():
        key_value[...] = pair

    @pl.when(step % 2 == 1)
    def _():
        both = key_value[...] + pair
        key[...] = both[:size].T
        value[...] = both[size:].T

    @pl.when(step == pl.num_programs(0) - 1)
    def _():
        experts = router.shape[0]
        router[...] = total[:experts]

        def row(i):
            return total[experts + i : experts + i + 1, :]

        gain2[...] = row(0)
        counts = row(1)[:, :experts] + row(2)[:, :experts]
        probs = row(3)[:, :experts] + row(4)[:, :experts]
        kept = row(5)[:, :experts]
        share = counts / (kept * 8.0)
        load[...] = share * float(experts)
        loss[...] = float(experts) * jnp.sum(share * (probs / kept), axis=-1, keepdims=True)
        gain1[...] = row(SMALL)
        count = head_gains.shape[1]
        for part in range(2):
            sums = row(SMALL + 1)[:, part * size : (part + 1) * size]
            sums = pltpu.roll(jnp.broadcast_to(sums, (8, size)), (size - info[2] * count) % size, 1)
            head_gains[part : part + 1] = sums[:1, :count]


def body(
    tokens,
    cotangent,
    doc_lengths,
    padding,
    expert_ids,
    norm1_gain,
    w_query,
    key_weight,
    value_weight,
    q_gain,
    k_gain,
    w_out,
    norm2_gain,
    w_router,
    w_gate,
    w_up,
    w_down,
):
    core = lax.axis_index("tensor")
    context = lax.axis_index("context")
    mine = lax.axis_index("fsdp")
    place_x = context // SIDE
    place_z = context % SIDE
    sign = 1 - 2 * core
    span, width = tokens.shape[1:]
    half = width // 2
    size = 4 * q_gain.shape[0]
    expert_count = w_router.shape[1]
    local_experts, shard, hidden_units = w_gate.shape
    spans = SIDE * SIDE
    count = span * spans
    info = jnp.stack(
        [core, context * local_experts, mine, context]
        + [(mine + sign * i) % SIDE for i in range(SIDE)]
        + [place_x, place_z, sign, context // (spans // 2)]
    ).astype(jnp.int32)
    token_rows = tokens[0]
    cot_rows = cotangent[0]
    ids = expert_ids[0]
    pad_column = padding[0][:, None]

    first, second, inverse1 = call(
        token_message_kernel,
        [scalars] + [whole] * 3,
        [((HALF, half + EXTRA), bf16), ((HALF, half + EXTRA), bf16), ((span, 1), f32)],
    )(info, token_rows, ids, pad_column)

    positions = jnp.arange(count, dtype=jnp.int32)
    ends = jnp.cumsum(doc_lengths[0])
    passed = positions[:, None] >= ends[None, :]
    doc_index = jnp.sum(passed.astype(jnp.int32), axis=-1)
    starts = jnp.sum(jnp.where(passed, doc_lengths, 0), axis=-1)
    doc_rows = doc_index[:, None]
    doc_columns = doc_index[None, :]
    offsets = (positions - starts).astype(f32)
    frequency = theta_base ** (-jnp.arange(size // 2, dtype=f32) * 2.0 / size)
    angles = offsets[:, None] * frequency[None, :]
    cosine = jnp.cos(angles)
    sine = jnp.sin(angles)
    cosine = join([cosine, cosine], 1)
    sine = join([-sine, sine], 1)
    dense = call(
        dense_message_kernel,
        None,
        [((4 * size + expert_count + SMALL, shard), bf16)],
        grid_spec=pltpu.PrefetchScalarGridSpec(
            num_scalar_prefetch=1,
            grid=(1,),
            in_specs=[
                pl.BlockSpec((shard, size), lambda i, info: (0, info[3])),
                pl.BlockSpec((shard, size), lambda i, info: (0, info[11])),
                pl.BlockSpec((shard, size), lambda i, info: (0, info[11])),
                pl.BlockSpec((size, shard), lambda i, info: (info[3], 0)),
            ]
            + [whole] * 5,
            out_specs=[whole],
        ),
    )(
        after(info, first), w_query, key_weight, value_weight, w_out, w_router.T,
        norm1_gain[None], norm2_gain[None], q_gain[None], k_gain[None],
    )[0]
    dense_pieces = ring_gather(dense, moves_y())
    first_near, second_near = two_gathers(
        first, second, moves_z(), moves_x(), (dense_pieces[3],), (dense_pieces[1],)
    )
    pairs = join([w_gate, after(w_up, first_near[2])], 2)
    cot_half = lax.dynamic_slice_in_dim(cot_rows, core * half, half, axis=1)
    cot_all = lax.all_gather(cot_half, "context", axis=0)
    pairs_all = lax.all_gather(pairs, "fsdp", axis=0)
    first_pieces, second_pieces = two_gathers(
        stack(first_near),
        stack(second_near),
        moves_x(),
        moves_z(),
        (dense_pieces[2], cosine, sine, doc_rows),
    )
    token_pieces = first_pieces + second_pieces
    extra_rows = expert_count + SMALL
    dense_own, dense_away, out_own_rows, out_away_rows, extra = call(
        dense_split_kernel,
        [scalars] + [whole] * 4,
        [
            ((3 * size, half), bf16),
            ((3 * size, half), bf16),
            ((size, half), bf16),
            ((size, half), bf16),
            ((extra_rows, width), bf16),
        ],
    )(info, *dense_pieces)
    dense_came = other_core(dense_away)
    out_came_rows = other_core(out_away_rows)
    gain1 = lax.dynamic_slice(extra, (expert_count, core * half), (1, half)).astype(f32)
    gain_rows = extra[expert_count + 2 : expert_count + 4].reshape(2, SIDE, shard)[:, :, : size // SIDE]
    head_gains = jnp.pad(gain_rows.reshape(2, size).astype(f32), ((0, 6), (0, 0)))

    mark_spec = pl.BlockSpec((SIDE, HALF, EXTRA), lambda i: (0, 0, half // EXTRA))
    chosen, pads = call(
        slots_kernel,
        [scalars] + [mark_spec] * 8,
        [((spans, span, EXTRA), bf16), ((8, EXTRA), f32)],
        grid=(1,),
        out_specs=[whole, whole],
    )(info, *token_pieces)

    head_shape = (spans, span, size)
    own_part, away_part, normed1 = call(
        project_kernel,
        [scalars] + [whole] * 11,
        [((spans, span, 3 * size), f32), ((spans, span, 3 * size), bf16), ((spans, span, half), bf16)],
        flops=4 * count * half * 3 * size,
        moved=2 * 10**7,
    )(info, gain1, after(dense_own, cot_all), dense_came, *token_pieces)
    down_all = lax.all_gather(after(w_down, own_part), "fsdp", axis=0)
    mixed, raw, queries, keys, values, log_totals = call(
        attend_kernel,
        [whole] * 8,
        [
            (head_shape, bf16),
            ((count, 2 * size), f32),
            ((count, size), bf16),
            ((count, size), bf16),
            ((count, size), bf16),
            ((count, 1), f32),
        ],
        flops=4 * 10**9,
        moved=3 * 10**7,
    )(own_part, other_core(away_part), cosine, sine, head_gains, doc_rows, doc_columns, pads)
    mixed_came = other_core(mixed)
    piece_shape = (SIDE, HALF, half)
    branch_pieces = call(
        out_kernel, [scalars] + [whole] * 4, [(piece_shape, bf16)] * 8, flops=4 * count * size * half, moved=10**7
    )(info, mixed, mixed_came, out_own_rows, out_came_rows)
    branch = plane_scatter(branch_pieces)

    residual2, inverse2, normed2, probs, gates, picked_total, first, second = call(
        router_kernel,
        [scalars] + [whole] * 5,
        [
            ((span, width), f32),
            ((span, 1), f32),
            ((span, width), bf16),
            ((span, expert_count), f32),
            ((span, expert_count), f32),
            ((span, 1), f32),
            ((HALF, half + EXTRA), bf16),
            ((HALF, half + EXTRA), bf16),
        ],
    )(info, token_rows, branch, other_core(branch), ids, extra)
    cot_other = other_core(after(cot_all, first))
    slot_count = spans * SLOTS
    slot_grads = call(
        pick_spans_kernel,
        [scalars] + [whole] * 3,
        [((local_experts, slot_count, width), bf16)],
        flops=4 * 10**9,
        moved=2 * 10**7,
    )(info, chosen, cot_all, cot_other)[0]
    row_pieces = plane_gather(
        first, second, ((), (), (pairs_all,), (slot_grads,))
    )
    away_pieces = [other_core(piece) for piece in row_pieces]

    slot_rows, slot_marks = call(
        pick_rows_kernel,
        [scalars] + [whole] * 17,
        [((local_experts, slot_count, width), bf16), ((local_experts, slot_count, EXTRA), bf16)],
        flops=4 * 10**9,
        moved=2 * 10**7,
    )(info, chosen, *row_pieces, *away_pieces)
    expert_flops = 2 * local_experts * slot_count * width * hidden_units
    slot_half = (local_experts, slot_count, half)
    slot_hidden = (local_experts, slot_count, hidden_units)
    back_own, back_other, back_marks, hidden, pair_grads = per_expert(
        expert_kernel,
        info,
        [slot_rows, slot_marks, slot_grads, pairs_all, down_all],
        [slot_half, slot_half, (local_experts, slot_count, EXTRA), slot_hidden, slot_hidden[:2] + (2 * hidden_units,)],
        5 * expert_flops,
        5 * 10**7,
    )
    back_came = other_core(back_other)
    gate_grads, up_grads = per_expert(
        expert_grad_kernel,
        info,
        [slot_rows, pair_grads],
        [(SIDE, local_experts, shard, hidden_units)] * 2,
        2 * expert_flops,
        3 * 10**7,
    )
    grad_pieces = call(
        put_rows_kernel,
        [scalars] + [whole] * 4,
        [((SIDE, HALF, half + EXTRA), bf16)] * 8,
        flops=2 * 10**9,
        moved=2 * 10**7,
    )(info, chosen, back_own, after(back_came, gate_grads), back_marks)
    out_own, out_other, *down_grads = per_expert(
        expert_out_kernel,
        info,
        [slot_grads, after(hidden, grad_pieces[0]), down_all],
        [slot_half, slot_half] + [(local_experts, hidden_units, shard)] * 4,
        2 * expert_flops,
        3 * 10**7,
    )
    mixture_spans = call(
        put_spans_kernel,
        [whole] * 3,
        [((spans, span, half), bf16)],
        flops=2 * 10**9,
        moved=2 * 10**7,
    )(chosen, out_own, other_core(out_other))[0]
    gate_mine = lax.psum_scatter(after(gate_grads, grad_pieces[0]), "fsdp", scatter_dimension=0, tiled=False)
    grad_message = plane_scatter(grad_pieces, ((out_own,), (), ()))
    up_mine = lax.psum_scatter(after(up_grads, grad_pieces[0]), "fsdp", scatter_dimension=0, tiled=False)

    first, second, grad_residual2, router_rows = call(
        router_back_kernel,
        [scalars] + [whole] * 12,
        [
            ((HALF, half), bf16),
            ((HALF, half), bf16),
            ((span, width), f32),
            ((extra_rows, width), bf16),
        ],
        scratch_shapes=[pltpu.VMEM((span, width), bf16)],
    )(
        info, grad_message, other_core(grad_message), residual2, inverse2, normed2, probs, gates, picked_total,
        ids, pad_column, cot_rows, extra,
    )

    out_pieces = plane_gather(first, second, ((), (), (), (mixture_spans,)))
    heads_own, heads_away = call(
        heads_back_kernel,
        [scalars] + [whole] * 10,
        [((spans, span, size), f32)] * 2,
        flops=4 * count * size * half,
        moved=10**7,
    )(info, out_own_rows, out_came_rows, *out_pieces)
    mixture = lax.psum_scatter(after(mixture_spans, heads_own), "context", scatter_dimension=0, tiled=False)
    result = call(result_kernel, [scalars] + [whole] * 3, [((span, width), f32)])(
        info, mixture, other_core(mixture), residual2
    )[0]
    heads_came, gate_mine, up_mine = together(other_core(heads_away), gate_mine, up_mine)
    grads, gain_grads = call(
        attend_back_kernel,
        [whole] * 13,
        [((spans, span, 3 * size), bf16), ((8, size), f32)],
        flops=8 * 10**9,
        moved=3 * 10**7,
        scratch_shapes=[pltpu.VMEM((count, size), bf16)] + [pltpu.VMEM((count, size), f32)] * 3,
    )(
        heads_own, heads_came, raw, queries, keys, values, log_totals,
        cosine, sine, head_gains, doc_rows, doc_columns, pads,
    )
    grads_came = other_core(grads)
    down_passing = moves_y()[0](down_grads[2])
    down_ahead = moves_y()[1](after(down_grads[3], down_passing))
    project_own, project_away, gain1_part = call(
        project_grad_kernel,
        [whole] * 6,
        [((3 * size, half), bf16)] * 2 + [((8, half), f32)],
        flops=4 * count * half * 3 * size,
        moved=2 * 10**7,
    )(grads, after(grads_came, down_passing), normed1, dense_own, dense_came, gain1)
    out_grad_own, out_grad_away = call(
        out_grad_kernel,
        [scalars] + [whole] * 10,
        [((size, half), bf16)] * 2,
        flops=4 * count * size * half,
        moved=10**7,
    )(info, after(mixed, heads_own), mixed_came, *out_pieces)
    project_came = other_core(project_away)
    message_shape = (4 * size + SMALL + extra_rows, shard)
    project_pieces = call(
        project_chunk_kernel, [scalars] + [whole] * 9, [(message_shape, bf16)] * 4
    )(
        info, project_own, project_came, gain1_part, other_core(gain1_part), gain_grads, other_core(gain_grads),
        out_grad_own, other_core(out_grad_away), router_rows,
    )
    passing = moves_y()[0](project_pieces[2])
    from_ahead = moves_y()[1](project_pieces[3])
    input_pieces = call(
        input_back_kernel,
        [scalars] + [whole] * 4,
        [(piece_shape, bf16)] * 8,
        flops=4 * count * half * 3 * size,
        moved=3 * 10**7,
    )(info, grads, after(grads_came, project_pieces[0]), dense_own, dense_came)
    from_behind = moves_y()[0](add_low(project_pieces[1], after(passing, input_pieces[0], down_ahead)))
    message = low_sum((project_pieces[0], from_behind, from_ahead))
    message_all = lax.all_gather(message, "context", axis=0)
    down_behind = moves_y()[0](add_low(down_grads[1], down_passing))
    final_rows = plane_scatter(input_pieces, ((), (down_behind,), ()))
    grad_input = call(final_rows_kernel, [scalars] + [whole] * 6, [((span, width), f32)])(
        info, final_rows, other_core(final_rows), token_rows, inverse1, extra, grad_residual2
    )[0]
    final_gate = gate_mine.astype(f32)
    final_up = up_mine.astype(f32)
    final_down = down_grads[0].astype(f32) + down_ahead.astype(f32) + down_behind.astype(f32)
    (
        final_query, final_out, final_key, final_value, final_router, final_gain1, final_gain2, final_head_gains,
        expert_load, balance_loss,
    ) = call(
        project_final_kernel,
        [scalars, pl.BlockSpec((SIDE,) + message_shape, lambda i: (i, 0, 0))],
        [
            ((shard, spans * size), f32),
            ((spans * size, shard), f32),
            ((shard, 2 * size), f32),
            ((shard, 2 * size), f32),
            ((expert_count, shard), f32),
            ((1, shard), f32),
            ((1, shard), f32),
            ((2, size // SIDE), f32),
            ((1, expert_count), f32),
            ((1, 1), f32),
        ],
        grid=(SIDE,),
        out_specs=[
            pl.BlockSpec((shard, SIDE * size), lambda i: (0, i)),
            pl.BlockSpec((SIDE * size, shard), lambda i: (i, 0)),
            pl.BlockSpec((shard, size), lambda i: (0, i // 2)),
            pl.BlockSpec((shard, size), lambda i: (0, i // 2)),
        ]
        + [whole] * 6,
        scratch_shapes=[pltpu.VMEM((SMALL + extra_rows, shard), f32), pltpu.VMEM((2 * size, shard), f32)],
    )(info, after(message_all, grad_input, final_gate, final_up, final_down, result))

    return (
        result[None],
        balance_loss.reshape(()),
        expert_load.reshape(expert_count),
        grad_input[None],
        final_gain1.reshape(shard),
        final_query,
        final_key,
        final_value,
        final_head_gains[0],
        final_head_gains[1],
        final_out,
        final_gain2.reshape(shard),
        final_router.T,
        final_gate,
        final_up,
        final_down,
    )


def solution(mesh):
    in_specs = (
        P("fsdp", "context", None),
        P("fsdp", "context", None),
        P("fsdp", None),
        P("fsdp", "context"),
        P("fsdp", "context", None),
        P("fsdp"),
        P("fsdp", "tensor"),
        P("fsdp", "tensor"),
        P("fsdp", "tensor"),
        P("fsdp"),
        P("fsdp"),
        P("tensor", "fsdp"),
        P("fsdp"),
        P("fsdp", None),
        P("context", "fsdp", "tensor"),
        P("context", "fsdp", "tensor"),
        P("context", "tensor", "fsdp"),
    )
    out_specs = (
        P("fsdp", "context", None),
        P(),
        P(),
        P("fsdp", "context", None),
        P("fsdp"),
        P("fsdp", "tensor"),
        P("fsdp", "tensor"),
        P("fsdp", "tensor"),
        P("fsdp"),
        P("fsdp"),
        P("tensor", "fsdp"),
        P("fsdp"),
        P("fsdp", None),
        P("context", "fsdp", "tensor"),
        P("context", "fsdp", "tensor"),
        P("context", "tensor", "fsdp"),
    )
    return jax.shard_map(body, mesh=mesh, in_specs=in_specs, out_specs=out_specs, check_vma=False)
```
